512 devices in a mesh: seq: 32 (over z_hi, x, core), ri: 4 (over z_lo), rj: 4 (over y).
Axes of the slice: x: 4, y: 4, z: 16 (z_hi: 4, z_lo: 4; z = z_hi * 4 + z_lo), core: 2. Of those that a mesh axis runs over, the one named last changes fastest.
Arguments:
- query_proj: bfloat16 [64, 1024, 256], P('seq', 'ri', 'rj'), may hold values from -8 to 8
- key_proj: bfloat16 [64, 1024, 256], P('seq', 'rj', 'ri'), may hold values from -8 to 8
- value_proj: bfloat16 [64, 1024, 256], P('seq', 'rj', 'ri'), may hold values from -6 to 6
- pair_bias: bfloat16 [8, 1024, 1024], P(None, 'ri', 'rj'), may hold values from -6 to 6
- attn_output: bfloat16 [64, 1024, 256], P('seq', 'ri', 'rj'), may hold values from -6 to 6
- output_grad: bfloat16 [64, 1024, 256], P('seq', 'ri', 'rj'), may hold values from -6 to 6
Outputs:
- query_grad: bfloat16 [64, 1024, 256], P('seq', 'ri', 'rj')
- key_grad: bfloat16 [64, 1024, 256], P('seq', 'rj', 'ri')
- value_grad: bfloat16 [64, 1024, 256], P('seq', 'rj', 'ri')
- bias_grad: float32 [8, 1024, 1024], P(None, 'ri', 'rj')
The draws below stay inside these ranges and needn't reach their ends.
All inputs are finite; a program needn't handle non-finite values.
Results may differ from the reference program's by a relative error of at most 0.014.
Values may be sent and summed in bfloat16 or wider, within the bound.
No kernel may reach another device: no remote copies, remote signals or barrier semaphores. Data moves between devices by JAX's collectives and lax.ppermute only.
A program may use at most 64 MiB of HBM per device.

```python
import jax
import jax.numpy as jnp
from jax import lax

H = 8
HEAD = 32
CM = 256
TILE = 256
SEQS = 64
R = 1024
N_RI = 4
N_RJ = 4


def draw_query_proj(key, part):
    key = jax.random.fold_in(key, 3)
    fresh = jnp.clip(jax.random.normal(key, (SEQS, R, CM), jnp.float32), -4.0, 4.0)
    return fresh.astype(jnp.bfloat16)


def draw_key_proj(key, part):
    key = jax.random.fold_in(key, 5)
    fresh = jnp.clip(jax.random.normal(key, (SEQS, R, CM), jnp.float32), -4.0, 4.0)
    return fresh.astype(jnp.bfloat16)


def steps_of(own_key, extent, shards, least, high):
    factor_of = 1.0
    for axis_at, parts in shards:
        heights = jax.random.uniform(jax.random.fold_in(jax.random.fold_in(own_key, 6), axis_at), (parts,), jnp.float32, least / len(shards), high / len(shards))
        factor_of = factor_of * jnp.repeat(jnp.exp(heights), extent[axis_at] // parts).reshape((-1,) + (1,) * (len(extent) - 1 - axis_at))
    return factor_of


def noise(key, shape, width, reach, cuts=(), dtype=jnp.bfloat16):
    drawn = width * jax.random.normal(key, shape, jnp.float32)
    if cuts:
        drawn = drawn * steps_of(key, shape, cuts, -0.22, 0.18)
    return jnp.clip(drawn, -reach, reach).astype(dtype)


def setup_inputs(seed: int = 0) -> dict:
    key_of = jax.random.split(jax.random.key(seed), 7)
    return {
        "query_proj": draw_query_proj(jax.random.fold_in(key_of[6], 71), 0),
        "key_proj": draw_key_proj(jax.random.fold_in(key_of[6], 71), 0),
        "value_proj": noise(key_of[2], (SEQS, R, CM), 1.0, 6.0, ((0, 32), (1, 4), (2, 4))),
        "pair_bias": noise(key_of[3], (H, R, R), 1.0, 6.0, ((1, 4), (2, 4))),
        "attn_output": noise(key_of[4], (SEQS, R, CM), 1.0, 6.0, ((0, 32), (1, 4), (2, 4))),
        "output_grad": noise(key_of[5], (SEQS, R, CM), 1.0, 6.0, ((0, 32), (1, 4), (2, 4))),
    }


def rounded(values):
    return lax.optimization_barrier(values.astype(jnp.bfloat16)).astype(jnp.float32)


def reference(query_proj, key_proj, value_proj, pair_bias, attn_output, output_grad):
    softmax_scale = HEAD ** -0.5
    bias_full = pair_bias.astype(jnp.float32)
    key_block = R // N_RJ

    def settle(terms):
        return jnp.sum(rounded(terms), axis=0).reshape(R, CM).astype(jnp.bfloat16)

    def one_sequence(carry, inputs):
        query_mat, key_mat, value_mat, out_mat, grad_mat = [x.astype(jnp.float32).reshape(R, H, HEAD) for x in inputs]
        logits = jnp.einsum('ihc,jhc->hij', query_mat, key_mat) * softmax_scale + bias_full
        row_top = jnp.max(logits, axis=2, keepdims=True)
        log_total = row_top + jnp.log(jnp.sum(jnp.exp(logits - row_top), axis=2, keepdims=True))
        weights = jnp.exp(logits - log_total)
        inner_dots = jnp.sum(grad_mat * out_mat, axis=2).T
        grad_weights = jnp.einsum('ihc,jhc->hij', grad_mat, value_mat)
        grad_logits = weights * (grad_weights - inner_dots[:, :, None])
        grad_low = rounded(grad_logits)
        query_terms = jnp.einsum('hibj,bjhc->bihc', grad_low.reshape(H, R, N_RJ, key_block),
                                 key_mat.reshape(N_RJ, key_block, H, HEAD)) * softmax_scale
        key_terms = jnp.einsum('hbij,bihc->bjhc', grad_low.reshape(H, N_RI, TILE, R),
                               query_mat.reshape(N_RI, TILE, H, HEAD)) * softmax_scale
        value_terms = jnp.einsum('hbij,bihc->bjhc', rounded(weights).reshape(H, N_RI, TILE, R),
                                 grad_mat.reshape(N_RI, TILE, H, HEAD))
        return carry + grad_logits, (settle(query_terms), settle(key_terms), settle(value_terms))

    start = jnp.zeros((H, R, R), jnp.float32)
    bias_grad, (query_grad, key_grad, value_grad) = lax.scan(
        one_sequence, start, (query_proj, key_proj, value_proj, attn_output, output_grad))
    return query_grad, key_grad, value_grad, bias_grad
```

```python
import jax
import jax.numpy as jnp
from jax import lax
from jax.experimental import pallas as pl
from jax.experimental.pallas import tpu as pltpu
from jax.sharding import Mesh
from jax.sharding import PartitionSpec as P

HEAD = 32
SCALE = HEAD**-0.5
N = 4
ROWS = 256
KEYS = N * ROWS
LANES = 128
CHUNK = 16
BF = jnp.bfloat16
F32 = jnp.float32
NT = (((1,), (1,)), ((), ()))
TN = (((0,), (0,)), ((), ()))


def attention_kernel(
    q_ref, g_ref, o_ref, kv0, kv1, kv2, kv3, bias_own, bias1, bias2, bias3,
    send, keep, dq_ref, d0, d1, d2, d3,
    kvs, bias, stack, raw, low, acc, dkv, sem_in, sem_out,
):
    ri, rj, core = (lax.axis_index(a) for a in ("ri", "rj", "core"))

    loads = []
    for t, src in enumerate((kv0, kv1, kv2, kv3)):
        block = lax.rem(ri + N - t, N)
        dst = kvs.at[:, pl.ds(pl.multiple_of(block * ROWS, ROWS), ROWS), :]
        loads.append(pltpu.make_async_copy(src, dst, sem_in.at[t]))
    for t, src in enumerate((bias_own.at[pl.ds(2 * rj, 2)], bias1, bias2, bias3)):
        block = lax.rem(rj + N - t, N)
        dst = bias.at[:, :, pl.ds(pl.multiple_of(block * ROWS, ROWS), ROWS)]
        loads.append(pltpu.make_async_copy(src, dst, sem_in.at[N + t]))
    for c in loads:
        c.start()

    lane = lax.broadcasted_iota(jnp.int32, (ROWS, LANES), 1) // HEAD
    for s in range(2):
        both = jnp.concatenate([q_ref[s], g_ref[s]], axis=1)
        for part in range(4):
            stack[s, part * ROWS : (part + 1) * ROWS, :] = jnp.where(lane == part, both, 0)
    for c in loads:
        c.wait()

    for s in range(2):

        @pl.loop(0, 4)
        def _(part):
            rows = pl.ds(pl.multiple_of(part * ROWS, ROWS), ROWS)
            raw[s, rows, :] = lax.dot_general(
                stack[s, rows, :], kvs[s], NT, preferred_element_type=F32
            )

    head_of = lax.broadcasted_iota(jnp.int32, (CHUNK, 2 * HEAD), 1) // HEAD
    for h in range(2):

        @pl.loop(0, ROWS // CHUNK)
        def _(i):
            r0 = pl.multiple_of(i * CHUNK, CHUNK)
            at_logits = pl.ds(pl.multiple_of(h * ROWS + r0, CHUNK), CHUNK)
            at_grads = pl.ds(pl.multiple_of((2 + h) * ROWS + r0, CHUNK), CHUNK)
            rows = pl.ds(r0, CHUNK)
            pair = bias[h, rows, :].astype(F32)
            total = None
            for s in range(2):
                logits = raw[s, at_logits, :] * SCALE + pair
                top = jnp.max(logits, axis=1, keepdims=True)
                weights = jnp.exp(logits - top)
                weights = weights * (1.0 / jnp.sum(weights, axis=1, keepdims=True))
                dots = g_ref[s, rows, :].astype(F32) * o_ref[s, rows, :].astype(F32)
                inner = jnp.sum(jnp.where(head_of == h, dots, 0.0), axis=1, keepdims=True)
                grad = weights * (raw[s, at_grads, :] - inner)
                low[s, at_logits, :] = grad.astype(BF)
                low[s, at_grads, :] = weights.astype(BF)
                total = grad if total is None else total + grad
            total = total.astype(BF)
            quarter = i // (64 // CHUNK)
            within = pl.ds(pl.multiple_of(lax.rem(i, 64 // CHUNK) * CHUNK, CHUNK), CHUNK)
            for j in range(N):
                acc[h, quarter * N + j, within, :] = total[:, j * ROWS : (j + 1) * ROWS]

    stores = [
        pltpu.make_async_copy(acc.at[1 - core], send, sem_out.at[N]),
        pltpu.make_async_copy(acc.at[core], keep, sem_out.at[N + 1]),
    ]
    for c in stores:
        c.start()

    for s in range(2):

        @pl.loop(0, N)
        def _(block):
            at = pl.ds(pl.multiple_of(block * ROWS, ROWS), ROWS)
            grads = lax.dot_general(stack[s], low[s, :, at], TN, preferred_element_type=F32)
            grads = grads.T
            grads = jnp.where(lane < 2, grads * SCALE, grads)
            dkv[s, at, :] = grads.astype(BF)

        half = [
            jnp.dot(
                low[s, h * ROWS : (h + 1) * ROWS, :], kvs[s], preferred_element_type=F32
            )
            for h in range(2)
        ]
        dq = jnp.where(lane == 0, half[0], half[1]) * SCALE
        dq_ref[s] = dq[:, : 2 * HEAD].astype(BF)

    for t, dst in enumerate((d0, d1, d2, d3)):
        block = lax.rem(ri + N - t, N)
        src = dkv.at[:, pl.ds(pl.multiple_of(block * ROWS, ROWS), ROWS), :]
        stores.append(pltpu.make_async_copy(src, dst, sem_out.at[t]))
        stores[-1].start()
    for c in stores:
        c.wait()


def attention(q, g, o, kvs, biases):
    seqs = q.shape[0]
    anywhere, vmem = pl.BlockSpec(memory_space=pl.ANY), pl.BlockSpec(memory_space=pltpu.VMEM)
    piece = jax.ShapeDtypeStruct((N * N, 64, ROWS), BF)
    grads = jax.ShapeDtypeStruct((seqs, ROWS, LANES), BF)
    return pl.pallas_call(
        attention_kernel,
        out_shape=(piece, piece, jax.ShapeDtypeStruct(q.shape, BF), *[grads] * N),
        in_specs=[vmem] * 3 + [anywhere] * 8,
        out_specs=(anywhere, anywhere, vmem, *[anywhere] * N),
        scratch_shapes=[
            pltpu.VMEM((seqs, KEYS, LANES), BF),
            pltpu.VMEM((2, ROWS, KEYS), BF),
            pltpu.VMEM((seqs, 4 * ROWS, LANES), BF),
            pltpu.VMEM((seqs, 4 * ROWS, KEYS), F32),
            pltpu.VMEM((seqs, 4 * ROWS, KEYS), BF),
            pltpu.VMEM((2, N * N, 64, ROWS), BF),
            pltpu.VMEM((seqs, KEYS, LANES), BF),
            pltpu.SemaphoreType.DMA((2 * N,)),
            pltpu.SemaphoreType.DMA((N + 2,)),
        ],
        compiler_params=pltpu.CompilerParams(vmem_limit_bytes=40 * 2**20),
        cost_estimate=pl.CostEstimate(
            flops=5 * 2 * 2**25, bytes_accessed=6 * 2**20, transcendentals=2**20
        ),
    )(q, g, o, *kvs, *biases)


def swap(x, axis, pairs):
    return lax.ppermute(x, axis, [(a, b) for a, b in pairs] + [(b, a) for a, b in pairs])


def body(query_proj, key_proj, value_proj, pair_bias, attn_output, output_grad):
    rj, core = lax.axis_index("rj"), lax.axis_index("core")

    kv = jnp.concatenate([key_proj, value_proj], axis=2)
    kvs = [
        lax.ppermute(
            kv,
            ("ri", "rj"),
            [(a * N + b, (b + t) % N * N + a) for a in range(N) for b in range(N)],
        )
        for t in range(N)
    ]
    biases = [pair_bias]
    for t in range(1, N):
        chunk = lax.dynamic_slice_in_dim(pair_bias, 2 * lax.rem(rj + t, N), 2, 0)
        biases.append(lax.ppermute(chunk, "rj", [(a, (a + t) % N) for a in range(N)]))

    send, keep, query_grad, *parts = attention(query_proj, output_grad, attn_output, kvs, biases)

    other = swap(send, "core", [(0, 1)])
    total = (keep.astype(F32) + other.astype(F32)).astype(BF)
    spread = lax.all_to_all(total, ("x", "rj"), 0, 0, tiled=True)
    total = jnp.sum(spread.reshape(N, N, 64, ROWS).astype(F32), axis=0).astype(BF)
    for pairs in ([(0, 1), (2, 3)], [(1, 2), (3, 0)]):
        other = swap(total, "zh", pairs)
        total = (total.astype(F32) + other.astype(F32)).astype(BF)
    mine = lax.all_gather(total, "x", axis=0)
    other = swap(mine, "core", [(0, 1)])
    even = jnp.where(core == 0, mine, other).astype(F32)
    odd = jnp.where(core == 0, other, mine).astype(F32)
    bias_grad = jnp.stack([even, odd], axis=2)
    bias_grad = bias_grad.transpose(1, 2, 0, 3, 4).reshape(2 * N, ROWS, ROWS)

    back = [
        lax.ppermute(
            parts[t],
            ("ri", "rj"),
            [((b + t) % N * N + a, a * N + b) for a in range(N) for b in range(N)],
        )
        for t in range(N)
    ]
    kv_grad = sum(x.astype(F32) for x in back).astype(BF)
    width = key_proj.shape[2]
    return query_grad, kv_grad[:, :, :width], kv_grad[:, :, width:], bias_grad


def solution(mesh):
    split = Mesh(
        mesh.devices.reshape(N, N, 2, N, N), ("zh", "x", "core", "ri", "rj")
    )
    seq = ("zh", "x", "core")
    rows, keys, tile = P(seq, "ri", "rj"), P(seq, "rj", "ri"), P(None, "ri", "rj")
    return jax.shard_map(
        body,
        mesh=split,
        in_specs=(rows, keys, keys, tile, rows, rows),
        out_specs=(rows, keys, keys, tile),
        check_vma=False,
    )
```

```python
import functools

import jax
import jax.numpy as jnp
from jax import lax
from jax.experimental import pallas as pl
from jax.experimental.pallas import tpu as pltpu
from jax.sharding import Mesh
from jax.sharding import PartitionSpec as P

HEAD = 32
SCALE = HEAD**-0.5
N = 4
ROWS = 256
KEYS = N * ROWS
LANES = 128
CHUNK = 32
UNROLL = 4
BF = jnp.bfloat16
F32 = jnp.float32
NT = (((1,), (1,)), ((), ()))
NN = (((1,), (0,)), ((), ()))


def attention_kernel(
    q_ref, g_ref, o_ref, kv0, kv1, kv2, kv3, bias,
    send, keep, dq_ref, d0, d1, d2, d3,
    stack, wide, raw, low, inner,
):
    ri, core = lax.axis_index("ri"), lax.axis_index("core")
    kvs = (kv0, kv1, kv2, kv3)
    blocks = [lax.rem(ri + N - t, N) for t in range(N)]
    channel = lax.broadcasted_iota(jnp.int32, (LANES, ROWS), 0) // HEAD

    for s in range(2):
        both = jnp.concatenate([q_ref[s], g_ref[s]], axis=0)
        for part in range(4):
            at = slice(part * ROWS, (part + 1) * ROWS)
            one = jnp.where(channel == part, both, 0)
            wide[s, :, at] = one
            stack[s, at, :] = one.T
        dots = g_ref[s].astype(F32) * o_ref[s].astype(F32)
        for h in range(2):
            sums = jnp.sum(dots[h * HEAD : (h + 1) * HEAD], axis=0, keepdims=True)
            inner[s, h] = jnp.broadcast_to(sums, (LANES, ROWS)).T

    for s in range(2):
        for t in range(N):
            at = slice(t * ROWS, (t + 1) * ROWS)
            raw[s, :, at] = lax.dot_general(stack[s], kvs[t][s], NN, preferred_element_type=F32)

    for out, h in ((send, 1 - core), (keep, core)):

        @pl.loop(0, ROWS // CHUNK, unroll=UNROLL)
        def _(i):
            r0 = pl.multiple_of(i * CHUNK, CHUNK)
            at_logits = pl.ds(pl.multiple_of(h * ROWS + r0, CHUNK), CHUNK)
            at_grads = pl.ds(pl.multiple_of((2 + h) * ROWS + r0, CHUNK), CHUNK)
            rows = pl.ds(r0, CHUNK)
            pair = jnp.concatenate([bias[b, h, rows, :] for b in blocks], axis=1).astype(F32)
            total = None
            for s in range(2):
                logits = raw[s, at_logits, :] * SCALE + pair
                top = jnp.max(logits, axis=1, keepdims=True)
                weights = jnp.exp(logits - top)
                weights = weights * (1.0 / jnp.sum(weights, axis=1, keepdims=True))
                dots = jnp.concatenate([inner[s, h, rows, :]] * (KEYS // LANES), axis=1)
                grad = weights * (raw[s, at_grads, :] - dots)
                low[s, at_logits, :] = grad.astype(BF)
                low[s, at_grads, :] = weights.astype(BF)
                total = grad if total is None else total + grad
            total = total.astype(BF)
            quarter = i // (64 // CHUNK)
            within = pl.ds(pl.multiple_of(lax.rem(i, 64 // CHUNK) * CHUNK, CHUNK), CHUNK)
            for t, b in enumerate(blocks):
                out[quarter * N + b, within, :] = total[:, t * ROWS : (t + 1) * ROWS]

    for s in range(2):
        for t, out in enumerate((d0, d1, d2, d3)):
            at = slice(t * ROWS, (t + 1) * ROWS)
            grads = lax.dot_general(wide[s], low[s, :, at], NN, preferred_element_type=F32)
            out[s] = jnp.where(channel < 2, grads * SCALE, grads).astype(BF)
        grads = None
        for t in range(N):
            at = slice(t * ROWS, (t + 1) * ROWS)
            term = lax.dot_general(
                low[s, : 2 * ROWS, at], kvs[t][s], NT, preferred_element_type=F32
            )
            grads = term if grads is None else grads + term
        for h in range(2):
            mine = grads[h * ROWS : (h + 1) * ROWS].T[h * HEAD : (h + 1) * HEAD]
            dq_ref[s, h * HEAD : (h + 1) * HEAD, :] = (mine * SCALE).astype(BF)


def attention(q, g, o, kvs, bias):
    seqs = q.shape[0]
    vmem = pl.BlockSpec(memory_space=pltpu.VMEM)
    piece = jax.ShapeDtypeStruct((N * N, 64, ROWS), BF)
    grads = jax.ShapeDtypeStruct((seqs, LANES, ROWS), BF)
    return pl.pallas_call(
        attention_kernel,
        out_shape=(piece, piece, jax.ShapeDtypeStruct(q.shape, BF), *[grads] * N),
        in_specs=[vmem] * 8,
        out_specs=(vmem,) * 7,
        scratch_shapes=[
            pltpu.VMEM((seqs, 4 * ROWS, LANES), BF),
            pltpu.VMEM((seqs, LANES, 4 * ROWS), BF),
            pltpu.VMEM((seqs, 4 * ROWS, KEYS), F32),
            pltpu.VMEM((seqs, 4 * ROWS, KEYS), BF),
            pltpu.VMEM((seqs, 2, ROWS, LANES), F32),
        ],
        compiler_params=pltpu.CompilerParams(vmem_limit_bytes=32 * 2**20),
        cost_estimate=pl.CostEstimate(
            flops=5 * 2 * 2**25, bytes_accessed=6 * 2**20, transcendentals=2**20
        ),
    )(q, g, o, *kvs, bias)


def hand_on_kernel(n, *refs):
    for src, dst in zip(refs[-2 * n : -n], refs[-n:]):
        dst[...] = src[...]


def hand_on(parts, after):
    anywhere, vmem = pl.BlockSpec(memory_space=pl.ANY), pl.BlockSpec(memory_space=pltpu.VMEM)
    return pl.pallas_call(
        functools.partial(hand_on_kernel, len(parts)),
        out_shape=[jax.ShapeDtypeStruct(x.shape, x.dtype) for x in parts],
        in_specs=[anywhere] * len(after) + [vmem] * len(parts),
        out_specs=[vmem] * len(parts),
        compiler_params=pltpu.CompilerParams(vmem_limit_bytes=8 * 2**20),
        cost_estimate=pl.CostEstimate(flops=0, bytes_accessed=2**20, transcendentals=0),
    )(*after, *parts)


def place_kernel(first, x_ref, *refs):
    out_ref, wide, sem = refs[-3:]
    core = lax.axis_index("core")
    head = core if first else 1 - core
    copies = []
    for j in range(N):
        for x in range(N):
            wide[j, x * 64 : (x + 1) * 64, :] = x_ref[x, j].astype(F32)
        copies.append(pltpu.make_async_copy(wide.at[j], out_ref.at[2 * j + head], sem.at[j]))
        copies[-1].start()
    for c in copies:
        c.wait()


def place(x, before=None):
    first = before is None
    anywhere, vmem = pl.BlockSpec(memory_space=pl.ANY), pl.BlockSpec(memory_space=pltpu.VMEM)
    return pl.pallas_call(
        lambda *refs: place_kernel(first, *refs),
        out_shape=jax.ShapeDtypeStruct((2 * N, ROWS, ROWS), F32),
        in_specs=[vmem] if first else [vmem, anywhere],
        out_specs=anywhere,
        scratch_shapes=[pltpu.VMEM((N, ROWS, ROWS), F32), pltpu.SemaphoreType.DMA((N,))],
        input_output_aliases={} if first else {1: 0},
        compiler_params=pltpu.CompilerParams(vmem_limit_bytes=8 * 2**20),
        cost_estimate=pl.CostEstimate(flops=2**18, bytes_accessed=3 * 2**19, transcendentals=0),
    )(*([x] if first else [x, before]))


def swap(x, axis, pairs):
    return lax.ppermute(x, axis, [(a, b) for a, b in pairs] + [(b, a) for a, b in pairs])


def add(a, b):
    return (a.astype(F32) + b.astype(F32)).astype(BF)


def body(query_proj, key_proj, value_proj, pair_bias, attn_output, output_grad):
    q, k, v, o, g = (
        jnp.swapaxes(x, 1, 2)
        for x in (query_proj, key_proj, value_proj, attn_output, output_grad)
    )
    grid = [(a, b) for a in range(N) for b in range(N)]

    kv = jnp.concatenate([k, v], axis=1)
    kvs = [
        lax.ppermute(kv, ("ri", "rj"), [(a * N + b, (b + t) % N * N + a) for a, b in grid])
        for t in range(N)
    ]
    bias = lax.all_to_all(pair_bias, "rj", 0, 0, tiled=True).reshape(N, 2, ROWS, ROWS)

    send, keep, dq, *parts = attention(q, g, o, kvs, bias)

    def home(part, t):
        return lax.ppermute(
            part, ("ri", "rj"), [((b + t) % N * N + a, a * N + b) for a, b in grid]
        )

    total = add(keep, swap(send, "core", [(0, 1)]))
    spread = lax.all_to_all(total, ("x", "rj"), 0, 0, tiled=True)
    total = jnp.sum(spread.reshape(N, N, 64, ROWS).astype(F32), axis=0).astype(BF)
    back = []
    for first, pairs in ((0, [(0, 1), (2, 3)]), (2, [(1, 2), (3, 0)])):
        other = swap(total, "zh", pairs)
        near = hand_on(parts[first : first + 2], (total, *back))
        homes = [home(part, first + t) for t, part in enumerate(near)]
        total = add(total, other)
        back += homes
    mine = lax.all_gather(total, "x", axis=0)
    bias_grad = place(swap(mine, "core", [(0, 1)]), place(mine))

    kv_grad = sum(x.astype(F32) for x in back).astype(BF)
    width = k.shape[1]
    grads = (dq, kv_grad[:, :width], kv_grad[:, width:])
    return *(jnp.swapaxes(x, 1, 2) for x in grads), bias_grad


def solution(mesh):
    split = Mesh(mesh.devices.reshape(N, N, 2, N, N), ("zh", "x", "core", "ri", "rj"))
    seq = ("zh", "x", "core")
    rows, keys, tile = P(seq, "ri", "rj"), P(seq, "rj", "ri"), P(None, "ri", "rj")
    return jax.shard_map(
        body,
        mesh=split,
        in_specs=(rows, keys, keys, tile, rows, rows),
        out_specs=(rows, keys, keys, tile),
        check_vma=False,
    )
```

```python
import jax
import jax.numpy as jnp
from jax import lax
from jax.experimental import pallas as pl
from jax.experimental.pallas import tpu as pltpu
from jax.sharding import Mesh
from jax.sharding import PartitionSpec as P

HEAD = 32
SCALE = HEAD**-0.5
N = 4
ROWS = 256
KEYS = N * ROWS
LANES = 128
CHUNK = 32
UNROLL = 4
BF = jnp.bfloat16
F32 = jnp.float32
NT = (((1,), (1,)), ((), ()))
NN = (((1,), (0,)), ((), ()))


def attention_kernel(
    q_ref, g_ref, o_ref, kv0, kv1, kv2, kv3, bias,
    send, keep, dq_ref, d0, d1, d2, d3,
    stack, wide, raw, low, inner,
):
    ri, core = lax.axis_index("ri"), lax.axis_index("core")
    kvs = (kv0, kv1, kv2, kv3)
    blocks = [lax.rem(ri + N - t, N) for t in range(N)]
    channel = lax.broadcasted_iota(jnp.int32, (LANES, ROWS), 0) // HEAD

    for s in range(2):
        both = jnp.concatenate([q_ref[s], g_ref[s]], axis=0)
        for part in range(4):
            at = slice(part * ROWS, (part + 1) * ROWS)
            one = jnp.where(channel == part, both, 0)
            wide[s, :, at] = one
            stack[s, at, :] = one.T
        dots = g_ref[s].astype(F32) * o_ref[s].astype(F32)
        for h in range(2):
            sums = jnp.sum(dots[h * HEAD : (h + 1) * HEAD], axis=0, keepdims=True)
            inner[s, h] = jnp.broadcast_to(sums, (LANES, ROWS)).T

    for s in range(2):
        for t in range(N):
            at = slice(t * ROWS, (t + 1) * ROWS)
            raw[s, :, at] = lax.dot_general(stack[s], kvs[t][s], NN, preferred_element_type=F32)

    for out, h in ((send, 1 - core), (keep, core)):

        @pl.loop(0, ROWS // CHUNK, unroll=UNROLL)
        def _(i):
            r0 = pl.multiple_of(i * CHUNK, CHUNK)
            at_logits = pl.ds(pl.multiple_of(h * ROWS + r0, CHUNK), CHUNK)
            at_grads = pl.ds(pl.multiple_of((2 + h) * ROWS + r0, CHUNK), CHUNK)
            rows = pl.ds(r0, CHUNK)
            pair = jnp.concatenate([bias[b, h, rows, :] for b in blocks], axis=1).astype(F32)
            total = None
            for s in range(2):
                logits = raw[s, at_logits, :] * SCALE + pair
                top = jnp.max(logits, axis=1, keepdims=True)
                weights = jnp.exp(logits - top)
                weights = weights * (1.0 / jnp.sum(weights, axis=1, keepdims=True))
                dots = jnp.concatenate([inner[s, h, rows, :]] * (KEYS // LANES), axis=1)
                grad = weights * (raw[s, at_grads, :] - dots)
                low[s, at_logits, :] = grad.astype(BF)
                low[s, at_grads, :] = weights.astype(BF)
                total = grad if total is None else total + grad
            total = total.astype(BF)
            quarter = i // (64 // CHUNK)
            within = pl.ds(pl.multiple_of(lax.rem(i, 64 // CHUNK) * CHUNK, CHUNK), CHUNK)
            for t, b in enumerate(blocks):
                out[quarter * N + b, within, :] = total[:, t * ROWS : (t + 1) * ROWS]

    for s in range(2):
        for t, out in enumerate((d0, d1, d2, d3)):
            at = slice(t * ROWS, (t + 1) * ROWS)
            grads = lax.dot_general(wide[s], low[s, :, at], NN, preferred_element_type=F32)
            out[s] = jnp.where(channel < 2, grads * SCALE, grads).astype(BF)
        grads = None
        for t in range(N):
            at = slice(t * ROWS, (t + 1) * ROWS)
            term = lax.dot_general(
                low[s, : 2 * ROWS, at], kvs[t][s], NT, preferred_element_type=F32
            )
            grads = term if grads is None else grads + term
        for h in range(2):
            mine = grads[h * ROWS : (h + 1) * ROWS].T[h * HEAD : (h + 1) * HEAD]
            dq_ref[s, h * HEAD : (h + 1) * HEAD, :] = (mine * SCALE).astype(BF)


def attention(q, g, o, kvs, bias):
    seqs = q.shape[0]
    vmem = pl.BlockSpec(memory_space=pltpu.VMEM)
    piece = jax.ShapeDtypeStruct((N * N, 64, ROWS), BF)
    grads = jax.ShapeDtypeStruct((seqs, LANES, ROWS), BF)
    return pl.pallas_call(
        attention_kernel,
        out_shape=(piece, piece, jax.ShapeDtypeStruct(q.shape, BF), *[grads] * N),
        in_specs=[vmem] * 8,
        out_specs=(vmem,) * 7,
        scratch_shapes=[
            pltpu.VMEM((seqs, 4 * ROWS, LANES), BF),
            pltpu.VMEM((seqs, LANES, 4 * ROWS), BF),
            pltpu.VMEM((seqs, 4 * ROWS, KEYS), F32),
            pltpu.VMEM((seqs, 4 * ROWS, KEYS), BF),
            pltpu.VMEM((seqs, 2, ROWS, LANES), F32),
        ],
        compiler_params=pltpu.CompilerParams(vmem_limit_bytes=32 * 2**20),
        cost_estimate=pl.CostEstimate(
            flops=5 * 2 * 2**25, bytes_accessed=6 * 2**20, transcendentals=2**20
        ),
    )(q, g, o, *kvs, bias)


def place_kernel(first, x_ref, *refs):
    out_ref, wide, sem = refs[-3:]
    core = lax.axis_index("core")
    head = core if first else 1 - core
    copies = []
    for j in range(N):
        for x in range(N):
            wide[j, x * 64 : (x + 1) * 64, :] = x_ref[x, j].astype(F32)
        copies.append(pltpu.make_async_copy(wide.at[j], out_ref.at[2 * j + head], sem.at[j]))
        copies[-1].start()
    for c in copies:
        c.wait()


def place(x, before=None):
    first = before is None
    anywhere, vmem = pl.BlockSpec(memory_space=pl.ANY), pl.BlockSpec(memory_space=pltpu.VMEM)
    return pl.pallas_call(
        lambda *refs: place_kernel(first, *refs),
        out_shape=jax.ShapeDtypeStruct((2 * N, ROWS, ROWS), F32),
        in_specs=[vmem] if first else [vmem, anywhere],
        out_specs=anywhere,
        scratch_shapes=[pltpu.VMEM((N, ROWS, ROWS), F32), pltpu.SemaphoreType.DMA((N,))],
        input_output_aliases={} if first else {1: 0},
        compiler_params=pltpu.CompilerParams(vmem_limit_bytes=8 * 2**20),
        cost_estimate=pl.CostEstimate(flops=2**18, bytes_accessed=3 * 2**19, transcendentals=0),
    )(*([x] if first else [x, before]))


def swap(x, axis, pairs):
    return lax.ppermute(x, axis, [(a, b) for a, b in pairs] + [(b, a) for a, b in pairs])


def add(a, b):
    return (a.astype(F32) + b.astype(F32)).astype(BF)


def body(query_proj, key_proj, value_proj, pair_bias, attn_output, output_grad):
    q, k, v, o, g = (
        jnp.swapaxes(x, 1, 2)
        for x in (query_proj, key_proj, value_proj, attn_output, output_grad)
    )
    grid = [(a, b) for a in range(N) for b in range(N)]

    kv = jnp.concatenate([k, v], axis=1)
    kvs = [
        lax.ppermute(kv, ("ri", "rj"), [(a * N + b, (b + t) % N * N + a) for a, b in grid])
        for t in range(N)
    ]
    bias = lax.all_to_all(pair_bias, "rj", 0, 0, tiled=True).reshape(N, 2, ROWS, ROWS)

    send, keep, dq, *parts = attention(q, g, o, kvs, bias)

    def home(part, t):
        return lax.ppermute(
            part, ("ri", "rj"), [((b + t) % N * N + a, a * N + b) for a, b in grid]
        )

    total = add(keep, swap(send, "core", [(0, 1)]))
    back = [home(part, t) for t, part in enumerate(parts)]
    spread = lax.all_to_all(total, ("x", "rj"), 0, 0, tiled=True)
    spread, *back = lax.optimization_barrier((spread, *back))
    total = jnp.sum(spread.reshape(N, N, 64, ROWS).astype(F32), axis=0).astype(BF)
    for pairs in ([(0, 1), (2, 3)], [(1, 2), (3, 0)]):
        total = add(total, swap(total, "zh", pairs))
    mine = lax.all_gather(total, "x", axis=0)
    bias_grad = place(swap(mine, "core", [(0, 1)]), place(mine))

    kv_grad = sum(x.astype(F32) for x in back).astype(BF)
    width = k.shape[1]
    grads = (dq, kv_grad[:, :width], kv_grad[:, width:])
    return *(jnp.swapaxes(x, 1, 2) for x in grads), bias_grad


def solution(mesh):
    split = Mesh(mesh.devices.reshape(N, N, 2, N, N), ("zh", "x", "core", "ri", "rj"))
    seq = ("zh", "x", "core")
    rows, keys, tile = P(seq, "ri", "rj"), P(seq, "rj", "ri"), P(None, "ri", "rj")
    return jax.shard_map(
        body,
        mesh=split,
        in_specs=(rows, keys, keys, tile, rows, rows),
        out_specs=(rows, keys, keys, tile),
        check_vma=False,
    )
```

```python
import jax
import jax.numpy as jnp
from jax import lax
from jax.experimental import pallas as pl
from jax.experimental.pallas import tpu as pltpu
from jax.sharding import Mesh
from jax.sharding import PartitionSpec as P

HEAD = 32
SCALE = HEAD**-0.5
N = 4
ROWS = 256
KEYS = N * ROWS
LANES = 128
CHUNK = 32
UNROLL = 4
BF = jnp.bfloat16
F32 = jnp.float32
NT = (((1,), (1,)), ((), ()))
NN = (((1,), (0,)), ((), ()))


def attention_kernel(
    q_ref, g_ref, o_ref, kv0, kv1, kv2, kv3, bias,
    send, keep, dq_ref, dkv_ref,
    stack, wide, raw, low, inner,
):
    ri, rj, core = (lax.axis_index(a) for a in ("ri", "rj", "core"))
    kvs = (kv0, kv1, kv2, kv3)
    blocks = [lax.rem(ri + N - t, N) for t in range(N)]
    channel = lax.broadcasted_iota(jnp.int32, (LANES, ROWS), 0) // HEAD

    for s in range(2):
        both = jnp.concatenate([q_ref[s], g_ref[s]], axis=0)
        for part in range(4):
            at = slice(part * ROWS, (part + 1) * ROWS)
            one = jnp.where(channel == part, both, 0)
            wide[s, :, at] = one
            stack[s, at, :] = one.T
        dots = g_ref[s].astype(F32) * o_ref[s].astype(F32)
        for h in range(2):
            sums = jnp.sum(dots[h * HEAD : (h + 1) * HEAD], axis=0, keepdims=True)
            inner[s, h] = jnp.broadcast_to(sums, (LANES, ROWS)).T

    for s in range(2):
        for t in range(N):
            at = slice(t * ROWS, (t + 1) * ROWS)
            raw[s, :, at] = lax.dot_general(stack[s], kvs[t][s], NN, preferred_element_type=F32)

    for out, h in ((send, 1 - core), (keep, core)):

        @pl.loop(0, ROWS // CHUNK, unroll=UNROLL)
        def _(i):
            r0 = pl.multiple_of(i * CHUNK, CHUNK)
            at_logits = pl.ds(pl.multiple_of(h * ROWS + r0, CHUNK), CHUNK)
            at_grads = pl.ds(pl.multiple_of((2 + h) * ROWS + r0, CHUNK), CHUNK)
            rows = pl.ds(r0, CHUNK)
            pair = jnp.concatenate([bias[b, h, rows, :] for b in blocks], axis=1).astype(F32)
            total = None
            for s in range(2):
                logits = raw[s, at_logits, :] * SCALE + pair
                top = jnp.max(logits, axis=1, keepdims=True)
                weights = jnp.exp(logits - top)
                weights = weights * (1.0 / jnp.sum(weights, axis=1, keepdims=True))
                dots = jnp.concatenate([inner[s, h, rows, :]] * (KEYS // LANES), axis=1)
                grad = weights * (raw[s, at_grads, :] - dots)
                low[s, at_logits, :] = grad.astype(BF)
                low[s, at_grads, :] = weights.astype(BF)
                total = grad if total is None else total + grad
            total = total.astype(BF)
            quarter = i // (64 // CHUNK)
            within = pl.ds(pl.multiple_of(lax.rem(i, 64 // CHUNK) * CHUNK, CHUNK), CHUNK)
            for t, b in enumerate(blocks):
                out[quarter * N + b, within, :] = total[:, t * ROWS : (t + 1) * ROWS]

    for s in range(2):
        for t, b in enumerate(blocks):
            at = slice(t * ROWS, (t + 1) * ROWS)
            grads = lax.dot_general(wide[s], low[s, :, at], NN, preferred_element_type=F32)
            grads = jnp.where(channel < 2, grads * SCALE, grads)
            dkv_ref[lax.rem(b + N - rj, N), s] = grads.astype(BF)
        grads = None
        for t in range(N):
            at = slice(t * ROWS, (t + 1) * ROWS)
            term = lax.dot_general(
                low[s, : 2 * ROWS, at], kvs[t][s], NT, preferred_element_type=F32
            )
            grads = term if grads is None else grads + term
        for h in range(2):
            mine = grads[h * ROWS : (h + 1) * ROWS].T[h * HEAD : (h + 1) * HEAD]
            dq_ref[s, h * HEAD : (h + 1) * HEAD, :] = (mine * SCALE).astype(BF)


def attention(q, g, o, kvs, bias):
    seqs = q.shape[0]
    vmem = pl.BlockSpec(memory_space=pltpu.VMEM)
    piece = jax.ShapeDtypeStruct((N * N, 64, ROWS), BF)
    grads = jax.ShapeDtypeStruct((N, seqs, LANES, ROWS), BF)
    return pl.pallas_call(
        attention_kernel,
        out_shape=(piece, piece, jax.ShapeDtypeStruct(q.shape, BF), grads),
        in_specs=[vmem] * 8,
        out_specs=(vmem,) * 4,
        scratch_shapes=[
            pltpu.VMEM((seqs, 4 * ROWS, LANES), BF),
            pltpu.VMEM((seqs, LANES, 4 * ROWS), BF),
            pltpu.VMEM((seqs, 4 * ROWS, KEYS), F32),
            pltpu.VMEM((seqs, 4 * ROWS, KEYS), BF),
            pltpu.VMEM((seqs, 2, ROWS, LANES), F32),
        ],
        compiler_params=pltpu.CompilerParams(vmem_limit_bytes=32 * 2**20),
        cost_estimate=pl.CostEstimate(
            flops=5 * 2 * 2**25, bytes_accessed=6 * 2**20, transcendentals=2**20
        ),
    )(q, g, o, *kvs, bias)


def split_kernel(after, x_ref, *outs):
    for t, out in enumerate(outs):
        out[...] = x_ref[t]


def choose_kernel(after, *refs):
    ri, rj = lax.axis_index("ri"), lax.axis_index("rj")
    for t, out in enumerate(refs[N:]):
        wanted = lax.rem(rj + 2 * N - ri - t, N)
        for source, x_ref in enumerate(refs[:N]):

            @pl.when(wanted == source)
            def _():
                out[...] = x_ref[...]


def hand_on(kernel, after, *args):
    anywhere, vmem = pl.BlockSpec(memory_space=pl.ANY), pl.BlockSpec(memory_space=pltpu.VMEM)
    return pl.pallas_call(
        kernel,
        out_shape=[jax.ShapeDtypeStruct(args[0].shape[-3:], BF)] * N,
        in_specs=[anywhere] + [vmem] * len(args),
        out_specs=[vmem] * N,
        compiler_params=pltpu.CompilerParams(vmem_limit_bytes=8 * 2**20),
        cost_estimate=pl.CostEstimate(flops=0, bytes_accessed=2**21, transcendentals=0),
    )(after, *args)


def place_kernel(first, x_ref, *refs):
    out_ref, wide, sem = refs[-3:]
    core = lax.axis_index("core")
    head = core if first else 1 - core
    copies = []
    for j in range(N):
        for x in range(N):
            wide[j, x * 64 : (x + 1) * 64, :] = x_ref[x, j].astype(F32)
        copies.append(pltpu.make_async_copy(wide.at[j], out_ref.at[2 * j + head], sem.at[j]))
        copies[-1].start()
    for c in copies:
        c.wait()


def place(x, before=None):
    first = before is None
    anywhere, vmem = pl.BlockSpec(memory_space=pl.ANY), pl.BlockSpec(memory_space=pltpu.VMEM)
    return pl.pallas_call(
        lambda *refs: place_kernel(first, *refs),
        out_shape=jax.ShapeDtypeStruct((2 * N, ROWS, ROWS), F32),
        in_specs=[vmem] if first else [vmem, anywhere],
        out_specs=anywhere,
        scratch_shapes=[pltpu.VMEM((N, ROWS, ROWS), F32), pltpu.SemaphoreType.DMA((N,))],
        input_output_aliases={} if first else {1: 0},
        compiler_params=pltpu.CompilerParams(vmem_limit_bytes=8 * 2**20),
        cost_estimate=pl.CostEstimate(flops=2**18, bytes_accessed=3 * 2**19, transcendentals=0),
    )(*([x] if first else [x, before]))


def swap(x, axis, pairs):
    return lax.ppermute(x, axis, [(a, b) for a, b in pairs] + [(b, a) for a, b in pairs])


def add(a, b):
    return (a.astype(F32) + b.astype(F32)).astype(BF)


def body(query_proj, key_proj, value_proj, pair_bias, attn_output, output_grad):
    q, k, v, o, g = (
        jnp.swapaxes(x, 1, 2)
        for x in (query_proj, key_proj, value_proj, attn_output, output_grad)
    )
    grid = [(a, b) for a in range(N) for b in range(N)]

    kv = jnp.concatenate([k, v], axis=1)
    kvs = [
        lax.ppermute(kv, ("ri", "rj"), [(a * N + b, (b + t) % N * N + a) for a, b in grid])
        for t in range(N)
    ]
    bias = lax.all_to_all(pair_bias, "rj", 0, 0, tiled=True).reshape(N, 2, ROWS, ROWS)

    send, keep, dq, dkv = attention(q, g, o, kvs, bias)

    def spread_out(parts, axis):
        return [parts[0]] + [
            lax.ppermute(parts[t], axis, [(a, (a + t) % N) for a in range(N)])
            for t in range(1, N)
        ]

    total = add(keep, swap(send, "core", [(0, 1)]))
    spread = lax.all_to_all(total, ("x", "rj"), 0, 0, tiled=True)
    total = jnp.sum(spread.reshape(N, N, 64, ROWS).astype(F32), axis=0).astype(BF)
    other = swap(total, "zh", [(0, 1), (2, 3)])
    parts = spread_out(hand_on(split_kernel, total, dkv), "rj")
    total = add(total, other)
    other = swap(total, "zh", [(1, 2), (3, 0)])
    parts = spread_out(hand_on(choose_kernel, total, *parts), "ri")
    total = add(total, other)
    mine = lax.all_gather(total, "x", axis=0)
    bias_grad = place(swap(mine, "core", [(0, 1)]), place(mine))

    kv_grad = sum(x.astype(F32) for x in parts).astype(BF)
    width = k.shape[1]
    grads = (dq, kv_grad[:, :width], kv_grad[:, width:])
    return *(jnp.swapaxes(x, 1, 2) for x in grads), bias_grad


def solution(mesh):
    split = Mesh(mesh.devices.reshape(N, N, 2, N, N), ("zh", "x", "core", "ri", "rj"))
    seq = ("zh", "x", "core")
    rows, keys, tile = P(seq, "ri", "rj"), P(seq, "rj", "ri"), P(None, "ri", "rj")
    return jax.shard_map(
        body,
        mesh=split,
        in_specs=(rows, keys, keys, tile, rows, rows),
        out_specs=(rows, keys, keys, tile),
        check_vma=False,
    )
```

```python
import jax
import jax.numpy as jnp
from jax import lax
from jax.experimental import pallas as pl
from jax.experimental.pallas import tpu as pltpu
from jax.sharding import Mesh
from jax.sharding import PartitionSpec as P

HEAD = 32
SCALE = HEAD**-0.5
N = 4
ROWS = 256
KEYS = N * ROWS
LANES = 128
CHUNK = 32
UNROLL = 4
BF = jnp.bfloat16
F32 = jnp.float32
NT = (((1,), (1,)), ((), ()))
NN = (((1,), (0,)), ((), ()))


def attention_kernel(
    q_ref, g_ref, o_ref, kv0, kv1, kv2, kv3, bias,
    send, keep, dq_ref, dkv_ref,
    stack, wide, raw, low, inner,
):
    ri, rj, core = (lax.axis_index(a) for a in ("ri", "rj", "core"))
    kvs = (kv0, kv1, kv2, kv3)
    blocks = [lax.rem(ri + N - t, N) for t in range(N)]
    channel = lax.broadcasted_iota(jnp.int32, (LANES, ROWS), 0) // HEAD

    for s in range(2):
        both = jnp.concatenate([q_ref[s], g_ref[s]], axis=0)
        for part in range(4):
            at = slice(part * ROWS, (part + 1) * ROWS)
            one = jnp.where(channel == part, both, 0)
            wide[s, :, at] = one
            stack[s, at, :] = one.T
        dots = g_ref[s].astype(F32) * o_ref[s].astype(F32)
        for h in range(2):
            sums = jnp.sum(dots[h * HEAD : (h + 1) * HEAD], axis=0, keepdims=True)
            inner[s, h] = jnp.broadcast_to(sums, (LANES, ROWS)).T

    for s in range(2):
        for t in range(N):
            at = slice(t * ROWS, (t + 1) * ROWS)
            raw[s, :, at] = lax.dot_general(stack[s], kvs[t][s], NN, preferred_element_type=F32)

    for out, h in ((send, 1 - core), (keep, core)):

        @pl.loop(0, ROWS // CHUNK, unroll=UNROLL)
        def _(i):
            r0 = pl.multiple_of(i * CHUNK, CHUNK)
            at_logits = pl.ds(pl.multiple_of(h * ROWS + r0, CHUNK), CHUNK)
            at_grads = pl.ds(pl.multiple_of((2 + h) * ROWS + r0, CHUNK), CHUNK)
            rows = pl.ds(r0, CHUNK)
            pair = jnp.concatenate([bias[b, h, rows, :] for b in blocks], axis=1).astype(F32)
            total = None
            for s in range(2):
                logits = raw[s, at_logits, :] * SCALE + pair
                top = jnp.max(logits, axis=1, keepdims=True)
                weights = jnp.exp(logits - top)
                weights = weights * (1.0 / jnp.sum(weights, axis=1, keepdims=True))
                dots = jnp.concatenate([inner[s, h, rows, :]] * (KEYS // LANES), axis=1)
                grad = weights * (raw[s, at_grads, :] - dots)
                low[s, at_logits, :] = grad.astype(BF)
                low[s, at_grads, :] = weights.astype(BF)
                total = grad if total is None else total + grad
            total = total.astype(BF)
            quarter = i // (64 // CHUNK)
            within = pl.ds(pl.multiple_of(lax.rem(i, 64 // CHUNK) * CHUNK, CHUNK), CHUNK)
            for t, b in enumerate(blocks):
                out[quarter * N + b, within, :] = total[:, t * ROWS : (t + 1) * ROWS]

    for s in range(2):
        for t, b in enumerate(blocks):
            at = slice(t * ROWS, (t + 1) * ROWS)
            grads = lax.dot_general(wide[s], low[s, :, at], NN, preferred_element_type=F32)
            grads = jnp.where(channel < 2, grads * SCALE, grads)
            dkv_ref[lax.rem(b + N - rj, N), s] = grads.astype(BF)
        grads = None
        for t in range(N):
            at = slice(t * ROWS, (t + 1) * ROWS)
            term = lax.dot_general(
                low[s, : 2 * ROWS, at], kvs[t][s], NT, preferred_element_type=F32
            )
            grads = term if grads is None else grads + term
        for h in range(2):
            mine = grads[h * ROWS : (h + 1) * ROWS].T[h * HEAD : (h + 1) * HEAD]
            dq_ref[s, h * HEAD : (h + 1) * HEAD, :] = (mine * SCALE).astype(BF)


def attention(q, g, o, kvs, bias):
    seqs = q.shape[0]
    vmem = pl.BlockSpec(memory_space=pltpu.VMEM)
    piece = jax.ShapeDtypeStruct((N * N, 64, ROWS), BF)
    grads = jax.ShapeDtypeStruct((N, seqs, LANES, ROWS), BF)
    return pl.pallas_call(
        attention_kernel,
        out_shape=(piece, piece, jax.ShapeDtypeStruct(q.shape, BF), grads),
        in_specs=[vmem] * 8,
        out_specs=(vmem,) * 4,
        scratch_shapes=[
            pltpu.VMEM((seqs, 4 * ROWS, LANES), BF),
            pltpu.VMEM((seqs, LANES, 4 * ROWS), BF),
            pltpu.VMEM((seqs, 4 * ROWS, KEYS), F32),
            pltpu.VMEM((seqs, 4 * ROWS, KEYS), BF),
            pltpu.VMEM((seqs, 2, ROWS, LANES), F32),
        ],
        compiler_params=pltpu.CompilerParams(vmem_limit_bytes=32 * 2**20),
        cost_estimate=pl.CostEstimate(
            flops=5 * 2 * 2**25, bytes_accessed=6 * 2**20, transcendentals=2**20
        ),
    )(q, g, o, *kvs, bias)


def split_kernel(after, x_ref, *outs):
    for t, out in enumerate(outs):
        out[...] = x_ref[t]


def choose_kernel(after, *refs):
    ri, rj = lax.axis_index("ri"), lax.axis_index("rj")
    for t, out in enumerate(refs[N:]):
        wanted = lax.rem(rj + 2 * N - ri - t, N)
        for source, x_ref in enumerate(refs[:N]):

            @pl.when(wanted == source)
            def _():
                out[...] = x_ref[...]


def hand_on(kernel, after, *args):
    anywhere, vmem = pl.BlockSpec(memory_space=pl.ANY), pl.BlockSpec(memory_space=pltpu.VMEM)
    return pl.pallas_call(
        kernel,
        out_shape=[jax.ShapeDtypeStruct(args[0].shape[-3:], BF)] * N,
        in_specs=[anywhere] + [vmem] * len(args),
        out_specs=[vmem] * N,
        compiler_params=pltpu.CompilerParams(vmem_limit_bytes=8 * 2**20),
        cost_estimate=pl.CostEstimate(flops=0, bytes_accessed=2**21, transcendentals=0),
    )(after, *args)


def place_kernel(first, x_ref, *refs):
    out_ref, wide, sem = refs[-3:]
    core = lax.axis_index("core")
    head = core if first else 1 - core
    copies = []
    for j in range(N):
        for x in range(N):
            wide[j, x * 64 : (x + 1) * 64, :] = x_ref[x, j].astype(F32)
        copies.append(pltpu.make_async_copy(wide.at[j], out_ref.at[2 * j + head], sem.at[j]))
        copies[-1].start()
    for c in copies:
        c.wait()


def place(x, before=None):
    first = before is None
    anywhere, vmem = pl.BlockSpec(memory_space=pl.ANY), pl.BlockSpec(memory_space=pltpu.VMEM)
    return pl.pallas_call(
        lambda *refs: place_kernel(first, *refs),
        out_shape=jax.ShapeDtypeStruct((2 * N, ROWS, ROWS), F32),
        in_specs=[vmem] if first else [vmem, anywhere],
        out_specs=anywhere,
        scratch_shapes=[pltpu.VMEM((N, ROWS, ROWS), F32), pltpu.SemaphoreType.DMA((N,))],
        input_output_aliases={} if first else {1: 0},
        compiler_params=pltpu.CompilerParams(vmem_limit_bytes=8 * 2**20),
        cost_estimate=pl.CostEstimate(flops=2**18, bytes_accessed=3 * 2**19, transcendentals=0),
    )(*([x] if first else [x, before]))


def swap(x, axis, pairs):
    return lax.ppermute(x, axis, [(a, b) for a, b in pairs] + [(b, a) for a, b in pairs])


def add(a, b):
    return (a.astype(F32) + b.astype(F32)).astype(BF)


def spread_out(parts, axis):
    steps = ([(a, (a + t) % N) for a in range(N)] for t in range(N))
    moved = [lax.ppermute(part, axis, step) for part, step in zip(parts[1:], list(steps)[1:])]
    return [parts[0], *moved]


def body(query_proj, key_proj, value_proj, pair_bias, attn_output, output_grad):
    q, k, v, o, g = (
        jnp.swapaxes(x, 1, 2)
        for x in (query_proj, key_proj, value_proj, attn_output, output_grad)
    )
    grid = [(a, b) for a in range(N) for b in range(N)]

    kv = jnp.concatenate([k, v], axis=1)
    kv = lax.ppermute(kv, ("ri", "rj"), [(a * N + b, b * N + a) for a, b in grid])
    kvs = spread_out([kv] * N, "ri")
    bias = lax.all_to_all(pair_bias, "rj", 0, 0, tiled=True).reshape(N, 2, ROWS, ROWS)

    send, keep, dq, dkv = attention(q, g, o, kvs, bias)

    total = add(keep, swap(send, "core", [(0, 1)]))
    spread = lax.all_to_all(total, ("x", "rj"), 0, 0, tiled=True)
    total = jnp.sum(spread.reshape(N, N, 64, ROWS).astype(F32), axis=0).astype(BF)
    other = swap(total, "zh", [(0, 1), (2, 3)])
    parts = spread_out(hand_on(split_kernel, total, dkv), "rj")
    total = add(total, other)
    other = swap(total, "zh", [(1, 2), (3, 0)])
    parts = spread_out(hand_on(choose_kernel, total, *parts), "ri")
    total = add(total, other)
    mine = lax.all_gather(total, "x", axis=0)
    bias_grad = place(swap(mine, "core", [(0, 1)]), place(mine))

    kv_grad = sum(x.astype(F32) for x in parts).astype(BF)
    width = k.shape[1]
    grads = (dq, kv_grad[:, :width], kv_grad[:, width:])
    return *(jnp.swapaxes(x, 1, 2) for x in grads), bias_grad


def solution(mesh):
    split = Mesh(mesh.devices.reshape(N, N, 2, N, N), ("zh", "x", "core", "ri", "rj"))
    seq = ("zh", "x", "core")
    rows, keys, tile = P(seq, "ri", "rj"), P(seq, "rj", "ri"), P(None, "ri", "rj")
    return jax.shard_map(
        body,
        mesh=split,
        in_specs=(rows, keys, keys, tile, rows, rows),
        out_specs=(rows, keys, keys, tile),
        check_vma=False,
    )
```

```python
import jax
import jax.numpy as jnp
from jax import lax
from jax.experimental import pallas as pl
from jax.experimental.pallas import tpu as pltpu
from jax.sharding import Mesh
from jax.sharding import PartitionSpec as P

HEAD = 32
SCALE = HEAD**-0.5
N = 4
ROWS = 256
KEYS = N * ROWS
LANES = 128
CHUNK = 32
UNROLL = 4
BF = jnp.bfloat16
F32 = jnp.float32
NT = (((1,), (1,)), ((), ()))
NN = (((1,), (0,)), ((), ()))


def attention_kernel(
    q_ref, g_ref, o_ref, kv0, kv1, kv2, kv3, bias,
    send, keep, dq_ref, dkv_ref,
    stack, wide, raw, low, inner,
):
    ri, rj, core = (lax.axis_index(a) for a in ("ri", "rj", "core"))
    kvs = (kv0, kv1, kv2, kv3)
    blocks = [lax.rem(ri + N - t, N) for t in range(N)]
    channel = lax.broadcasted_iota(jnp.int32, (LANES, ROWS), 0) // HEAD

    for s in range(2):
        both = jnp.concatenate([q_ref[s], g_ref[s]], axis=0)
        for part in range(4):
            at = slice(part * ROWS, (part + 1) * ROWS)
            one = jnp.where(channel == part, both, 0)
            wide[s, :, at] = one
            stack[s, at, :] = one.T
        dots = g_ref[s].astype(F32) * o_ref[s].astype(F32)
        for h in range(2):
            sums = jnp.sum(dots[h * HEAD : (h + 1) * HEAD], axis=0, keepdims=True)
            inner[s, h] = jnp.broadcast_to(sums, (LANES, ROWS)).T

    for s in range(2):
        for t in range(N):
            at = slice(t * ROWS, (t + 1) * ROWS)
            raw[s, :, at] = lax.dot_general(stack[s], kvs[t][s], NN, preferred_element_type=F32)

    for out, h in ((send, 1 - core), (keep, core)):

        @pl.loop(0, ROWS // CHUNK, unroll=UNROLL)
        def _(i):
            r0 = pl.multiple_of(i * CHUNK, CHUNK)
            at_logits = pl.ds(pl.multiple_of(h * ROWS + r0, CHUNK), CHUNK)
            at_grads = pl.ds(pl.multiple_of((2 + h) * ROWS + r0, CHUNK), CHUNK)
            rows = pl.ds(r0, CHUNK)
            pair = jnp.concatenate([bias[b, h, rows, :] for b in blocks], axis=1).astype(F32)
            total = None
            for s in range(2):
                logits = raw[s, at_logits, :] * SCALE + pair
                top = jnp.max(logits, axis=1, keepdims=True)
                weights = jnp.exp(logits - top)
                weights = weights * (1.0 / jnp.sum(weights, axis=1, keepdims=True))
                dots = jnp.concatenate([inner[s, h, rows, :]] * (KEYS // LANES), axis=1)
                grad = weights * (raw[s, at_grads, :] - dots)
                low[s, at_logits, :] = grad.astype(BF)
                low[s, at_grads, :] = weights.astype(BF)
                total = grad if total is None else total + grad
            total = total.astype(BF)
            quarter = i // (64 // CHUNK)
            within = pl.ds(pl.multiple_of(lax.rem(i, 64 // CHUNK) * CHUNK, CHUNK), CHUNK)
            for t, b in enumerate(blocks):
                out[quarter * N + b, within, :] = total[:, t * ROWS : (t + 1) * ROWS]

    for s in range(2):
        for t, b in enumerate(blocks):
            at = slice(t * ROWS, (t + 1) * ROWS)
            grads = lax.dot_general(wide[s], low[s, :, at], NN, preferred_element_type=F32)
            grads = jnp.where(channel < 2, grads * SCALE, grads)
            dkv_ref[lax.rem(b + N - rj, N), s] = grads.astype(BF)
        grads = None
        for t in range(N):
            at = slice(t * ROWS, (t + 1) * ROWS)
            term = lax.dot_general(
                low[s, : 2 * ROWS, at], kvs[t][s], NT, preferred_element_type=F32
            )
            grads = term if grads is None else grads + term
        for h in range(2):
            mine = grads[h * ROWS : (h + 1) * ROWS].T[h * HEAD : (h + 1) * HEAD]
            dq_ref[s, h * HEAD : (h + 1) * HEAD, :] = (mine * SCALE).astype(BF)


def attention(q, g, o, kvs, bias):
    seqs = q.shape[0]
    vmem = pl.BlockSpec(memory_space=pltpu.VMEM)
    piece = jax.ShapeDtypeStruct((N * N, 64, ROWS), BF)
    grads = jax.ShapeDtypeStruct((N, seqs, LANES, ROWS), BF)
    return pl.pallas_call(
        attention_kernel,
        out_shape=(piece, piece, jax.ShapeDtypeStruct(q.shape, BF), grads),
        in_specs=[vmem] * 8,
        out_specs=(vmem,) * 4,
        scratch_shapes=[
            pltpu.VMEM((seqs, 4 * ROWS, LANES), BF),
            pltpu.VMEM((seqs, LANES, 4 * ROWS), BF),
            pltpu.VMEM((seqs, 4 * ROWS, KEYS), F32),
            pltpu.VMEM((seqs, 4 * ROWS, KEYS), BF),
            pltpu.VMEM((seqs, 2, ROWS, LANES), F32),
        ],
        compiler_params=pltpu.CompilerParams(vmem_limit_bytes=32 * 2**20),
        cost_estimate=pl.CostEstimate(
            flops=5 * 2 * 2**25, bytes_accessed=6 * 2**20, transcendentals=2**20
        ),
    )(q, g, o, *kvs, bias)


def split_kernel(after, x_ref, *outs):
    for t, out in enumerate(outs):
        out[...] = x_ref[t]


def choose_kernel(after, *refs):
    ri, rj = lax.axis_index("ri"), lax.axis_index("rj")
    for t, out in enumerate(refs[N:]):
        wanted = lax.rem(rj + 2 * N - ri - t, N)
        for source, x_ref in enumerate(refs[:N]):

            @pl.when(wanted == source)
            def _():
                out[...] = x_ref[...]


def hand_on(kernel, after, *args):
    anywhere, vmem = pl.BlockSpec(memory_space=pl.ANY), pl.BlockSpec(memory_space=pltpu.VMEM)
    return pl.pallas_call(
        kernel,
        out_shape=[jax.ShapeDtypeStruct(args[0].shape[-3:], BF)] * N,
        in_specs=[anywhere] + [vmem] * len(args),
        out_specs=[vmem] * N,
        compiler_params=pltpu.CompilerParams(vmem_limit_bytes=8 * 2**20),
        cost_estimate=pl.CostEstimate(flops=0, bytes_accessed=2**21, transcendentals=0),
    )(after, *args)


def place_kernel(first, x_ref, *refs):
    out_ref, wide, sem = refs[-3:]
    core = lax.axis_index("core")
    head = core if first else 1 - core
    copies = []
    for j in range(N):
        for x in range(N):
            wide[j, x * 64 : (x + 1) * 64, :] = x_ref[x, j].astype(F32)
        copies.append(pltpu.make_async_copy(wide.at[j], out_ref.at[2 * j + head], sem.at[j]))
        copies[-1].start()
    for c in copies:
        c.wait()


def place(x, before=None):
    first = before is None
    anywhere, vmem = pl.BlockSpec(memory_space=pl.ANY), pl.BlockSpec(memory_space=pltpu.VMEM)
    return pl.pallas_call(
        lambda *refs: place_kernel(first, *refs),
        out_shape=jax.ShapeDtypeStruct((2 * N, ROWS, ROWS), F32),
        in_specs=[vmem] if first else [vmem, anywhere],
        out_specs=anywhere,
        scratch_shapes=[pltpu.VMEM((N, ROWS, ROWS), F32), pltpu.SemaphoreType.DMA((N,))],
        input_output_aliases={} if first else {1: 0},
        compiler_params=pltpu.CompilerParams(vmem_limit_bytes=8 * 2**20),
        cost_estimate=pl.CostEstimate(flops=2**18, bytes_accessed=3 * 2**19, transcendentals=0),
    )(*([x] if first else [x, before]))


def swap(x, axis, pairs):
    return lax.ppermute(x, axis, [(a, b) for a, b in pairs] + [(b, a) for a, b in pairs])


def add(a, b):
    return (a.astype(F32) + b.astype(F32)).astype(BF)


def spread_out(parts, axis):
    steps = ([(a, (a + t) % N) for a in range(N)] for t in range(N))
    moved = [lax.ppermute(part, axis, step) for part, step in zip(parts[1:], list(steps)[1:])]
    return [parts[0], *moved]


def body(query_proj, key_proj, value_proj, pair_bias, attn_output, output_grad):
    q, k, v, o, g = (
        jnp.swapaxes(x, 1, 2)
        for x in (query_proj, key_proj, value_proj, attn_output, output_grad)
    )
    grid = [(a, b) for a in range(N) for b in range(N)]

    kv = jnp.concatenate([k, v], axis=1)
    kv = lax.ppermute(kv, ("ri", "rj"), [(a * N + b, b * N + a) for a, b in grid])
    pair_bias, kv = lax.optimization_barrier((pair_bias, kv))
    kvs = spread_out([kv] * N, "ri")
    bias = lax.all_to_all(pair_bias, "rj", 0, 0, tiled=True).reshape(N, 2, ROWS, ROWS)

    send, keep, dq, dkv = attention(q, g, o, kvs, bias)

    total = add(keep, swap(send, "core", [(0, 1)]))
    spread = lax.all_to_all(total, ("x", "rj"), 0, 0, tiled=True)
    total = jnp.sum(spread.reshape(N, N, 64, ROWS).astype(F32), axis=0).astype(BF)
    other = swap(total, "zh", [(0, 1), (2, 3)])
    parts = spread_out(hand_on(split_kernel, total, dkv), "rj")
    total = add(total, other)
    other = swap(total, "zh", [(1, 2), (3, 0)])
    parts = spread_out(hand_on(choose_kernel, total, *parts), "ri")
    total = add(total, other)
    mine = lax.all_gather(total, "x", axis=0)
    bias_grad = place(swap(mine, "core", [(0, 1)]), place(mine))

    kv_grad = sum(x.astype(F32) for x in parts).astype(BF)
    width = k.shape[1]
    grads = (dq, kv_grad[:, :width], kv_grad[:, width:])
    return *(jnp.swapaxes(x, 1, 2) for x in grads), bias_grad


def solution(mesh):
    split = Mesh(mesh.devices.reshape(N, N, 2, N, N), ("zh", "x", "core", "ri", "rj"))
    seq = ("zh", "x", "core")
    rows, keys, tile = P(seq, "ri", "rj"), P(seq, "rj", "ri"), P(None, "ri", "rj")
    return jax.shard_map(
        body,
        mesh=split,
        in_specs=(rows, keys, keys, tile, rows, rows),
        out_specs=(rows, keys, keys, tile),
        check_vma=False,
    )
```

```python
import jax
import jax.numpy as jnp
from jax import lax
from jax.experimental import pallas as pl
from jax.experimental.pallas import tpu as pltpu
from jax.sharding import Mesh
from jax.sharding import PartitionSpec as P

HEAD = 32
SCALE = HEAD**-0.5
N = 4
ROWS = 256
KEYS = N * ROWS
LANES = 128
CHUNK = 32
UNROLL = 4
BF = jnp.bfloat16
F32 = jnp.float32
NT = (((1,), (1,)), ((), ()))
NN = (((1,), (0,)), ((), ()))


def attention_kernel(
    q_ref, g_ref, o_ref, kv0, kv1, kv2, kv3, bias,
    send, keep, dq_ref, dkv_ref,
    stack, wide, raw, low, inner,
):
    ri, core = lax.axis_index("ri"), lax.axis_index("core")
    kvs = (kv0, kv1, kv2, kv3)
    blocks = [lax.rem(ri + N - t, N) for t in range(N)]
    channel = lax.broadcasted_iota(jnp.int32, (LANES, ROWS), 0) // HEAD

    for s in range(2):
        both = jnp.concatenate([q_ref[s], g_ref[s]], axis=0)
        for part in range(4):
            at = slice(part * ROWS, (part + 1) * ROWS)
            one = jnp.where(channel == part, both, 0)
            wide[s, :, at] = one
            stack[s, at, :] = one.T
        dots = g_ref[s].astype(F32) * o_ref[s].astype(F32)
        for h in range(2):
            sums = jnp.sum(dots[h * HEAD : (h + 1) * HEAD], axis=0, keepdims=True)
            inner[s, h] = jnp.broadcast_to(sums, (LANES, ROWS)).T

    for s in range(2):
        for t in range(N):
            at = slice(t * ROWS, (t + 1) * ROWS)
            raw[s, :, at] = lax.dot_general(stack[s], kvs[t][s], NN, preferred_element_type=F32)

    for out, h in ((send, 1 - core), (keep, core)):

        @pl.loop(0, ROWS // CHUNK, unroll=UNROLL)
        def _(i):
            r0 = pl.multiple_of(i * CHUNK, CHUNK)
            at_logits = pl.ds(pl.multiple_of(h * ROWS + r0, CHUNK), CHUNK)
            at_grads = pl.ds(pl.multiple_of((2 + h) * ROWS + r0, CHUNK), CHUNK)
            rows = pl.ds(r0, CHUNK)
            pair = jnp.concatenate([bias[b, h, rows, :] for b in blocks], axis=1).astype(F32)
            total = None
            for s in range(2):
                logits = raw[s, at_logits, :] * SCALE + pair
                top = jnp.max(logits, axis=1, keepdims=True)
                weights = jnp.exp(logits - top)
                weights = weights * (1.0 / jnp.sum(weights, axis=1, keepdims=True))
                dots = jnp.concatenate([inner[s, h, rows, :]] * (KEYS // LANES), axis=1)
                grad = weights * (raw[s, at_grads, :] - dots)
                low[s, at_logits, :] = grad.astype(BF)
                low[s, at_grads, :] = weights.astype(BF)
                total = grad if total is None else total + grad
            total = total.astype(BF)
            quarter = i // (64 // CHUNK)
            within = pl.ds(pl.multiple_of(lax.rem(i, 64 // CHUNK) * CHUNK, CHUNK), CHUNK)
            for t, b in enumerate(blocks):
                out[quarter * N + b, within, :] = total[:, t * ROWS : (t + 1) * ROWS]

    for s in range(2):
        for t, b in enumerate(blocks):
            at = slice(t * ROWS, (t + 1) * ROWS)
            grads = lax.dot_general(wide[s], low[s, :, at], NN, preferred_element_type=F32)
            grads = jnp.where(channel < 2, grads * SCALE, grads)
            dkv_ref[b, s] = grads.astype(BF)
        grads = None
        for t in range(N):
            at = slice(t * ROWS, (t + 1) * ROWS)
            term = lax.dot_general(
                low[s, : 2 * ROWS, at], kvs[t][s], NT, preferred_element_type=F32
            )
            grads = term if grads is None else grads + term
        for h in range(2):
            mine = grads[h * ROWS : (h + 1) * ROWS].T[h * HEAD : (h + 1) * HEAD]
            dq_ref[s, h * HEAD : (h + 1) * HEAD, :] = (mine * SCALE).astype(BF)


def attention(q, g, o, kvs, bias):
    seqs = q.shape[0]
    vmem = pl.BlockSpec(memory_space=pltpu.VMEM)
    piece = jax.ShapeDtypeStruct((N * N, 64, ROWS), BF)
    grads = jax.ShapeDtypeStruct((N, seqs, LANES, ROWS), BF)
    return pl.pallas_call(
        attention_kernel,
        out_shape=(piece, piece, jax.ShapeDtypeStruct(q.shape, BF), grads),
        in_specs=[vmem] * 8,
        out_specs=(vmem,) * 4,
        scratch_shapes=[
            pltpu.VMEM((seqs, 4 * ROWS, LANES), BF),
            pltpu.VMEM((seqs, LANES, 4 * ROWS), BF),
            pltpu.VMEM((seqs, 4 * ROWS, KEYS), F32),
            pltpu.VMEM((seqs, 4 * ROWS, KEYS), BF),
            pltpu.VMEM((seqs, 2, ROWS, LANES), F32),
        ],
        compiler_params=pltpu.CompilerParams(vmem_limit_bytes=32 * 2**20),
        cost_estimate=pl.CostEstimate(
            flops=5 * 2 * 2**25, bytes_accessed=6 * 2**20, transcendentals=2**20
        ),
    )(q, g, o, *kvs, bias)


def place_kernel(first, x_ref, *refs):
    out_ref, wide, sem = refs[-3:]
    core = lax.axis_index("core")
    head = core if first else 1 - core
    copies = []
    for j in range(N):
        for x in range(N):
            wide[j, x * 64 : (x + 1) * 64, :] = x_ref[x, j].astype(F32)
        copies.append(pltpu.make_async_copy(wide.at[j], out_ref.at[2 * j + head], sem.at[j]))
        copies[-1].start()
    for c in copies:
        c.wait()


def place(x, before=None):
    first = before is None
    anywhere, vmem = pl.BlockSpec(memory_space=pl.ANY), pl.BlockSpec(memory_space=pltpu.VMEM)
    return pl.pallas_call(
        lambda *refs: place_kernel(first, *refs),
        out_shape=jax.ShapeDtypeStruct((2 * N, ROWS, ROWS), F32),
        in_specs=[vmem] if first else [vmem, anywhere],
        out_specs=anywhere,
        scratch_shapes=[pltpu.VMEM((N, ROWS, ROWS), F32), pltpu.SemaphoreType.DMA((N,))],
        input_output_aliases={} if first else {1: 0},
        compiler_params=pltpu.CompilerParams(vmem_limit_bytes=8 * 2**20),
        cost_estimate=pl.CostEstimate(flops=2**18, bytes_accessed=3 * 2**19, transcendentals=0),
    )(*([x] if first else [x, before]))


def swap(x, axis, pairs):
    return lax.ppermute(x, axis, [(a, b) for a, b in pairs] + [(b, a) for a, b in pairs])


def add(a, b):
    return (a.astype(F32) + b.astype(F32)).astype(BF)


def body(query_proj, key_proj, value_proj, pair_bias, attn_output, output_grad):
    q, k, v, o, g = (
        jnp.swapaxes(x, 1, 2)
        for x in (query_proj, key_proj, value_proj, attn_output, output_grad)
    )
    grid = [(a, b) for a in range(N) for b in range(N)]

    kv = jnp.concatenate([k, v], axis=1)
    kvs = [
        lax.ppermute(kv, ("ri", "rj"), [(a * N + b, (b + t) % N * N + a) for a, b in grid])
        for t in range(N)
    ]
    bias = lax.all_to_all(pair_bias, "rj", 0, 0, tiled=True).reshape(N, 2, ROWS, ROWS)

    send, keep, dq, dkv = attention(q, g, o, kvs, bias)

    total = add(keep, swap(send, "core", [(0, 1)]))
    spread = lax.all_to_all(total, ("x", "rj"), 0, 0, tiled=True)
    total = jnp.sum(spread.reshape(N, N, 64, ROWS).astype(F32), axis=0).astype(BF)
    total = add(total, swap(total, "zh", [(0, 1), (2, 3)]))
    back = lax.psum_scatter(dkv.reshape(-1, ROWS), "ri", scatter_dimension=0, tiled=True)
    total, back = lax.optimization_barrier((total, back))
    back = lax.ppermute(back, ("ri", "rj"), [(a * N + b, b * N + a) for a, b in grid])
    total = add(total, swap(total, "zh", [(1, 2), (3, 0)]))
    mine, back = lax.optimization_barrier((lax.all_gather(total, "x", axis=0), back))
    bias_grad = place(swap(mine, "core", [(0, 1)]), place(mine))

    kv_grad = back.reshape(dkv.shape[1:])
    width = k.shape[1]
    grads = (dq, kv_grad[:, :width], kv_grad[:, width:])
    return *(jnp.swapaxes(x, 1, 2) for x in grads), bias_grad


def solution(mesh):
    split = Mesh(mesh.devices.reshape(N, N, 2, N, N), ("zh", "x", "core", "ri", "rj"))
    seq = ("zh", "x", "core")
    rows, keys, tile = P(seq, "ri", "rj"), P(seq, "rj", "ri"), P(None, "ri", "rj")
    return jax.shard_map(
        body,
        mesh=split,
        in_specs=(rows, keys, keys, tile, rows, rows),
        out_specs=(rows, keys, keys, tile),
        check_vma=False,
    )
```

```python
import jax
import jax.numpy as jnp
from jax import lax
from jax.experimental import pallas as pl
from jax.experimental.pallas import tpu as pltpu
from jax.sharding import Mesh
from jax.sharding import PartitionSpec as P

HEAD = 32
SCALE = HEAD**-0.5
N = 4
ROWS = 256
KEYS = N * ROWS
LANES = 128
SEQS = 4
CHUNK = 32
UNROLL = 4
BF = jnp.bfloat16
F32 = jnp.float32
NT = (((1,), (1,)), ((), ()))
NN = (((1,), (0,)), ((), ()))


def attention_kernel(
    qgo_ref, kv0, kv1, kv2, kv3, bias,
    bias_grad, dq_ref, dkv_ref,
    stack, wide, raw, low, inner,
):
    ri, rj = lax.axis_index("ri"), lax.axis_index("rj")
    kvs = (kv0, kv1, kv2, kv3)
    blocks = [lax.rem(ri + N - t, N) for t in range(N)]
    channel = lax.broadcasted_iota(jnp.int32, (2 * HEAD, ROWS), 0) // HEAD

    for s in range(SEQS):
        for part in range(2):
            at = slice(part * ROWS, (part + 1) * ROWS)
            one = jnp.where(channel == part, qgo_ref[s, : 2 * HEAD], 0)
            wide[s, :, at] = one
            stack[s, at, :] = one.T
        dots = qgo_ref[s, HEAD : 2 * HEAD].astype(F32) * qgo_ref[s, 2 * HEAD :].astype(F32)
        sums = jnp.sum(dots, axis=0, keepdims=True)
        inner[s] = jnp.broadcast_to(sums, (LANES, ROWS)).T

    for s in range(SEQS):
        for t in range(N):
            at = slice(t * ROWS, (t + 1) * ROWS)
            raw[s, :, at] = lax.dot_general(stack[s], kvs[t][s], NN, preferred_element_type=F32)

    @pl.loop(0, ROWS // CHUNK, unroll=UNROLL)
    def _(i):
        r0 = pl.multiple_of(i * CHUNK, CHUNK)
        at_logits = pl.ds(r0, CHUNK)
        at_grads = pl.ds(pl.multiple_of(ROWS + r0, CHUNK), CHUNK)
        pair = jnp.concatenate([bias[b, at_logits, :] for b in blocks], axis=1).astype(F32)
        total = None
        for s in range(SEQS):
            logits = raw[s, at_logits, :] * SCALE + pair
            top = jnp.max(logits, axis=1, keepdims=True)
            weights = jnp.exp(logits - top)
            weights = weights * (1.0 / jnp.sum(weights, axis=1, keepdims=True))
            dots = jnp.concatenate([inner[s, at_logits, :]] * (KEYS // LANES), axis=1)
            grad = weights * (raw[s, at_grads, :] - dots)
            low[s, at_logits, :] = grad.astype(BF)
            low[s, at_grads, :] = weights.astype(BF)
            total = grad if total is None else total + grad
        total = total.astype(BF)
        quarter = i // (64 // CHUNK)
        within = pl.ds(pl.multiple_of(lax.rem(i, 64 // CHUNK) * CHUNK, CHUNK), CHUNK)
        for t, b in enumerate(blocks):
            bias_grad[quarter * N + b, within, :] = total[:, t * ROWS : (t + 1) * ROWS]

    for s in range(SEQS):
        query_grads = None
        for t, b in enumerate(blocks):
            at = slice(t * ROWS, (t + 1) * ROWS)
            grads = lax.dot_general(wide[s], low[s, :, at], NN, preferred_element_type=F32)
            grads = jnp.where(channel == 0, grads * SCALE, grads)
            dkv_ref[lax.rem(b + N - rj, N), s] = grads.astype(BF)
            term = lax.dot_general(low[s, :ROWS, at], kvs[t][s], NT, preferred_element_type=F32)
            query_grads = term if query_grads is None else query_grads + term
        dq_ref[s] = (query_grads.T[:HEAD] * SCALE).astype(BF)


def attention(qgo, kvs, bias):
    vmem = pl.BlockSpec(memory_space=pltpu.VMEM)
    return pl.pallas_call(
        attention_kernel,
        out_shape=(
            jax.ShapeDtypeStruct((N * N, 64, ROWS), BF),
            jax.ShapeDtypeStruct((SEQS, HEAD, ROWS), BF),
            jax.ShapeDtypeStruct((N, SEQS, 2 * HEAD, ROWS), BF),
        ),
        in_specs=[vmem] * 6,
        out_specs=(vmem,) * 3,
        scratch_shapes=[
            pltpu.VMEM((SEQS, 2 * ROWS, 2 * HEAD), BF),
            pltpu.VMEM((SEQS, 2 * HEAD, 2 * ROWS), BF),
            pltpu.VMEM((SEQS, 2 * ROWS, KEYS), F32),
            pltpu.VMEM((SEQS, 2 * ROWS, KEYS), BF),
            pltpu.VMEM((SEQS, ROWS, LANES), F32),
        ],
        compiler_params=pltpu.CompilerParams(vmem_limit_bytes=32 * 2**20),
        cost_estimate=pl.CostEstimate(
            flops=5 * 2 * 2**25, bytes_accessed=6 * 2**20, transcendentals=2**20
        ),
    )(qgo, *kvs, bias)


def split_kernel(after, x_ref, *outs):
    for t, out in enumerate(outs):
        out[...] = x_ref[t]


def choose_kernel(after, *refs):
    ri, rj = lax.axis_index("ri"), lax.axis_index("rj")
    for t, out in enumerate(refs[N:]):
        wanted = lax.rem(rj + 2 * N - ri - t, N)
        for source, x_ref in enumerate(refs[:N]):

            @pl.when(wanted == source)
            def _():
                out[...] = x_ref[...]


def hand_on(kernel, after, *args):
    anywhere, vmem = pl.BlockSpec(memory_space=pl.ANY), pl.BlockSpec(memory_space=pltpu.VMEM)
    return pl.pallas_call(
        kernel,
        out_shape=[jax.ShapeDtypeStruct(args[0].shape[-3:], BF)] * N,
        in_specs=[anywhere] + [vmem] * len(args),
        out_specs=[vmem] * N,
        compiler_params=pltpu.CompilerParams(vmem_limit_bytes=8 * 2**20),
        cost_estimate=pl.CostEstimate(flops=0, bytes_accessed=2**21, transcendentals=0),
    )(after, *args)


def place_kernel(first, x_ref, *refs):
    out_ref, wide, sem = refs[-3:]
    core = lax.axis_index("core")
    head = core if first else 1 - core
    copies = []
    for j in range(N):
        for x in range(N):
            at = (x * N + j) * 64
            wide[j, x * 64 : (x + 1) * 64, :] = x_ref[at : at + 64, :].astype(F32)
        copies.append(pltpu.make_async_copy(wide.at[j], out_ref.at[2 * j + head], sem.at[j]))
        copies[-1].start()
    for c in copies:
        c.wait()


def place(x, before=None):
    first = before is None
    anywhere, vmem = pl.BlockSpec(memory_space=pl.ANY), pl.BlockSpec(memory_space=pltpu.VMEM)
    return pl.pallas_call(
        lambda *refs: place_kernel(first, *refs),
        out_shape=jax.ShapeDtypeStruct((2 * N, ROWS, ROWS), F32),
        in_specs=[vmem] if first else [vmem, anywhere],
        out_specs=anywhere,
        scratch_shapes=[pltpu.VMEM((N, ROWS, ROWS), F32), pltpu.SemaphoreType.DMA((N,))],
        input_output_aliases={} if first else {1: 0},
        compiler_params=pltpu.CompilerParams(vmem_limit_bytes=8 * 2**20),
        cost_estimate=pl.CostEstimate(flops=2**18, bytes_accessed=3 * 2**19, transcendentals=0),
    )(*([x] if first else [x, before]))


def swap(x, axis, pairs):
    return lax.ppermute(x, axis, [(a, b) for a, b in pairs] + [(b, a) for a, b in pairs])


def add(a, b):
    return (a.astype(F32) + b.astype(F32)).astype(BF)


def body(query_proj, key_proj, value_proj, pair_bias, attn_output, output_grad):
    q, k, v, o, g = (
        jnp.swapaxes(x, 1, 2)
        for x in (query_proj, key_proj, value_proj, attn_output, output_grad)
    )
    grid = [(a, b) for a in range(N) for b in range(N)]

    core = lax.axis_index("core")

    def half(x, which):
        return jnp.where(which == 0, x[:, :HEAD], x[:, HEAD:])

    def halves(which):
        return jnp.concatenate([half(x, which) for x in (k, v, q, g, o)], axis=1)

    both = jnp.concatenate([halves(core), swap(halves(1 - core), "core", [(0, 1)])])
    kv, qgo = both[:, : 2 * HEAD], both[:, 2 * HEAD :]
    kvs = [
        lax.ppermute(kv, ("ri", "rj"), [(a * N + b, (b + t) % N * N + a) for a, b in grid])
        for t in range(N)
    ]
    bias = lax.dynamic_index_in_dim(pair_bias.reshape(N, 2, ROWS, ROWS), core, 1, False)
    bias = lax.all_to_all(bias, "rj", 0, 0, tiled=True)

    total, dq, dkv = attention(qgo, kvs, bias)

    def spread_out(parts, axis):
        return [parts[0]] + [
            lax.ppermute(parts[t], axis, [(a, (a + t) % N) for a in range(N)])
            for t in range(1, N)
        ]

    spread = lax.all_to_all(total, ("x", "rj"), 0, 0, tiled=True)
    total = jnp.sum(spread.reshape(N, N, 64, ROWS).astype(F32), axis=0).astype(BF)
    other = swap(total, "zh", [(0, 1), (2, 3)])
    parts = spread_out(hand_on(split_kernel, total, dkv), "rj")
    total = add(total, other)
    other = swap(total, "zh", [(1, 2), (3, 0)])
    parts = spread_out(hand_on(choose_kernel, total, *parts), "ri")
    total = add(total, other)
    mine = lax.all_gather(total, "x", axis=0, tiled=True).reshape(-1, ROWS)

    dkv = sum(x.astype(F32) for x in parts).astype(BF)
    grads = jnp.concatenate([dkv, dq], axis=1)
    own, others = grads[: SEQS // 2], grads[SEQS // 2 :]
    theirs = swap(jnp.concatenate([mine, others.reshape(-1, ROWS)]), "core", [(0, 1)])
    bias_grad = place(theirs, place(mine))
    heads = own, theirs[mine.shape[0] :].reshape(own.shape)
    first, second = (jnp.where(core == c, *heads) for c in range(2))

    def whole(part):
        at = slice(part * HEAD, (part + 1) * HEAD)
        return jnp.swapaxes(jnp.concatenate([first[:, at], second[:, at]], axis=1), 1, 2)

    return whole(2), whole(0), whole(1), bias_grad


def solution(mesh):
    split = Mesh(mesh.devices.reshape(N, N, 2, N, N), ("zh", "x", "core", "ri", "rj"))
    seq = ("zh", "x", "core")
    rows, keys, tile = P(seq, "ri", "rj"), P(seq, "rj", "ri"), P(None, "ri", "rj")
    return jax.shard_map(
        body,
        mesh=split,
        in_specs=(rows, keys, keys, tile, rows, rows),
        out_specs=(rows, keys, keys, tile),
        check_vma=False,
    )
```

```python
import jax
import jax.numpy as jnp
from jax import lax
from jax.experimental import pallas as pl
from jax.experimental.pallas import tpu as pltpu
from jax.sharding import Mesh
from jax.sharding import PartitionSpec as P

HEAD = 32
SCALE = HEAD**-0.5
N = 4
ROWS = 256
KEYS = N * ROWS
LANES = 128
SEQS = 4
CHUNK = 32
UNROLL = 4
BF = jnp.bfloat16
F32 = jnp.float32
NT = (((1,), (1,)), ((), ()))
NN = (((1,), (0,)), ((), ()))


def pack_kernel(k_ref, v_ref, q_ref, g_ref, o_ref, bias_ref, keep, send, bias_out, sem):
    core = lax.axis_index("core")
    copies = []
    for out, which in ((send, 1 - core), (keep, core)):
        half = pl.ds(pl.multiple_of(which * HEAD, HEAD), HEAD)
        for i, x_ref in enumerate((k_ref, v_ref, q_ref, g_ref, o_ref)):
            copies.append((x_ref.at[:, half, :], out.at[:, i * HEAD : (i + 1) * HEAD, :]))
    for j in range(N):
        copies.append((bias_ref.at[2 * j + core], bias_out.at[j]))
    copies = [pltpu.make_async_copy(*c, sem.at[i]) for i, c in enumerate(copies)]
    for c in copies:
        c.start()
    for c in copies:
        c.wait()


def pack(*args):
    hbm = pl.BlockSpec(memory_space=pltpu.HBM)
    half = jax.ShapeDtypeStruct((SEQS // 2, 5 * HEAD, ROWS), BF)
    return pl.pallas_call(
        pack_kernel,
        out_shape=(half, half, jax.ShapeDtypeStruct((N, ROWS, ROWS), BF)),
        in_specs=[hbm] * 6,
        out_specs=(hbm,) * 3,
        scratch_shapes=[pltpu.SemaphoreType.DMA((10 + N,))],
        compiler_params=pltpu.CompilerParams(vmem_limit_bytes=56 * 2**20),
        cost_estimate=pl.CostEstimate(flops=0, bytes_accessed=2**21, transcendentals=0),
    )(*args)


def attention_kernel(
    qgo_ref, kv0, kv1, kv2, kv3, bias,
    bias_grad, dq_ref, dkv_ref,
    stack, wide, raw, low, inner,
):
    ri, rj = lax.axis_index("ri"), lax.axis_index("rj")
    kvs = (kv0, kv1, kv2, kv3)
    blocks = [lax.rem(ri + N - t, N) for t in range(N)]
    channel = lax.broadcasted_iota(jnp.int32, (2 * HEAD, ROWS), 0) // HEAD

    for s in range(SEQS):
        for part in range(2):
            at = slice(part * ROWS, (part + 1) * ROWS)
            one = jnp.where(channel == part, qgo_ref[s, : 2 * HEAD], 0)
            wide[s, :, at] = one
            stack[s, at, :] = one.T
        dots = qgo_ref[s, HEAD : 2 * HEAD].astype(F32) * qgo_ref[s, 2 * HEAD :].astype(F32)
        sums = jnp.sum(dots, axis=0, keepdims=True)
        inner[s] = jnp.broadcast_to(sums, (LANES, ROWS)).T

    for s in range(SEQS):
        for t in range(N):
            at = slice(t * ROWS, (t + 1) * ROWS)
            raw[s, :, at] = lax.dot_general(stack[s], kvs[t][s], NN, preferred_element_type=F32)

    @pl.loop(0, ROWS // CHUNK, unroll=UNROLL)
    def _(i):
        r0 = pl.multiple_of(i * CHUNK, CHUNK)
        at_logits = pl.ds(r0, CHUNK)
        at_grads = pl.ds(pl.multiple_of(ROWS + r0, CHUNK), CHUNK)
        pair = jnp.concatenate([bias[b, at_logits, :] for b in blocks], axis=1).astype(F32)
        total = None
        for s in range(SEQS):
            logits = raw[s, at_logits, :] * SCALE + pair
            top = jnp.max(logits, axis=1, keepdims=True)
            weights = jnp.exp(logits - top)
            weights = weights * (1.0 / jnp.sum(weights, axis=1, keepdims=True))
            dots = jnp.concatenate([inner[s, at_logits, :]] * (KEYS // LANES), axis=1)
            grad = weights * (raw[s, at_grads, :] - dots)
            low[s, at_logits, :] = grad.astype(BF)
            low[s, at_grads, :] = weights.astype(BF)
            total = grad if total is None else total + grad
        total = total.astype(BF)
        quarter = i // (64 // CHUNK)
        within = pl.ds(pl.multiple_of(lax.rem(i, 64 // CHUNK) * CHUNK, CHUNK), CHUNK)
        for t, b in enumerate(blocks):
            bias_grad[quarter * N + b, within, :] = total[:, t * ROWS : (t + 1) * ROWS]

    for s in range(SEQS):
        query_grads = None
        for t, b in enumerate(blocks):
            at = slice(t * ROWS, (t + 1) * ROWS)
            grads = lax.dot_general(wide[s], low[s, :, at], NN, preferred_element_type=F32)
            grads = jnp.where(channel == 0, grads * SCALE, grads)
            dkv_ref[lax.rem(b + N - rj, N), s] = grads.astype(BF)
            term = lax.dot_general(low[s, :ROWS, at], kvs[t][s], NT, preferred_element_type=F32)
            query_grads = term if query_grads is None else query_grads + term
        dq_ref[s] = (query_grads.T[:HEAD] * SCALE).astype(BF)


def attention(qgo, kvs, bias):
    vmem = pl.BlockSpec(memory_space=pltpu.VMEM)
    return pl.pallas_call(
        attention_kernel,
        out_shape=(
            jax.ShapeDtypeStruct((N * N, 64, ROWS), BF),
            jax.ShapeDtypeStruct((SEQS, HEAD, ROWS), BF),
            jax.ShapeDtypeStruct((N, SEQS, 2 * HEAD, ROWS), BF),
        ),
        in_specs=[vmem] * 6,
        out_specs=(vmem,) * 3,
        scratch_shapes=[
            pltpu.VMEM((SEQS, 2 * ROWS, 2 * HEAD), BF),
            pltpu.VMEM((SEQS, 2 * HEAD, 2 * ROWS), BF),
            pltpu.VMEM((SEQS, 2 * ROWS, KEYS), F32),
            pltpu.VMEM((SEQS, 2 * ROWS, KEYS), BF),
            pltpu.VMEM((SEQS, ROWS, LANES), F32),
        ],
        compiler_params=pltpu.CompilerParams(vmem_limit_bytes=32 * 2**20),
        cost_estimate=pl.CostEstimate(
            flops=5 * 2 * 2**25, bytes_accessed=6 * 2**20, transcendentals=2**20
        ),
    )(qgo, *kvs, bias)


def split_kernel(after, x_ref, *outs):
    for t, out in enumerate(outs):
        out[...] = x_ref[t]


def choose_kernel(after, *refs):
    ri, rj = lax.axis_index("ri"), lax.axis_index("rj")
    for t, out in enumerate(refs[N:]):
        wanted = lax.rem(rj + 2 * N - ri - t, N)
        for source, x_ref in enumerate(refs[:N]):

            @pl.when(wanted == source)
            def _():
                out[...] = x_ref[...]


def hand_on(kernel, after, *args):
    anywhere, vmem = pl.BlockSpec(memory_space=pl.ANY), pl.BlockSpec(memory_space=pltpu.VMEM)
    return pl.pallas_call(
        kernel,
        out_shape=[jax.ShapeDtypeStruct(args[0].shape[-3:], BF)] * N,
        in_specs=[anywhere] + [vmem] * len(args),
        out_specs=[vmem] * N,
        compiler_params=pltpu.CompilerParams(vmem_limit_bytes=8 * 2**20),
        cost_estimate=pl.CostEstimate(flops=0, bytes_accessed=2**21, transcendentals=0),
    )(after, *args)


def place_heads(x_ref, out_ref, wide, sem, head):
    copies = []
    for j in range(N):
        for x in range(N):
            at = (x * N + j) * 64
            wide[j, x * 64 : (x + 1) * 64, :] = x_ref[at : at + 64, :].astype(F32)
        copies.append(pltpu.make_async_copy(wide.at[j], out_ref.at[2 * j + head], sem.at[j]))
        copies[-1].start()
    return copies


def place_kernel(x_ref, out_ref, wide, sem):
    for c in place_heads(x_ref, out_ref, wide, sem, lax.axis_index("core")):
        c.wait()


def finish_kernel(x_ref, own_ref, before, out_ref, dk_ref, dv_ref, dq_ref, wide, both, sem):
    core = lax.axis_index("core")
    copies = place_heads(x_ref, out_ref, wide, sem, 1 - core)
    mine = pl.ds(pl.multiple_of(core * HEAD, HEAD), HEAD)
    theirs = pl.ds(pl.multiple_of((1 - core) * HEAD, HEAD), HEAD)
    for i, grad_ref in enumerate((dk_ref, dv_ref, dq_ref)):
        for s in range(SEQS // 2):
            at = N * ROWS + (s * 3 + i) * HEAD
            both[i, s, mine, :] = own_ref[s, i * HEAD : (i + 1) * HEAD, :]
            both[i, s, theirs, :] = x_ref[at : at + HEAD, :]
        copies.append(pltpu.make_async_copy(both.at[i], grad_ref, sem.at[N + i]))
        copies[-1].start()
    for c in copies:
        c.wait()


def place(x):
    anywhere, vmem = pl.BlockSpec(memory_space=pl.ANY), pl.BlockSpec(memory_space=pltpu.VMEM)
    return pl.pallas_call(
        place_kernel,
        out_shape=jax.ShapeDtypeStruct((2 * N, ROWS, ROWS), F32),
        in_specs=[vmem],
        out_specs=anywhere,
        scratch_shapes=[pltpu.VMEM((N, ROWS, ROWS), F32), pltpu.SemaphoreType.DMA((N,))],
        compiler_params=pltpu.CompilerParams(vmem_limit_bytes=8 * 2**20),
        cost_estimate=pl.CostEstimate(flops=2**18, bytes_accessed=3 * 2**19, transcendentals=0),
    )(x)


def finish(x, own, before):
    anywhere, vmem = pl.BlockSpec(memory_space=pl.ANY), pl.BlockSpec(memory_space=pltpu.VMEM)
    grad = jax.ShapeDtypeStruct((SEQS // 2, 2 * HEAD, ROWS), BF)
    return pl.pallas_call(
        finish_kernel,
        out_shape=(jax.ShapeDtypeStruct(before.shape, F32), grad, grad, grad),
        in_specs=[vmem, vmem, anywhere],
        out_specs=(anywhere,) * 4,
        scratch_shapes=[
            pltpu.VMEM((N, ROWS, ROWS), F32),
            pltpu.VMEM((3, *grad.shape), BF),
            pltpu.SemaphoreType.DMA((N + 3,)),
        ],
        input_output_aliases={2: 0},
        compiler_params=pltpu.CompilerParams(vmem_limit_bytes=8 * 2**20),
        cost_estimate=pl.CostEstimate(flops=2**18, bytes_accessed=2**21, transcendentals=0),
    )(x, own, before)


def swap(x, axis, pairs):
    return lax.ppermute(x, axis, [(a, b) for a, b in pairs] + [(b, a) for a, b in pairs])


def add(a, b):
    return (a.astype(F32) + b.astype(F32)).astype(BF)


def body(query_proj, key_proj, value_proj, pair_bias, attn_output, output_grad):
    q, k, v, o, g = (
        jnp.swapaxes(x, 1, 2)
        for x in (query_proj, key_proj, value_proj, attn_output, output_grad)
    )
    grid = [(a, b) for a in range(N) for b in range(N)]

    keep, send, bias = pack(k, v, q, g, o, pair_bias)
    both = jnp.concatenate([keep, swap(send, "core", [(0, 1)])])
    kv, qgo = both[:, : 2 * HEAD], both[:, 2 * HEAD :]
    kvs = [
        lax.ppermute(kv, ("ri", "rj"), [(a * N + b, (b + t) % N * N + a) for a, b in grid])
        for t in range(N)
    ]
    bias = lax.all_to_all(bias, "rj", 0, 0, tiled=True)

    total, dq, dkv = attention(qgo, kvs, bias)

    def spread_out(parts, axis):
        return [parts[0]] + [
            lax.ppermute(parts[t], axis, [(a, (a + t) % N) for a in range(N)])
            for t in range(1, N)
        ]

    spread = lax.all_to_all(total, ("x", "rj"), 0, 0, tiled=True)
    total = jnp.sum(spread.reshape(N, N, 64, ROWS).astype(F32), axis=0).astype(BF)
    other = swap(total, "zh", [(0, 1), (2, 3)])
    parts = spread_out(hand_on(split_kernel, total, dkv), "rj")
    total = add(total, other)
    other = swap(total, "zh", [(1, 2), (3, 0)])
    parts = spread_out(hand_on(choose_kernel, total, *parts), "ri")
    total = add(total, other)
    mine = lax.all_gather(total, "x", axis=0, tiled=True).reshape(-1, ROWS)

    dkv = sum(x.astype(F32) for x in parts).astype(BF)
    grads = jnp.concatenate([dkv, dq], axis=1)
    own, others = grads[: SEQS // 2], grads[SEQS // 2 :]
    theirs = swap(jnp.concatenate([mine, others.reshape(-1, ROWS)]), "core", [(0, 1)])
    bias_grad, dk, dv, dq = finish(theirs, own, place(mine))
    return *(jnp.swapaxes(x, 1, 2) for x in (dq, dk, dv)), bias_grad


def solution(mesh):
    split = Mesh(mesh.devices.reshape(N, N, 2, N, N), ("zh", "x", "core", "ri", "rj"))
    seq = ("zh", "x", "core")
    rows, keys, tile = P(seq, "ri", "rj"), P(seq, "rj", "ri"), P(None, "ri", "rj")
    return jax.shard_map(
        body,
        mesh=split,
        in_specs=(rows, keys, keys, tile, rows, rows),
        out_specs=(rows, keys, keys, tile),
        check_vma=False,
    )
```

```python
import jax
import jax.numpy as jnp
from jax import lax
from jax.experimental import pallas as pl
from jax.experimental.pallas import tpu as pltpu
from jax.sharding import Mesh
from jax.sharding import PartitionSpec as P

HEAD = 32
SCALE = HEAD**-0.5
N = 4
ROWS = 256
KEYS = N * ROWS
LANES = 128
SEQS = 4
CHUNK = 32
UNROLL = 4
BF = jnp.bfloat16
F32 = jnp.float32
NT = (((1,), (1,)), ((), ()))
NN = (((1,), (0,)), ((), ()))


def pack_kernel(*refs):
    inputs, bias_ref = refs[:5], refs[5]
    keep, send, bias_out, held, bias_held, sem = refs[6:]
    core = lax.axis_index("core")
    inward = [
        pltpu.make_async_copy(x_ref, held.at[i], sem.at[i]) for i, x_ref in enumerate(inputs)
    ]
    for j in range(N):
        src = bias_ref.at[2 * j + core]
        inward.append(pltpu.make_async_copy(src, bias_held.at[j], sem.at[5 + j]))
    for c in inward:
        c.start()
    outward = []
    for i in range(5):
        inward[i].wait()
        to = slice(i * HEAD, (i + 1) * HEAD)
        for out, which in ((send, 1 - core), (keep, core)):
            half = pl.ds(pl.multiple_of(which * HEAD, HEAD), HEAD)
            here = sem.at[5 + N + len(outward)]
            outward.append(pltpu.make_async_copy(held.at[i, :, half, :], out.at[:, to, :], here))
            outward[-1].start()
    for j in range(N):
        inward[5 + j].wait()
        here = sem.at[5 + N + len(outward)]
        outward.append(pltpu.make_async_copy(bias_held.at[j], bias_out.at[j], here))
        outward[-1].start()
    for c in outward:
        c.wait()


def pack(*args):
    hbm = pl.BlockSpec(memory_space=pltpu.HBM)
    half = jax.ShapeDtypeStruct((SEQS // 2, 5 * HEAD, ROWS), BF)
    return pl.pallas_call(
        pack_kernel,
        out_shape=(half, half, jax.ShapeDtypeStruct((N, ROWS, ROWS), BF)),
        in_specs=[hbm] * 6,
        out_specs=(hbm,) * 3,
        scratch_shapes=[
            pltpu.VMEM((5, *args[0].shape), BF),
            pltpu.VMEM((N, ROWS, ROWS), BF),
            pltpu.SemaphoreType.DMA((15 + 2 * N,)),
        ],
        compiler_params=pltpu.CompilerParams(vmem_limit_bytes=56 * 2**20),
        cost_estimate=pl.CostEstimate(flops=0, bytes_accessed=2**21, transcendentals=0),
    )(*args)


def attention_kernel(
    qgo_ref, kv0, kv1, kv2, kv3, bias,
    bias_grad, dq_ref, dkv_ref,
    stack, wide, raw, low, inner,
):
    ri, rj = lax.axis_index("ri"), lax.axis_index("rj")
    kvs = (kv0, kv1, kv2, kv3)
    blocks = [lax.rem(ri + 2 * N - rj - t, N) for t in range(N)]
    channel = lax.broadcasted_iota(jnp.int32, (2 * HEAD, ROWS), 0) // HEAD

    for s in range(SEQS):
        for part in range(2):
            at = slice(part * ROWS, (part + 1) * ROWS)
            one = jnp.where(channel == part, qgo_ref[s, : 2 * HEAD], 0)
            wide[s, :, at] = one
            stack[s, at, :] = one.T
        dots = qgo_ref[s, HEAD : 2 * HEAD].astype(F32) * qgo_ref[s, 2 * HEAD :].astype(F32)
        sums = jnp.sum(dots, axis=0, keepdims=True)
        inner[s] = jnp.broadcast_to(sums, (LANES, ROWS)).T

    for s in range(SEQS):
        for t in range(N):
            at = slice(t * ROWS, (t + 1) * ROWS)
            raw[s, :, at] = lax.dot_general(stack[s], kvs[t][s], NN, preferred_element_type=F32)

    @pl.loop(0, ROWS // CHUNK, unroll=UNROLL)
    def _(i):
        r0 = pl.multiple_of(i * CHUNK, CHUNK)
        at_logits = pl.ds(r0, CHUNK)
        at_grads = pl.ds(pl.multiple_of(ROWS + r0, CHUNK), CHUNK)
        pair = jnp.concatenate([bias[b, at_logits, :] for b in blocks], axis=1).astype(F32)
        total = None
        for s in range(SEQS):
            logits = raw[s, at_logits, :] * SCALE + pair
            top = jnp.max(logits, axis=1, keepdims=True)
            weights = jnp.exp(logits - top)
            weights = weights * (1.0 / jnp.sum(weights, axis=1, keepdims=True))
            dots = jnp.concatenate([inner[s, at_logits, :]] * (KEYS // LANES), axis=1)
            grad = weights * (raw[s, at_grads, :] - dots)
            low[s, at_logits, :] = grad.astype(BF)
            low[s, at_grads, :] = weights.astype(BF)
            total = grad if total is None else total + grad
        total = total.astype(BF)
        quarter = i // (64 // CHUNK)
        within = pl.ds(pl.multiple_of(lax.rem(i, 64 // CHUNK) * CHUNK, CHUNK), CHUNK)
        for t, b in enumerate(blocks):
            bias_grad[quarter * N + b, within, :] = total[:, t * ROWS : (t + 1) * ROWS]

    for s in range(SEQS):
        query_grads = None
        for t, b in enumerate(blocks):
            at = slice(t * ROWS, (t + 1) * ROWS)
            grads = lax.dot_general(wide[s], low[s, :, at], NN, preferred_element_type=F32)
            grads = jnp.where(channel == 0, grads * SCALE, grads)
            dkv_ref[lax.rem(b + N - rj, N), s] = grads.astype(BF)
            term = lax.dot_general(low[s, :ROWS, at], kvs[t][s], NT, preferred_element_type=F32)
            query_grads = term if query_grads is None else query_grads + term
        dq_ref[s] = (query_grads.T[:HEAD] * SCALE).astype(BF)


def attention(qgo, kvs, bias):
    vmem = pl.BlockSpec(memory_space=pltpu.VMEM)
    return pl.pallas_call(
        attention_kernel,
        out_shape=(
            jax.ShapeDtypeStruct((N * N, 64, ROWS), BF),
            jax.ShapeDtypeStruct((SEQS, HEAD, ROWS), BF),
            jax.ShapeDtypeStruct((N, SEQS, 2 * HEAD, ROWS), BF),
        ),
        in_specs=[vmem] * 6,
        out_specs=(vmem,) * 3,
        scratch_shapes=[
            pltpu.VMEM((SEQS, 2 * ROWS, 2 * HEAD), BF),
            pltpu.VMEM((SEQS, 2 * HEAD, 2 * ROWS), BF),
            pltpu.VMEM((SEQS, 2 * ROWS, KEYS), F32),
            pltpu.VMEM((SEQS, 2 * ROWS, KEYS), BF),
            pltpu.VMEM((SEQS, ROWS, LANES), F32),
        ],
        compiler_params=pltpu.CompilerParams(vmem_limit_bytes=32 * 2**20),
        cost_estimate=pl.CostEstimate(
            flops=5 * 2 * 2**25, bytes_accessed=6 * 2**20, transcendentals=2**20
        ),
    )(qgo, *kvs, bias)


def split_kernel(after, x_ref, *outs):
    for t, out in enumerate(outs):
        out[...] = x_ref[t]


def choose_kernel(after, *refs):
    ri, rj = lax.axis_index("ri"), lax.axis_index("rj")
    for t, out in enumerate(refs[N:]):
        wanted = lax.rem(rj + 2 * N - ri - t, N)
        for source, x_ref in enumerate(refs[:N]):

            @pl.when(wanted == source)
            def _():
                out[...] = x_ref[...]


def hand_on(kernel, after, *args):
    anywhere, vmem = pl.BlockSpec(memory_space=pl.ANY), pl.BlockSpec(memory_space=pltpu.VMEM)
    return pl.pallas_call(
        kernel,
        out_shape=[jax.ShapeDtypeStruct(args[0].shape[-3:], BF)] * N,
        in_specs=[anywhere] + [vmem] * len(args),
        out_specs=[vmem] * N,
        compiler_params=pltpu.CompilerParams(vmem_limit_bytes=8 * 2**20),
        cost_estimate=pl.CostEstimate(flops=0, bytes_accessed=2**21, transcendentals=0),
    )(after, *args)


def place_heads(x_ref, out_ref, wide, sem, head):
    copies = []
    for j in range(N):
        for x in range(N):
            at = (x * N + j) * 64
            wide[j, x * 64 : (x + 1) * 64, :] = x_ref[at : at + 64, :].astype(F32)
        copies.append(pltpu.make_async_copy(wide.at[j], out_ref.at[2 * j + head], sem.at[j]))
        copies[-1].start()
    return copies


def place_kernel(x_ref, out_ref, wide, sem):
    for c in place_heads(x_ref, out_ref, wide, sem, lax.axis_index("core")):
        c.wait()


def finish_kernel(x_ref, own_ref, before, out_ref, dk_ref, dv_ref, dq_ref, wide, both, sem):
    core = lax.axis_index("core")
    copies = place_heads(x_ref, out_ref, wide, sem, 1 - core)
    mine = pl.ds(pl.multiple_of(core * HEAD, HEAD), HEAD)
    theirs = pl.ds(pl.multiple_of((1 - core) * HEAD, HEAD), HEAD)
    for i, grad_ref in enumerate((dk_ref, dv_ref, dq_ref)):
        for s in range(SEQS // 2):
            at = N * ROWS + (s * 3 + i) * HEAD
            both[i, s, mine, :] = own_ref[s, i * HEAD : (i + 1) * HEAD, :]
            both[i, s, theirs, :] = x_ref[at : at + HEAD, :]
        copies.append(pltpu.make_async_copy(both.at[i], grad_ref, sem.at[N + i]))
        copies[-1].start()
    for c in copies:
        c.wait()


def place(x):
    anywhere, vmem = pl.BlockSpec(memory_space=pl.ANY), pl.BlockSpec(memory_space=pltpu.VMEM)
    return pl.pallas_call(
        place_kernel,
        out_shape=jax.ShapeDtypeStruct((2 * N, ROWS, ROWS), F32),
        in_specs=[vmem],
        out_specs=anywhere,
        scratch_shapes=[pltpu.VMEM((N, ROWS, ROWS), F32), pltpu.SemaphoreType.DMA((N,))],
        compiler_params=pltpu.CompilerParams(vmem_limit_bytes=8 * 2**20),
        cost_estimate=pl.CostEstimate(flops=2**18, bytes_accessed=3 * 2**19, transcendentals=0),
    )(x)


def finish(x, own, before):
    anywhere, vmem = pl.BlockSpec(memory_space=pl.ANY), pl.BlockSpec(memory_space=pltpu.VMEM)
    grad = jax.ShapeDtypeStruct((SEQS // 2, 2 * HEAD, ROWS), BF)
    return pl.pallas_call(
        finish_kernel,
        out_shape=(jax.ShapeDtypeStruct(before.shape, F32), grad, grad, grad),
        in_specs=[vmem, vmem, anywhere],
        out_specs=(anywhere,) * 4,
        scratch_shapes=[
            pltpu.VMEM((N, ROWS, ROWS), F32),
            pltpu.VMEM((3, *grad.shape), BF),
            pltpu.SemaphoreType.DMA((N + 3,)),
        ],
        input_output_aliases={2: 0},
        compiler_params=pltpu.CompilerParams(vmem_limit_bytes=8 * 2**20),
        cost_estimate=pl.CostEstimate(flops=2**18, bytes_accessed=2**21, transcendentals=0),
    )(x, own, before)


def swap(x, axis, pairs):
    return lax.ppermute(x, axis, [(a, b) for a, b in pairs] + [(b, a) for a, b in pairs])


def add(a, b):
    return (a.astype(F32) + b.astype(F32)).astype(BF)


def body(query_proj, key_proj, value_proj, pair_bias, attn_output, output_grad):
    q, k, v, o, g = (
        jnp.swapaxes(x, 1, 2)
        for x in (query_proj, key_proj, value_proj, attn_output, output_grad)
    )
    grid = [(a, b) for a in range(N) for b in range(N)]

    keep, send, bias = pack(k, v, q, g, o, pair_bias)
    both = jnp.concatenate([keep, swap(send, "core", [(0, 1)])])
    kv, qgo = both[:, : 2 * HEAD], both[:, 2 * HEAD :]
    kvs = [
        lax.ppermute(kv, ("ri", "rj"), [(a * N + b, (a + b + t) % N * N + a) for a, b in grid])
        for t in range(N)
    ]
    bias = lax.all_to_all(bias, "rj", 0, 0, tiled=True)

    total, dq, dkv = attention(qgo, kvs, bias)

    def spread_out(parts, axis):
        return [parts[0]] + [
            lax.ppermute(parts[t], axis, [(a, (a + t) % N) for a in range(N)])
            for t in range(1, N)
        ]

    spread = lax.all_to_all(total, ("x", "rj"), 0, 0, tiled=True)
    total = jnp.sum(spread.reshape(N, N, 64, ROWS).astype(F32), axis=0).astype(BF)
    other = swap(total, "zh", [(0, 1), (2, 3)])
    parts = spread_out(hand_on(split_kernel, total, dkv), "rj")
    total = add(total, other)
    other = swap(total, "zh", [(1, 2), (3, 0)])
    parts = spread_out(hand_on(choose_kernel, total, *parts), "ri")
    total = add(total, other)
    mine = lax.all_gather(total, "x", axis=0, tiled=True).reshape(-1, ROWS)

    dkv = sum(x.astype(F32) for x in parts).astype(BF)
    grads = jnp.concatenate([dkv, dq], axis=1)
    own, others = grads[: SEQS // 2], grads[SEQS // 2 :]
    theirs = swap(jnp.concatenate([mine, others.reshape(-1, ROWS)]), "core", [(0, 1)])
    bias_grad, dk, dv, dq = finish(theirs, own, place(mine))
    return *(jnp.swapaxes(x, 1, 2) for x in (dq, dk, dv)), bias_grad


def solution(mesh):
    split = Mesh(mesh.devices.reshape(N, N, 2, N, N), ("zh", "x", "core", "ri", "rj"))
    seq = ("zh", "x", "core")
    rows, keys, tile = P(seq, "ri", "rj"), P(seq, "rj", "ri"), P(None, "ri", "rj")
    return jax.shard_map(
        body,
        mesh=split,
        in_specs=(rows, keys, keys, tile, rows, rows),
        out_specs=(rows, keys, keys, tile),
        check_vma=False,
    )
```

```python
import jax
import jax.numpy as jnp
from jax import lax
from jax.experimental import pallas as pl
from jax.experimental.pallas import tpu as pltpu
from jax.sharding import Mesh
from jax.sharding import PartitionSpec as P

HEAD = 32
SCALE = HEAD**-0.5
N = 4
ROWS = 256
KEYS = N * ROWS
LANES = 128
SEQS = 4
CHUNK = 32
UNROLL = 4
BF = jnp.bfloat16
F32 = jnp.float32
NT = (((1,), (1,)), ((), ()))
NN = (((1,), (0,)), ((), ()))


def pack_kernel(*refs):
    inputs, bias_ref = refs[:5], refs[5]
    keep, send, bias_out, held, bias_held, sem = refs[6:]
    core = lax.axis_index("core")
    inward = [
        pltpu.make_async_copy(x_ref, held.at[i], sem.at[i]) for i, x_ref in enumerate(inputs)
    ]
    for j in range(N):
        src = bias_ref.at[2 * j + core]
        inward.append(pltpu.make_async_copy(src, bias_held.at[j], sem.at[5 + j]))
    for c in inward:
        c.start()
    outward = []
    for i in range(5):
        inward[i].wait()
        to = slice(i * HEAD, (i + 1) * HEAD)
        for out, which in ((send, 1 - core), (keep, core)):
            half = pl.ds(pl.multiple_of(which * HEAD, HEAD), HEAD)
            here = sem.at[5 + N + len(outward)]
            outward.append(pltpu.make_async_copy(held.at[i, :, half, :], out.at[:, to, :], here))
            outward[-1].start()
    for j in range(N):
        inward[5 + j].wait()
        here = sem.at[5 + N + len(outward)]
        outward.append(pltpu.make_async_copy(bias_held.at[j], bias_out.at[j], here))
        outward[-1].start()
    for c in outward:
        c.wait()


def pack(*args):
    hbm = pl.BlockSpec(memory_space=pltpu.HBM)
    half = jax.ShapeDtypeStruct((SEQS // 2, 5 * HEAD, ROWS), BF)
    return pl.pallas_call(
        pack_kernel,
        out_shape=(half, half, jax.ShapeDtypeStruct((N, ROWS, ROWS), BF)),
        in_specs=[hbm] * 6,
        out_specs=(hbm,) * 3,
        scratch_shapes=[
            pltpu.VMEM((5, *args[0].shape), BF),
            pltpu.VMEM((N, ROWS, ROWS), BF),
            pltpu.SemaphoreType.DMA((15 + 2 * N,)),
        ],
        compiler_params=pltpu.CompilerParams(vmem_limit_bytes=56 * 2**20),
        cost_estimate=pl.CostEstimate(flops=0, bytes_accessed=2**21, transcendentals=0),
    )(*args)


def attention_kernel(
    qgo_ref, kv0, kv1, kv2, kv3, bias,
    bias_grad, dq_ref, dkv0, dkv1, dkv2, dkv3,
    stack, wide, raw, low, inner,
):
    ri, rj = lax.axis_index("ri"), lax.axis_index("rj")
    kvs, dkv_refs = (kv0, kv1, kv2, kv3), (dkv0, dkv1, dkv2, dkv3)
    blocks = [lax.rem(ri + 2 * N - rj - t, N) for t in range(N)]
    channel = lax.broadcasted_iota(jnp.int32, (2 * HEAD, ROWS), 0) // HEAD

    for s in range(SEQS):
        for part in range(2):
            at = slice(part * ROWS, (part + 1) * ROWS)
            one = jnp.where(channel == part, qgo_ref[s, : 2 * HEAD], 0)
            wide[s, :, at] = one
            stack[s, at, :] = one.T
        dots = qgo_ref[s, HEAD : 2 * HEAD].astype(F32) * qgo_ref[s, 2 * HEAD :].astype(F32)
        sums = jnp.sum(dots, axis=0, keepdims=True)
        inner[s] = jnp.broadcast_to(sums, (LANES, ROWS)).T

    for s in range(SEQS):
        for t in range(N):
            at = slice(t * ROWS, (t + 1) * ROWS)
            raw[s, :, at] = lax.dot_general(stack[s], kvs[t][s], NN, preferred_element_type=F32)

    @pl.loop(0, ROWS // CHUNK, unroll=UNROLL)
    def _(i):
        r0 = pl.multiple_of(i * CHUNK, CHUNK)
        at_logits = pl.ds(r0, CHUNK)
        at_grads = pl.ds(pl.multiple_of(ROWS + r0, CHUNK), CHUNK)
        pair = jnp.concatenate([bias[b, at_logits, :] for b in blocks], axis=1).astype(F32)
        total = None
        for s in range(SEQS):
            logits = raw[s, at_logits, :] * SCALE + pair
            top = jnp.max(logits, axis=1, keepdims=True)
            weights = jnp.exp(logits - top)
            weights = weights * (1.0 / jnp.sum(weights, axis=1, keepdims=True))
            dots = jnp.concatenate([inner[s, at_logits, :]] * (KEYS // LANES), axis=1)
            grad = weights * (raw[s, at_grads, :] - dots)
            low[s, at_logits, :] = grad.astype(BF)
            low[s, at_grads, :] = weights.astype(BF)
            total = grad if total is None else total + grad
        total = total.astype(BF)
        quarter = i // (64 // CHUNK)
        within = pl.ds(pl.multiple_of(lax.rem(i, 64 // CHUNK) * CHUNK, CHUNK), CHUNK)
        for t, b in enumerate(blocks):
            bias_grad[quarter * N + b, within, :] = total[:, t * ROWS : (t + 1) * ROWS]

    for s in range(SEQS):
        query_grads = None
        for t in range(N):
            at = slice(t * ROWS, (t + 1) * ROWS)
            term = lax.dot_general(low[s, :ROWS, at], kvs[t][s], NT, preferred_element_type=F32)
            query_grads = term if query_grads is None else query_grads + term
        dq_ref[s] = (query_grads.T[:HEAD] * SCALE).astype(BF)
        for u, dkv_ref in enumerate(dkv_refs):
            t = lax.rem(ri + 3 * N - 2 * rj - u, N)
            at = pl.ds(pl.multiple_of(t * ROWS, ROWS), ROWS)
            grads = lax.dot_general(wide[s], low[s, :, at], NN, preferred_element_type=F32)
            dkv_ref[s] = jnp.where(channel == 0, grads * SCALE, grads).astype(BF)


def attention(qgo, kvs, bias):
    vmem = pl.BlockSpec(memory_space=pltpu.VMEM)
    return pl.pallas_call(
        attention_kernel,
        out_shape=(
            jax.ShapeDtypeStruct((N * N, 64, ROWS), BF),
            jax.ShapeDtypeStruct((SEQS, HEAD, ROWS), BF),
            *[jax.ShapeDtypeStruct((SEQS, 2 * HEAD, ROWS), BF)] * N,
        ),
        in_specs=[vmem] * 6,
        out_specs=(vmem,) * (N + 2),
        scratch_shapes=[
            pltpu.VMEM((SEQS, 2 * ROWS, 2 * HEAD), BF),
            pltpu.VMEM((SEQS, 2 * HEAD, 2 * ROWS), BF),
            pltpu.VMEM((SEQS, 2 * ROWS, KEYS), F32),
            pltpu.VMEM((SEQS, 2 * ROWS, KEYS), BF),
            pltpu.VMEM((SEQS, ROWS, LANES), F32),
        ],
        compiler_params=pltpu.CompilerParams(vmem_limit_bytes=32 * 2**20),
        cost_estimate=pl.CostEstimate(
            flops=5 * 2 * 2**25, bytes_accessed=6 * 2**20, transcendentals=2**20
        ),
    )(qgo, *kvs, bias)


def copy_kernel(after, *refs):
    for x_ref, out in zip(refs[: len(refs) // 2], refs[len(refs) // 2 :]):
        out[...] = x_ref[...]


def choose_kernel(after, *refs):
    ri, rj = lax.axis_index("ri"), lax.axis_index("rj")
    for t, out in enumerate(refs[N:]):
        wanted = lax.rem(rj + 2 * N - ri - t, N)
        for source, x_ref in enumerate(refs[:N]):

            @pl.when(wanted == source)
            def _():
                out[...] = x_ref[...]


def hand_on(kernel, after, *args):
    anywhere, vmem = pl.BlockSpec(memory_space=pl.ANY), pl.BlockSpec(memory_space=pltpu.VMEM)
    return pl.pallas_call(
        kernel,
        out_shape=[jax.ShapeDtypeStruct(x.shape, BF) for x in args],
        in_specs=[anywhere] + [vmem] * len(args),
        out_specs=[vmem] * len(args),
        compiler_params=pltpu.CompilerParams(vmem_limit_bytes=8 * 2**20),
        cost_estimate=pl.CostEstimate(flops=0, bytes_accessed=2**21, transcendentals=0),
    )(after, *args)


def place_heads(x_ref, out_ref, wide, sem, head):
    copies = []
    for j in range(N):
        for x in range(N):
            at = (x * N + j) * 64
            wide[j, x * 64 : (x + 1) * 64, :] = x_ref[at : at + 64, :].astype(F32)
        copies.append(pltpu.make_async_copy(wide.at[j], out_ref.at[2 * j + head], sem.at[j]))
        copies[-1].start()
    return copies


def place_kernel(x_ref, out_ref, wide, sem):
    for c in place_heads(x_ref, out_ref, wide, sem, lax.axis_index("core")):
        c.wait()


def finish_kernel(x_ref, own_ref, before, out_ref, dk_ref, dv_ref, dq_ref, wide, both, sem):
    core = lax.axis_index("core")
    copies = place_heads(x_ref, out_ref, wide, sem, 1 - core)
    mine = pl.ds(pl.multiple_of(core * HEAD, HEAD), HEAD)
    theirs = pl.ds(pl.multiple_of((1 - core) * HEAD, HEAD), HEAD)
    for i, grad_ref in enumerate((dk_ref, dv_ref, dq_ref)):
        for s in range(SEQS // 2):
            at = N * ROWS + (s * 3 + i) * HEAD
            both[i, s, mine, :] = own_ref[s, i * HEAD : (i + 1) * HEAD, :]
            both[i, s, theirs, :] = x_ref[at : at + HEAD, :]
        copies.append(pltpu.make_async_copy(both.at[i], grad_ref, sem.at[N + i]))
        copies[-1].start()
    for c in copies:
        c.wait()


def place(x):
    anywhere, vmem = pl.BlockSpec(memory_space=pl.ANY), pl.BlockSpec(memory_space=pltpu.VMEM)
    return pl.pallas_call(
        place_kernel,
        out_shape=jax.ShapeDtypeStruct((2 * N, ROWS, ROWS), F32),
        in_specs=[vmem],
        out_specs=anywhere,
        scratch_shapes=[pltpu.VMEM((N, ROWS, ROWS), F32), pltpu.SemaphoreType.DMA((N,))],
        compiler_params=pltpu.CompilerParams(vmem_limit_bytes=8 * 2**20),
        cost_estimate=pl.CostEstimate(flops=2**18, bytes_accessed=3 * 2**19, transcendentals=0),
    )(x)


def finish(x, own, before):
    anywhere, vmem = pl.BlockSpec(memory_space=pl.ANY), pl.BlockSpec(memory_space=pltpu.VMEM)
    grad = jax.ShapeDtypeStruct((SEQS // 2, 2 * HEAD, ROWS), BF)
    return pl.pallas_call(
        finish_kernel,
        out_shape=(jax.ShapeDtypeStruct(before.shape, F32), grad, grad, grad),
        in_specs=[vmem, vmem, anywhere],
        out_specs=(anywhere,) * 4,
        scratch_shapes=[
            pltpu.VMEM((N, ROWS, ROWS), F32),
            pltpu.VMEM((3, *grad.shape), BF),
            pltpu.SemaphoreType.DMA((N + 3,)),
        ],
        input_output_aliases={2: 0},
        compiler_params=pltpu.CompilerParams(vmem_limit_bytes=8 * 2**20),
        cost_estimate=pl.CostEstimate(flops=2**18, bytes_accessed=2**21, transcendentals=0),
    )(x, own, before)


def swap(x, axis, pairs):
    return lax.ppermute(x, axis, [(a, b) for a, b in pairs] + [(b, a) for a, b in pairs])


def add(a, b):
    return (a.astype(F32) + b.astype(F32)).astype(BF)


def body(query_proj, key_proj, value_proj, pair_bias, attn_output, output_grad):
    q, k, v, o, g = (
        jnp.swapaxes(x, 1, 2)
        for x in (query_proj, key_proj, value_proj, attn_output, output_grad)
    )
    grid = [(a, b) for a in range(N) for b in range(N)]

    keep, send, bias = pack(k, v, q, g, o, pair_bias)
    both = jnp.concatenate([keep, swap(send, "core", [(0, 1)])])
    kv, qgo = both[:, : 2 * HEAD], both[:, 2 * HEAD :]
    kvs = [
        lax.ppermute(kv, ("ri", "rj"), [(a * N + b, (a + b + t) % N * N + a) for a, b in grid])
        for t in range(N)
    ]
    bias = lax.all_to_all(bias, "rj", 0, 0, tiled=True)

    total, dq, *parts = attention(qgo, kvs, bias)

    def onward(part, axis, t):
        return lax.ppermute(part, axis, [(a, (a + t) % N) for a in range(N)])

    spread = lax.all_to_all(total, ("x", "rj"), 0, 0, tiled=True)
    first = [onward(parts[t], "rj", t) for t in range(1, 2)]
    spread, parts[0], *first = lax.optimization_barrier((spread, parts[0], *first))
    total = jnp.sum(spread.reshape(N, N, 64, ROWS).astype(F32), axis=0).astype(BF)
    other = swap(total, "zh", [(0, 1), (2, 3)])
    rest = hand_on(copy_kernel, total, *parts[2:])
    first += [onward(part, "rj", t) for t, part in enumerate(rest, 2)]
    total = add(total, other)
    other = swap(total, "zh", [(1, 2), (3, 0)])
    parts = hand_on(choose_kernel, total, parts[0], *first)
    parts = [parts[0]] + [onward(parts[t], "ri", t) for t in range(1, N)]
    total = add(total, other)
    mine = lax.all_gather(total, "x", axis=0, tiled=True).reshape(-1, ROWS)

    dkv = sum(x.astype(F32) for x in parts).astype(BF)
    grads = jnp.concatenate([dkv, dq], axis=1)
    own, others = grads[: SEQS // 2], grads[SEQS // 2 :]
    theirs = swap(jnp.concatenate([mine, others.reshape(-1, ROWS)]), "core", [(0, 1)])
    bias_grad, dk, dv, dq = finish(theirs, own, place(mine))
    return *(jnp.swapaxes(x, 1, 2) for x in (dq, dk, dv)), bias_grad


def solution(mesh):
    split = Mesh(mesh.devices.reshape(N, N, 2, N, N), ("zh", "x", "core", "ri", "rj"))
    seq = ("zh", "x", "core")
    rows, keys, tile = P(seq, "ri", "rj"), P(seq, "rj", "ri"), P(None, "ri", "rj")
    return jax.shard_map(
        body,
        mesh=split,
        in_specs=(rows, keys, keys, tile, rows, rows),
        out_specs=(rows, keys, keys, tile),
        check_vma=False,
    )
```

```python
import jax
import jax.numpy as jnp
from jax import lax
from jax.experimental import pallas as pl
from jax.experimental.pallas import tpu as pltpu
from jax.sharding import Mesh
from jax.sharding import PartitionSpec as P

HEAD = 32
SCALE = HEAD**-0.5
N = 4
ROWS = 256
KEYS = N * ROWS
LANES = 128
SEQS = 4
CHUNK = 32
UNROLL = 8
BF = jnp.bfloat16
F32 = jnp.float32
NT = (((1,), (1,)), ((), ()))
NN = (((1,), (0,)), ((), ()))


def pack_kernel(*refs):
    inputs, bias_ref = refs[:5], refs[5]
    keep, send, bias_out, held, bias_held, sem = refs[6:]
    core = lax.axis_index("core")
    inward = [
        pltpu.make_async_copy(x_ref, held.at[i], sem.at[i]) for i, x_ref in enumerate(inputs)
    ]
    bias_in = pltpu.make_async_copy(bias_ref.at[:, core], bias_held, sem.at[5])
    for c in (*inward, bias_in):
        c.start()
    for c in inward:
        c.wait()
    outward = []
    for i, (out, which) in enumerate(((send, 1 - core), (keep, core))):
        half = pl.ds(pl.multiple_of(which * HEAD, HEAD), HEAD)
        outward.append(pltpu.make_async_copy(held.at[:, :, half, :], out, sem.at[6 + i]))
        outward[-1].start()
    bias_in.wait()
    outward.append(pltpu.make_async_copy(bias_held, bias_out, sem.at[8]))
    outward[-1].start()
    for c in outward:
        c.wait()


def pack(*args):
    hbm = pl.BlockSpec(memory_space=pltpu.HBM)
    half = jax.ShapeDtypeStruct((5, SEQS // 2, HEAD, ROWS), BF)
    return pl.pallas_call(
        pack_kernel,
        out_shape=(half, half, jax.ShapeDtypeStruct((N, ROWS, ROWS), BF)),
        in_specs=[hbm] * 6,
        out_specs=(hbm,) * 3,
        scratch_shapes=[
            pltpu.VMEM((5, *args[0].shape), BF),
            pltpu.VMEM((N, ROWS, ROWS), BF),
            pltpu.SemaphoreType.DMA((9,)),
        ],
        compiler_params=pltpu.CompilerParams(vmem_limit_bytes=56 * 2**20),
        cost_estimate=pl.CostEstimate(flops=0, bytes_accessed=2**21, transcendentals=0),
    )(*args)


def attention_kernel(
    qgo_ref, kv0, kv1, kv2, kv3, bias,
    bias_grad, dq_ref, dkv_ref,
    stack, wide, raw, low, inner,
):
    ri, rj = lax.axis_index("ri"), lax.axis_index("rj")
    kvs = (kv0, kv1, kv2, kv3)
    blocks = [lax.rem(ri + 2 * N - rj - t, N) for t in range(N)]
    channel = lax.broadcasted_iota(jnp.int32, (2 * HEAD, ROWS), 0) // HEAD

    for s in range(SEQS):
        for part in range(2):
            at = slice(part * ROWS, (part + 1) * ROWS)
            one = jnp.where(channel == part, jnp.concatenate([qgo_ref[0, s], qgo_ref[1, s]]), 0)
            wide[s, :, at] = one
            stack[s, at, :] = one.T
        dots = qgo_ref[1, s].astype(F32) * qgo_ref[2, s].astype(F32)
        sums = jnp.sum(dots, axis=0, keepdims=True)
        inner[s] = jnp.broadcast_to(sums, (LANES, ROWS)).T

    for s in range(SEQS):
        for t in range(N):
            at = slice(t * ROWS, (t + 1) * ROWS)
            kv = jnp.concatenate([kvs[t][0, s], kvs[t][1, s]])
            raw[s, :, at] = lax.dot_general(stack[s], kv, NN, preferred_element_type=F32)

    @pl.loop(0, ROWS // CHUNK, unroll=UNROLL)
    def _(i):
        r0 = pl.multiple_of(i * CHUNK, CHUNK)
        at_logits = pl.ds(r0, CHUNK)
        at_grads = pl.ds(pl.multiple_of(ROWS + r0, CHUNK), CHUNK)
        pair = jnp.concatenate([bias[b, at_logits, :] for b in blocks], axis=1).astype(F32)
        total = None
        for s in range(SEQS):
            logits = raw[s, at_logits, :] * SCALE + pair
            top = jnp.max(logits, axis=1, keepdims=True)
            weights = jnp.exp(logits - top)
            weights = weights * (1.0 / jnp.sum(weights, axis=1, keepdims=True))
            dots = jnp.concatenate([inner[s, at_logits, :]] * (KEYS // LANES), axis=1)
            grad = weights * (raw[s, at_grads, :] - dots)
            low[s, at_logits, :] = grad.astype(BF)
            low[s, at_grads, :] = weights.astype(BF)
            total = grad if total is None else total + grad
        total = total.astype(BF)
        quarter = i // (64 // CHUNK)
        within = pl.ds(pl.multiple_of(lax.rem(i, 64 // CHUNK) * CHUNK, CHUNK), CHUNK)
        for t, b in enumerate(blocks):
            bias_grad[quarter * N + b, within, :] = total[:, t * ROWS : (t + 1) * ROWS]

    for s in range(SEQS):
        query_grads = None
        for t, b in enumerate(blocks):
            at = slice(t * ROWS, (t + 1) * ROWS)
            grads = lax.dot_general(wide[s], low[s, :, at], NN, preferred_element_type=F32)
            grads = jnp.where(channel == 0, grads * SCALE, grads)
            dkv_ref[lax.rem(b + N - rj, N), s] = grads.astype(BF)
            key = kvs[t][0, s]
            term = lax.dot_general(low[s, :ROWS, at], key, NT, preferred_element_type=F32)
            query_grads = term if query_grads is None else query_grads + term
        dq_ref[s] = (query_grads.T * SCALE).astype(BF)


def attention(qgo, kvs, bias):
    vmem = pl.BlockSpec(memory_space=pltpu.VMEM)
    return pl.pallas_call(
        attention_kernel,
        out_shape=(
            jax.ShapeDtypeStruct((N * N, 64, ROWS), BF),
            jax.ShapeDtypeStruct((SEQS, HEAD, ROWS), BF),
            jax.ShapeDtypeStruct((N, SEQS, 2 * HEAD, ROWS), BF),
        ),
        in_specs=[vmem] * 6,
        out_specs=(vmem,) * 3,
        scratch_shapes=[
            pltpu.VMEM((SEQS, 2 * ROWS, 2 * HEAD), BF),
            pltpu.VMEM((SEQS, 2 * HEAD, 2 * ROWS), BF),
            pltpu.VMEM((SEQS, 2 * ROWS, KEYS), F32),
            pltpu.VMEM((SEQS, 2 * ROWS, KEYS), BF),
            pltpu.VMEM((SEQS, ROWS, LANES), F32),
        ],
        compiler_params=pltpu.CompilerParams(vmem_limit_bytes=32 * 2**20),
        cost_estimate=pl.CostEstimate(
            flops=5 * 2 * 2**25, bytes_accessed=6 * 2**20, transcendentals=2**20
        ),
    )(qgo, *kvs, bias)


def split_kernel(after, x_ref, *outs):
    for t, out in enumerate(outs):
        out[...] = x_ref[t]


def choose_kernel(after, *refs):
    ri, rj = lax.axis_index("ri"), lax.axis_index("rj")
    for t, out in enumerate(refs[N:]):
        wanted = lax.rem(rj + 2 * N - ri - t, N)
        for source, x_ref in enumerate(refs[:N]):

            @pl.when(wanted == source)
            def _():
                out[...] = x_ref[...]


def hand_on(kernel, after, *args):
    anywhere, vmem = pl.BlockSpec(memory_space=pl.ANY), pl.BlockSpec(memory_space=pltpu.VMEM)
    return pl.pallas_call(
        kernel,
        out_shape=[jax.ShapeDtypeStruct(args[0].shape[-3:], BF)] * N,
        in_specs=[anywhere] + [vmem] * len(args),
        out_specs=[vmem] * N,
        compiler_params=pltpu.CompilerParams(vmem_limit_bytes=8 * 2**20),
        cost_estimate=pl.CostEstimate(flops=0, bytes_accessed=2**21, transcendentals=0),
    )(after, *args)


def place_heads(x_ref, out_ref, wide, sem, head):
    copies = []
    for j in range(N):
        for x in range(N):
            at = (x * N + j) * 64
            wide[j, x * 64 : (x + 1) * 64, :] = x_ref[at : at + 64, :].astype(F32)
        copies.append(pltpu.make_async_copy(wide.at[j], out_ref.at[2 * j + head], sem.at[j]))
        copies[-1].start()
    return copies


def place_kernel(x_ref, out_ref, wide, sem):
    for c in place_heads(x_ref, out_ref, wide, sem, lax.axis_index("core")):
        c.wait()


def finish_kernel(x_ref, own_ref, before, out_ref, dk_ref, dv_ref, dq_ref, wide, both, sem):
    core = lax.axis_index("core")
    copies = place_heads(x_ref, out_ref, wide, sem, 1 - core)
    mine = pl.ds(pl.multiple_of(core * HEAD, HEAD), HEAD)
    theirs = pl.ds(pl.multiple_of((1 - core) * HEAD, HEAD), HEAD)
    for i, grad_ref in enumerate((dk_ref, dv_ref, dq_ref)):
        for s in range(SEQS // 2):
            at = N * ROWS + (s * 3 + i) * HEAD
            both[i, s, mine, :] = own_ref[s, i * HEAD : (i + 1) * HEAD, :]
            both[i, s, theirs, :] = x_ref[at : at + HEAD, :]
        copies.append(pltpu.make_async_copy(both.at[i], grad_ref, sem.at[N + i]))
        copies[-1].start()
    for c in copies:
        c.wait()


def place(x):
    anywhere, vmem = pl.BlockSpec(memory_space=pl.ANY), pl.BlockSpec(memory_space=pltpu.VMEM)
    return pl.pallas_call(
        place_kernel,
        out_shape=jax.ShapeDtypeStruct((2 * N, ROWS, ROWS), F32),
        in_specs=[vmem],
        out_specs=anywhere,
        scratch_shapes=[pltpu.VMEM((N, ROWS, ROWS), F32), pltpu.SemaphoreType.DMA((N,))],
        compiler_params=pltpu.CompilerParams(vmem_limit_bytes=8 * 2**20),
        cost_estimate=pl.CostEstimate(flops=2**18, bytes_accessed=3 * 2**19, transcendentals=0),
    )(x)


def finish(x, own, before):
    anywhere, vmem = pl.BlockSpec(memory_space=pl.ANY), pl.BlockSpec(memory_space=pltpu.VMEM)
    grad = jax.ShapeDtypeStruct((SEQS // 2, 2 * HEAD, ROWS), BF)
    return pl.pallas_call(
        finish_kernel,
        out_shape=(jax.ShapeDtypeStruct(before.shape, F32), grad, grad, grad),
        in_specs=[vmem, vmem, anywhere],
        out_specs=(anywhere,) * 4,
        scratch_shapes=[
            pltpu.VMEM((N, ROWS, ROWS), F32),
            pltpu.VMEM((3, *grad.shape), BF),
            pltpu.SemaphoreType.DMA((N + 3,)),
        ],
        input_output_aliases={2: 0},
        compiler_params=pltpu.CompilerParams(vmem_limit_bytes=8 * 2**20),
        cost_estimate=pl.CostEstimate(flops=2**18, bytes_accessed=2**21, transcendentals=0),
    )(x, own, before)


def swap(x, axis, pairs):
    return lax.ppermute(x, axis, [(a, b) for a, b in pairs] + [(b, a) for a, b in pairs])


def add(a, b):
    return (a.astype(F32) + b.astype(F32)).astype(BF)


def body(query_proj, key_proj, value_proj, pair_bias, attn_output, output_grad):
    q, k, v, o, g = (
        jnp.swapaxes(x, 1, 2)
        for x in (query_proj, key_proj, value_proj, attn_output, output_grad)
    )
    grid = [(a, b) for a in range(N) for b in range(N)]

    keep, send, bias = pack(k, v, q, g, o, pair_bias.reshape(N, 2, ROWS, ROWS))
    given = swap(send, "core", [(0, 1)])
    kv, qgo = (jnp.concatenate([keep[at], given[at]], axis=1) for at in (slice(2), slice(2, 5)))
    kvs = [
        lax.ppermute(kv, ("ri", "rj"), [(a * N + b, (a + b + t) % N * N + a) for a, b in grid])
        for t in range(N)
    ]
    bias = lax.all_to_all(bias, "rj", 0, 0, tiled=True)

    total, dq, dkv = attention(qgo, kvs, bias)

    def spread_out(parts, axis):
        return [parts[0]] + [
            lax.ppermute(parts[t], axis, [(a, (a + t) % N) for a in range(N)])
            for t in range(1, N)
        ]

    spread = lax.all_to_all(total, ("x", "rj"), 0, 0, tiled=True)
    total = jnp.sum(spread.reshape(N, N, 64, ROWS).astype(F32), axis=0).astype(BF)
    other = swap(total, "zh", [(0, 1), (2, 3)])
    parts = spread_out(hand_on(split_kernel, total, dkv), "rj")
    total = add(total, other)
    other = swap(total, "zh", [(1, 2), (3, 0)])
    parts = spread_out(hand_on(choose_kernel, total, *parts), "ri")
    total = add(total, other)
    mine = lax.all_gather(total, "x", axis=0, tiled=True).reshape(-1, ROWS)

    dkv = sum(x.astype(F32) for x in parts).astype(BF)
    grads = jnp.concatenate([dkv, dq], axis=1)
    own, others = grads[: SEQS // 2], grads[SEQS // 2 :]
    theirs = swap(jnp.concatenate([mine, others.reshape(-1, ROWS)]), "core", [(0, 1)])
    bias_grad, dk, dv, dq = finish(theirs, own, place(mine))
    return *(jnp.swapaxes(x, 1, 2) for x in (dq, dk, dv)), bias_grad


def solution(mesh):
    split = Mesh(mesh.devices.reshape(N, N, 2, N, N), ("zh", "x", "core", "ri", "rj"))
    seq = ("zh", "x", "core")
    rows, keys, tile = P(seq, "ri", "rj"), P(seq, "rj", "ri"), P(None, "ri", "rj")
    return jax.shard_map(
        body,
        mesh=split,
        in_specs=(rows, keys, keys, tile, rows, rows),
        out_specs=(rows, keys, keys, tile),
        check_vma=False,
    )
```

```python
import jax
import jax.numpy as jnp
from jax import lax
from jax.experimental import pallas as pl
from jax.experimental.pallas import tpu as pltpu
from jax.sharding import Mesh
from jax.sharding import PartitionSpec as P

HEAD = 32
SCALE = HEAD**-0.5
N = 4
ROWS = 256
KEYS = N * ROWS
LANES = 128
SEQS = 4
CHUNK = 32
UNROLL = 8
BF = jnp.bfloat16
F32 = jnp.float32
NT = (((1,), (1,)), ((), ()))
NN = (((1,), (0,)), ((), ()))


def pack_kernel(*refs):
    inputs, bias_ref = refs[:5], refs[5]
    keep, send, bias_out, held, bias_held, sem = refs[6:]
    core = lax.axis_index("core")
    inward = [
        pltpu.make_async_copy(x_ref, held.at[i], sem.at[i]) for i, x_ref in enumerate(inputs)
    ]
    bias_in = pltpu.make_async_copy(bias_ref.at[:, core], bias_held, sem.at[5])
    for c in (*inward, bias_in):
        c.start()
    for c in inward:
        c.wait()
    outward = []
    for i, (out, which) in enumerate(((send, 1 - core), (keep, core))):
        half = pl.ds(pl.multiple_of(which * HEAD, HEAD), HEAD)
        outward.append(pltpu.make_async_copy(held.at[:, :, half, :], out, sem.at[6 + i]))
        outward[-1].start()
    bias_in.wait()
    outward.append(pltpu.make_async_copy(bias_held, bias_out, sem.at[8]))
    outward[-1].start()
    for c in outward:
        c.wait()


def pack(*args):
    hbm = pl.BlockSpec(memory_space=pltpu.HBM)
    half = jax.ShapeDtypeStruct((5, SEQS // 2, HEAD, ROWS), BF)
    return pl.pallas_call(
        pack_kernel,
        out_shape=(half, half, jax.ShapeDtypeStruct((N, ROWS, ROWS), BF)),
        in_specs=[hbm] * 6,
        out_specs=(hbm,) * 3,
        scratch_shapes=[
            pltpu.VMEM((5, *args[0].shape), BF),
            pltpu.VMEM((N, ROWS, ROWS), BF),
            pltpu.SemaphoreType.DMA((9,)),
        ],
        compiler_params=pltpu.CompilerParams(vmem_limit_bytes=56 * 2**20),
        cost_estimate=pl.CostEstimate(flops=0, bytes_accessed=2**21, transcendentals=0),
    )(*args)


def attention_kernel(
    qgo_ref, kv0, kv1, kv2, kv3, bias,
    bias_grad, dq_ref, dkv_ref,
    stack, wide, raw, low, inner,
):
    ri, rj = lax.axis_index("ri"), lax.axis_index("rj")
    kvs = (kv0, kv1, kv2, kv3)
    blocks = [lax.rem(ri + 2 * N - rj - t, N) for t in range(N)]
    channel = lax.broadcasted_iota(jnp.int32, (2 * HEAD, ROWS), 0) // HEAD

    for s in range(SEQS):
        for part in range(2):
            at = slice(part * ROWS, (part + 1) * ROWS)
            one = jnp.where(channel == part, jnp.concatenate([qgo_ref[0, s], qgo_ref[1, s]]), 0)
            wide[s, :, at] = one
            stack[s, at, :] = one.T
        dots = qgo_ref[1, s].astype(F32) * qgo_ref[2, s].astype(F32)
        sums = jnp.sum(dots, axis=0, keepdims=True)
        inner[s] = jnp.broadcast_to(sums, (LANES, ROWS)).T

    for s in range(SEQS):
        for t in range(N):
            at = slice(t * ROWS, (t + 1) * ROWS)
            kv = jnp.concatenate([kvs[t][0, s], kvs[t][1, s]])
            raw[s, :, at] = lax.dot_general(stack[s], kv, NN, preferred_element_type=F32)

    @pl.loop(0, ROWS // CHUNK, unroll=UNROLL)
    def _(i):
        r0 = pl.multiple_of(i * CHUNK, CHUNK)
        at_logits = pl.ds(r0, CHUNK)
        at_grads = pl.ds(pl.multiple_of(ROWS + r0, CHUNK), CHUNK)
        pair = jnp.concatenate([bias[b, at_logits, :] for b in blocks], axis=1).astype(F32)
        total = None
        for s in range(SEQS):
            logits = raw[s, at_logits, :] * SCALE + pair
            top = jnp.max(logits, axis=1, keepdims=True)
            weights = jnp.exp(logits - top)
            weights = weights * (1.0 / jnp.sum(weights, axis=1, keepdims=True))
            dots = jnp.concatenate([inner[s, at_logits, :]] * (KEYS // LANES), axis=1)
            grad = weights * (raw[s, at_grads, :] - dots)
            low[s, at_logits, :] = grad.astype(BF)
            low[s, at_grads, :] = weights.astype(BF)
            total = grad if total is None else total + grad
        total = total.astype(BF)
        quarter = i // (64 // CHUNK)
        within = pl.ds(pl.multiple_of(lax.rem(i, 64 // CHUNK) * CHUNK, CHUNK), CHUNK)
        for t, b in enumerate(blocks):
            bias_grad[quarter * N + b, within, :] = total[:, t * ROWS : (t + 1) * ROWS]

    for s in range(SEQS):
        query_grads = None
        for t, b in enumerate(blocks):
            at = slice(t * ROWS, (t + 1) * ROWS)
            grads = lax.dot_general(wide[s], low[s, :, at], NN, preferred_element_type=F32)
            grads = jnp.where(channel == 0, grads * SCALE, grads)
            dkv_ref[lax.rem(b + N - rj, N), s] = grads.astype(BF)
            key = kvs[t][0, s]
            term = lax.dot_general(low[s, :ROWS, at], key, NT, preferred_element_type=F32)
            query_grads = term if query_grads is None else query_grads + term
        dq_ref[s] = (query_grads.T * SCALE).astype(BF)


def attention(qgo, kvs, bias):
    vmem = pl.BlockSpec(memory_space=pltpu.VMEM)
    return pl.pallas_call(
        attention_kernel,
        out_shape=(
            jax.ShapeDtypeStruct((N * N, 64, ROWS), BF),
            jax.ShapeDtypeStruct((SEQS, HEAD, ROWS), BF),
            jax.ShapeDtypeStruct((N, SEQS, 2 * HEAD, ROWS), BF),
        ),
        in_specs=[vmem] * 6,
        out_specs=(vmem,) * 3,
        scratch_shapes=[
            pltpu.VMEM((SEQS, 2 * ROWS, 2 * HEAD), BF),
            pltpu.VMEM((SEQS, 2 * HEAD, 2 * ROWS), BF),
            pltpu.VMEM((SEQS, 2 * ROWS, KEYS), F32),
            pltpu.VMEM((SEQS, 2 * ROWS, KEYS), BF),
            pltpu.VMEM((SEQS, ROWS, LANES), F32),
        ],
        compiler_params=pltpu.CompilerParams(vmem_limit_bytes=32 * 2**20),
        cost_estimate=pl.CostEstimate(
            flops=5 * 2 * 2**25, bytes_accessed=6 * 2**20, transcendentals=2**20
        ),
    )(qgo, *kvs, bias)


def split_kernel(after, x_ref, *outs):
    for t, out in enumerate(outs):
        out[...] = x_ref[t]


def choose_kernel(after, *refs):
    ri, rj = lax.axis_index("ri"), lax.axis_index("rj")
    for t, out in enumerate(refs[N:]):
        wanted = lax.rem(rj + 2 * N - ri - t, N)
        for source, x_ref in enumerate(refs[:N]):

            @pl.when(wanted == source)
            def _():
                out[...] = x_ref[...]


def hand_on(kernel, after, *args):
    anywhere, vmem = pl.BlockSpec(memory_space=pl.ANY), pl.BlockSpec(memory_space=pltpu.VMEM)
    return pl.pallas_call(
        kernel,
        out_shape=[jax.ShapeDtypeStruct(args[0].shape[-3:], BF)] * N,
        in_specs=[anywhere] + [vmem] * len(args),
        out_specs=[vmem] * N,
        compiler_params=pltpu.CompilerParams(vmem_limit_bytes=8 * 2**20),
        cost_estimate=pl.CostEstimate(flops=0, bytes_accessed=2**21, transcendentals=0),
    )(after, *args)


def place_heads(x_ref, out_ref, wide, sem, head):
    copies, place = [], lax.axis_index("x")
    for j in range(N):
        for t in range(N):
            at, rows = (t * N + j) * 64, lax.rem(place + N - t, N) * 64
            wide[j, pl.ds(pl.multiple_of(rows, 64), 64), :] = x_ref[at : at + 64, :].astype(F32)
        copies.append(pltpu.make_async_copy(wide.at[j], out_ref.at[2 * j + head], sem.at[j]))
        copies[-1].start()
    return copies


def place_kernel(x_ref, out_ref, wide, sem):
    for c in place_heads(x_ref, out_ref, wide, sem, lax.axis_index("core")):
        c.wait()


def finish_kernel(x_ref, own_ref, before, out_ref, dk_ref, dv_ref, dq_ref, wide, both, sem):
    core = lax.axis_index("core")
    copies = place_heads(x_ref, out_ref, wide, sem, 1 - core)
    mine = pl.ds(pl.multiple_of(core * HEAD, HEAD), HEAD)
    theirs = pl.ds(pl.multiple_of((1 - core) * HEAD, HEAD), HEAD)
    for i, grad_ref in enumerate((dk_ref, dv_ref, dq_ref)):
        for s in range(SEQS // 2):
            at = N * ROWS + (s * 3 + i) * HEAD
            both[i, s, mine, :] = own_ref[s, i * HEAD : (i + 1) * HEAD, :]
            both[i, s, theirs, :] = x_ref[at : at + HEAD, :]
        copies.append(pltpu.make_async_copy(both.at[i], grad_ref, sem.at[N + i]))
        copies[-1].start()
    for c in copies:
        c.wait()


def place(x):
    anywhere, vmem = pl.BlockSpec(memory_space=pl.ANY), pl.BlockSpec(memory_space=pltpu.VMEM)
    return pl.pallas_call(
        place_kernel,
        out_shape=jax.ShapeDtypeStruct((2 * N, ROWS, ROWS), F32),
        in_specs=[vmem],
        out_specs=anywhere,
        scratch_shapes=[pltpu.VMEM((N, ROWS, ROWS), F32), pltpu.SemaphoreType.DMA((N,))],
        compiler_params=pltpu.CompilerParams(vmem_limit_bytes=8 * 2**20),
        cost_estimate=pl.CostEstimate(flops=2**18, bytes_accessed=3 * 2**19, transcendentals=0),
    )(x)


def finish(x, own, before):
    anywhere, vmem = pl.BlockSpec(memory_space=pl.ANY), pl.BlockSpec(memory_space=pltpu.VMEM)
    grad = jax.ShapeDtypeStruct((SEQS // 2, 2 * HEAD, ROWS), BF)
    return pl.pallas_call(
        finish_kernel,
        out_shape=(jax.ShapeDtypeStruct(before.shape, F32), grad, grad, grad),
        in_specs=[vmem, vmem, anywhere],
        out_specs=(anywhere,) * 4,
        scratch_shapes=[
            pltpu.VMEM((N, ROWS, ROWS), F32),
            pltpu.VMEM((3, *grad.shape), BF),
            pltpu.SemaphoreType.DMA((N + 3,)),
        ],
        input_output_aliases={2: 0},
        compiler_params=pltpu.CompilerParams(vmem_limit_bytes=8 * 2**20),
        cost_estimate=pl.CostEstimate(flops=2**18, bytes_accessed=2**21, transcendentals=0),
    )(x, own, before)


def swap(x, axis, pairs):
    return lax.ppermute(x, axis, [(a, b) for a, b in pairs] + [(b, a) for a, b in pairs])


def add(a, b):
    return (a.astype(F32) + b.astype(F32)).astype(BF)


def body(query_proj, key_proj, value_proj, pair_bias, attn_output, output_grad):
    q, k, v, o, g = (
        jnp.swapaxes(x, 1, 2)
        for x in (query_proj, key_proj, value_proj, attn_output, output_grad)
    )
    grid = [(a, b) for a in range(N) for b in range(N)]

    keep, send, bias = pack(k, v, q, g, o, pair_bias.reshape(N, 2, ROWS, ROWS))
    given = swap(send, "core", [(0, 1)])
    kv, qgo = (jnp.concatenate([keep[at], given[at]], axis=1) for at in (slice(2), slice(2, 5)))
    kvs = [
        lax.ppermute(kv, ("ri", "rj"), [(a * N + b, (a + b + t) % N * N + a) for a, b in grid])
        for t in range(N)
    ]
    bias = lax.all_to_all(bias, "rj", 0, 0, tiled=True)

    total, dq, dkv = attention(qgo, kvs, bias)

    def spread_out(parts, axis):
        return [parts[0]] + [
            lax.ppermute(parts[t], axis, [(a, (a + t) % N) for a in range(N)])
            for t in range(1, N)
        ]

    spread = lax.all_to_all(total, ("x", "rj"), 0, 0, tiled=True)
    total = jnp.sum(spread.reshape(N, N, 64, ROWS).astype(F32), axis=0).astype(BF)
    other = swap(total, "zh", [(0, 1), (2, 3)])
    parts = spread_out(hand_on(split_kernel, total, dkv), "rj")
    total = add(total, other)
    other = swap(total, "zh", [(1, 2), (3, 0)])
    parts = spread_out(hand_on(choose_kernel, total, *parts), "ri")
    total = add(total, other)
    total, *parts = lax.optimization_barrier((total, *parts))
    mine = jnp.concatenate(spread_out([total] * N, "x")).reshape(-1, ROWS)

    dkv = sum(x.astype(F32) for x in parts).astype(BF)
    grads = jnp.concatenate([dkv, dq], axis=1)
    own, others = grads[: SEQS // 2], grads[SEQS // 2 :]
    theirs = swap(jnp.concatenate([mine, others.reshape(-1, ROWS)]), "core", [(0, 1)])
    bias_grad, dk, dv, dq = finish(theirs, own, place(mine))
    return *(jnp.swapaxes(x, 1, 2) for x in (dq, dk, dv)), bias_grad


def solution(mesh):
    split = Mesh(mesh.devices.reshape(N, N, 2, N, N), ("zh", "x", "core", "ri", "rj"))
    seq = ("zh", "x", "core")
    rows, keys, tile = P(seq, "ri", "rj"), P(seq, "rj", "ri"), P(None, "ri", "rj")
    return jax.shard_map(
        body,
        mesh=split,
        in_specs=(rows, keys, keys, tile, rows, rows),
        out_specs=(rows, keys, keys, tile),
        check_vma=False,
    )
```

```python
import jax
import jax.numpy as jnp
from jax import lax
from jax.experimental import pallas as pl
from jax.experimental.pallas import tpu as pltpu
from jax.sharding import Mesh
from jax.sharding import PartitionSpec as P

HEAD = 32
SCALE = HEAD**-0.5
N = 4
ROWS = 256
KEYS = N * ROWS
LANES = 128
SEQS = 4
CHUNK = 32
UNROLL = 8
BF = jnp.bfloat16
F32 = jnp.float32
NT = (((1,), (1,)), ((), ()))
NN = (((1,), (0,)), ((), ()))


def pick_kernel(q_ref, g_ref, o_ref, first, second, send):
    other = 1 - lax.axis_index("core")
    at = 0
    half = pl.ds(pl.multiple_of(other * HEAD, HEAD), HEAD)
    for x_ref in (q_ref, g_ref, o_ref):
        for s in range(SEQS // 2):
            send[at : at + HEAD, :] = x_ref[s, half, :]
            at += HEAD
    for x_ref in (first, second):
        for s in range(SEQS):
            for part in range(2):
                half = pl.ds(pl.multiple_of((2 * part + other) * HEAD, HEAD), HEAD)
                send[at : at + HEAD, :] = x_ref[s, half, :]
                at += HEAD


def pick(*args):
    vmem = pl.BlockSpec(memory_space=pltpu.VMEM)
    rows = (3 * (SEQS // 2) + 2 * SEQS * 2) * HEAD
    return pl.pallas_call(
        pick_kernel,
        out_shape=jax.ShapeDtypeStruct((rows, ROWS), BF),
        in_specs=[vmem] * 5,
        out_specs=vmem,
        compiler_params=pltpu.CompilerParams(vmem_limit_bytes=8 * 2**20),
        cost_estimate=pl.CostEstimate(flops=0, bytes_accessed=2**20, transcendentals=0),
    )(*args)


def attention_kernel(
    q_ref, g_ref, o_ref, first, second, given, bias,
    bias_grad, dq_ref, dkv_ref,
    stack, wide, raw, low, inner,
):
    ri, rj, core = (lax.axis_index(a) for a in ("ri", "rj", "core"))
    own = pl.ds(pl.multiple_of(core * HEAD, HEAD), HEAD)
    rounds = [2 * core, 2 * core + 1, 2 - 2 * core, 3 - 2 * core]
    blocks = [lax.rem(ri + 2 * N - rj - t, N) for t in rounds]

    def query_side(i, s):
        if s < SEQS // 2:
            return (q_ref, g_ref, o_ref)[i][s, own, :]
        at = (i * (SEQS // 2) + s - SEQS // 2) * HEAD
        return given[at : at + HEAD, :]

    def key_side(part, t, s):
        place = 2 * core + s if s < SEQS // 2 else 2 * (1 - core) + s - SEQS // 2
        if t < 2:
            half = pl.ds(pl.multiple_of((2 * part + core) * HEAD, HEAD), HEAD)
            return (first, second)[t][place, half, :]
        at = 3 * (SEQS // 2) + (((t - 2) * SEQS + place) * 2 + part)
        return given[pl.ds(pl.multiple_of(at * HEAD, HEAD), HEAD), :]
    channel = lax.broadcasted_iota(jnp.int32, (2 * HEAD, ROWS), 0) // HEAD

    for s in range(SEQS):
        for part in range(2):
            at = slice(part * ROWS, (part + 1) * ROWS)
            one = jnp.where(channel == part, jnp.concatenate([query_side(0, s), query_side(1, s)]), 0)
            wide[s, :, at] = one
            stack[s, at, :] = one.T
        dots = query_side(1, s).astype(F32) * query_side(2, s).astype(F32)
        sums = jnp.sum(dots, axis=0, keepdims=True)
        inner[s] = jnp.broadcast_to(sums, (LANES, ROWS)).T

    for s in range(SEQS):
        for t in range(N):
            at = slice(t * ROWS, (t + 1) * ROWS)
            kv = jnp.concatenate([key_side(0, t, s), key_side(1, t, s)])
            raw[s, :, at] = lax.dot_general(stack[s], kv, NN, preferred_element_type=F32)

    @pl.loop(0, ROWS // CHUNK, unroll=UNROLL)
    def _(i):
        r0 = pl.multiple_of(i * CHUNK, CHUNK)
        at_logits = pl.ds(r0, CHUNK)
        at_grads = pl.ds(pl.multiple_of(ROWS + r0, CHUNK), CHUNK)
        pair = jnp.concatenate([bias[b, at_logits, :] for b in blocks], axis=1).astype(F32)
        total = None
        for s in range(SEQS):
            logits = raw[s, at_logits, :] * SCALE + pair
            top = jnp.max(logits, axis=1, keepdims=True)
            weights = jnp.exp(logits - top)
            weights = weights * (1.0 / jnp.sum(weights, axis=1, keepdims=True))
            dots = jnp.concatenate([inner[s, at_logits, :]] * (KEYS // LANES), axis=1)
            grad = weights * (raw[s, at_grads, :] - dots)
            low[s, at_logits, :] = grad.astype(BF)
            low[s, at_grads, :] = weights.astype(BF)
            total = grad if total is None else total + grad
        total = total.astype(BF)
        quarter = i // (64 // CHUNK)
        within = pl.ds(pl.multiple_of(lax.rem(i, 64 // CHUNK) * CHUNK, CHUNK), CHUNK)
        for t, b in enumerate(blocks):
            bias_grad[quarter * N + b, within, :] = total[:, t * ROWS : (t + 1) * ROWS]

    for s in range(SEQS):
        query_grads = None
        for t, b in enumerate(blocks):
            at = slice(t * ROWS, (t + 1) * ROWS)
            grads = lax.dot_general(wide[s], low[s, :, at], NN, preferred_element_type=F32)
            grads = jnp.where(channel == 0, grads * SCALE, grads)
            dkv_ref[lax.rem(b + N - rj, N), s] = grads.astype(BF)
            key = key_side(0, t, s)
            term = lax.dot_general(low[s, :ROWS, at], key, NT, preferred_element_type=F32)
            query_grads = term if query_grads is None else query_grads + term
        dq_ref[s] = (query_grads.T * SCALE).astype(BF)


def attention(*args):
    vmem = pl.BlockSpec(memory_space=pltpu.VMEM)
    return pl.pallas_call(
        attention_kernel,
        out_shape=(
            jax.ShapeDtypeStruct((N * N, 64, ROWS), BF),
            jax.ShapeDtypeStruct((SEQS, HEAD, ROWS), BF),
            jax.ShapeDtypeStruct((N, SEQS, 2 * HEAD, ROWS), BF),
        ),
        in_specs=[vmem] * 7,
        out_specs=(vmem,) * 3,
        scratch_shapes=[
            pltpu.VMEM((SEQS, 2 * ROWS, 2 * HEAD), BF),
            pltpu.VMEM((SEQS, 2 * HEAD, 2 * ROWS), BF),
            pltpu.VMEM((SEQS, 2 * ROWS, KEYS), F32),
            pltpu.VMEM((SEQS, 2 * ROWS, KEYS), BF),
            pltpu.VMEM((SEQS, ROWS, LANES), F32),
        ],
        compiler_params=pltpu.CompilerParams(vmem_limit_bytes=32 * 2**20),
        cost_estimate=pl.CostEstimate(
            flops=5 * 2 * 2**25, bytes_accessed=6 * 2**20, transcendentals=2**20
        ),
    )(*args)


def split_kernel(after, x_ref, *outs):
    for t, out in enumerate(outs):
        out[...] = x_ref[t]


def choose_kernel(after, *refs):
    ri, rj = lax.axis_index("ri"), lax.axis_index("rj")
    for t, out in enumerate(refs[N:]):
        wanted = lax.rem(rj + 2 * N - ri - t, N)
        for source, x_ref in enumerate(refs[:N]):

            @pl.when(wanted == source)
            def _():
                out[...] = x_ref[...]


def hand_on(kernel, after, *args):
    anywhere, vmem = pl.BlockSpec(memory_space=pl.ANY), pl.BlockSpec(memory_space=pltpu.VMEM)
    return pl.pallas_call(
        kernel,
        out_shape=[jax.ShapeDtypeStruct(args[0].shape[-3:], BF)] * N,
        in_specs=[anywhere] + [vmem] * len(args),
        out_specs=[vmem] * N,
        compiler_params=pltpu.CompilerParams(vmem_limit_bytes=8 * 2**20),
        cost_estimate=pl.CostEstimate(flops=0, bytes_accessed=2**21, transcendentals=0),
    )(after, *args)


def place_heads(x_ref, out_ref, wide, sem, head):
    copies = []
    for j in range(N):
        for x in range(N):
            at = (x * N + j) * 64
            wide[j, x * 64 : (x + 1) * 64, :] = x_ref[at : at + 64, :].astype(F32)
        copies.append(pltpu.make_async_copy(wide.at[j], out_ref.at[2 * j + head], sem.at[j]))
        copies[-1].start()
    return copies


def place_kernel(x_ref, out_ref, wide, sem):
    for c in place_heads(x_ref, out_ref, wide, sem, lax.axis_index("core")):
        c.wait()


def finish_kernel(x_ref, own_ref, before, out_ref, dk_ref, dv_ref, dq_ref, wide, both, sem):
    core = lax.axis_index("core")
    copies = place_heads(x_ref, out_ref, wide, sem, 1 - core)
    mine = pl.ds(pl.multiple_of(core * HEAD, HEAD), HEAD)
    theirs = pl.ds(pl.multiple_of((1 - core) * HEAD, HEAD), HEAD)
    for i, grad_ref in enumerate((dk_ref, dv_ref, dq_ref)):
        for s in range(SEQS // 2):
            at = N * ROWS + (s * 3 + i) * HEAD
            both[i, s, mine, :] = own_ref[s, i * HEAD : (i + 1) * HEAD, :]
            both[i, s, theirs, :] = x_ref[at : at + HEAD, :]
        copies.append(pltpu.make_async_copy(both.at[i], grad_ref, sem.at[N + i]))
        copies[-1].start()
    for c in copies:
        c.wait()


def place(x):
    anywhere, vmem = pl.BlockSpec(memory_space=pl.ANY), pl.BlockSpec(memory_space=pltpu.VMEM)
    return pl.pallas_call(
        place_kernel,
        out_shape=jax.ShapeDtypeStruct((2 * N, ROWS, ROWS), F32),
        in_specs=[vmem],
        out_specs=anywhere,
        scratch_shapes=[pltpu.VMEM((N, ROWS, ROWS), F32), pltpu.SemaphoreType.DMA((N,))],
        compiler_params=pltpu.CompilerParams(vmem_limit_bytes=8 * 2**20),
        cost_estimate=pl.CostEstimate(flops=2**18, bytes_accessed=3 * 2**19, transcendentals=0),
    )(x)


def finish(x, own, before):
    anywhere, vmem = pl.BlockSpec(memory_space=pl.ANY), pl.BlockSpec(memory_space=pltpu.VMEM)
    grad = jax.ShapeDtypeStruct((SEQS // 2, 2 * HEAD, ROWS), BF)
    return pl.pallas_call(
        finish_kernel,
        out_shape=(jax.ShapeDtypeStruct(before.shape, F32), grad, grad, grad),
        in_specs=[vmem, vmem, anywhere],
        out_specs=(anywhere,) * 4,
        scratch_shapes=[
            pltpu.VMEM((N, ROWS, ROWS), F32),
            pltpu.VMEM((3, *grad.shape), BF),
            pltpu.SemaphoreType.DMA((N + 3,)),
        ],
        input_output_aliases={2: 0},
        compiler_params=pltpu.CompilerParams(vmem_limit_bytes=8 * 2**20),
        cost_estimate=pl.CostEstimate(flops=2**18, bytes_accessed=2**21, transcendentals=0),
    )(x, own, before)


def swap(x, axis, pairs):
    return lax.ppermute(x, axis, [(a, b) for a, b in pairs] + [(b, a) for a, b in pairs])


def add(a, b):
    return (a.astype(F32) + b.astype(F32)).astype(BF)


def body(query_proj, key_proj, value_proj, pair_bias, attn_output, output_grad):
    q, k, v, o, g = (
        jnp.swapaxes(x, 1, 2)
        for x in (query_proj, key_proj, value_proj, attn_output, output_grad)
    )
    grid = [(a, b) for a in range(N) for b in range(N)]

    core = lax.axis_index("core")
    held = jnp.concatenate([k, v], axis=1)
    theirs = swap(held, "core", [(0, 1)])
    kv = jnp.concatenate([jnp.where(core == c, held, theirs) for c in range(2)])
    spread = []
    for i in range(2):
        steps = []
        for c in range(2):
            for a, b in grid:
                target = (a + b + 2 * c + i) % N * N + a
                steps.append((c * N * N + a * N + b, c * N * N + target))
        spread.append(lax.ppermute(kv, ("core", "ri", "rj"), steps))
    bias = lax.dynamic_index_in_dim(pair_bias.reshape(N, 2, ROWS, ROWS), core, 1, False)
    bias = lax.all_to_all(bias, "rj", 0, 0, tiled=True)
    given = swap(pick(q, g, o, *spread), "core", [(0, 1)])

    total, dq, dkv = attention(q, g, o, *spread, given, bias)

    def spread_out(parts, axis):
        return [parts[0]] + [
            lax.ppermute(parts[t], axis, [(a, (a + t) % N) for a in range(N)])
            for t in range(1, N)
        ]

    spread = lax.all_to_all(total, ("x", "rj"), 0, 0, tiled=True)
    total = jnp.sum(spread.reshape(N, N, 64, ROWS).astype(F32), axis=0).astype(BF)
    other = swap(total, "zh", [(0, 1), (2, 3)])
    parts = spread_out(hand_on(split_kernel, total, dkv), "rj")
    total = add(total, other)
    other = swap(total, "zh", [(1, 2), (3, 0)])
    parts = spread_out(hand_on(choose_kernel, total, *parts), "ri")
    total = add(total, other)
    mine = lax.all_gather(total, "x", axis=0, tiled=True).reshape(-1, ROWS)

    dkv = sum(x.astype(F32) for x in parts).astype(BF)
    grads = jnp.concatenate([dkv, dq], axis=1)
    own, others = grads[: SEQS // 2], grads[SEQS // 2 :]
    theirs = swap(jnp.concatenate([mine, others.reshape(-1, ROWS)]), "core", [(0, 1)])
    bias_grad, dk, dv, dq = finish(theirs, own, place(mine))
    return *(jnp.swapaxes(x, 1, 2) for x in (dq, dk, dv)), bias_grad


def solution(mesh):
    split = Mesh(mesh.devices.reshape(N, N, 2, N, N), ("zh", "x", "core", "ri", "rj"))
    seq = ("zh", "x", "core")
    rows, keys, tile = P(seq, "ri", "rj"), P(seq, "rj", "ri"), P(None, "ri", "rj")
    return jax.shard_map(
        body,
        mesh=split,
        in_specs=(rows, keys, keys, tile, rows, rows),
        out_specs=(rows, keys, keys, tile),
        check_vma=False,
    )
```

```python
import jax
import jax.numpy as jnp
from jax import lax
from jax.experimental import pallas as pl
from jax.experimental.pallas import tpu as pltpu
from jax.sharding import Mesh
from jax.sharding import PartitionSpec as P

HEAD = 32
SCALE = HEAD**-0.5
N = 4
ROWS = 256
KEYS = N * ROWS
LANES = 128
SEQS = 4
CHUNK = 32
UNROLL = 8
BF = jnp.bfloat16
F32 = jnp.float32
NT = (((1,), (1,)), ((), ()))
NN = (((1,), (0,)), ((), ()))


def pick_kernel(q_ref, g_ref, o_ref, first, second, send):
    other = 1 - lax.axis_index("core")
    at = 0
    half = pl.ds(pl.multiple_of(other * HEAD, HEAD), HEAD)
    for x_ref in (q_ref, g_ref, o_ref):
        for s in range(SEQS // 2):
            send[at : at + HEAD, :] = x_ref[s, half, :]
            at += HEAD
    for x_ref in (first, second):
        for s in range(SEQS):
            for part in range(2):
                half = pl.ds(pl.multiple_of((2 * part + other) * HEAD, HEAD), HEAD)
                send[at : at + HEAD, :] = x_ref[s, half, :]
                at += HEAD


def pick(*args):
    vmem = pl.BlockSpec(memory_space=pltpu.VMEM)
    rows = (3 * (SEQS // 2) + 2 * SEQS * 2) * HEAD
    return pl.pallas_call(
        pick_kernel,
        out_shape=jax.ShapeDtypeStruct((rows, ROWS), BF),
        in_specs=[vmem] * 5,
        out_specs=vmem,
        compiler_params=pltpu.CompilerParams(vmem_limit_bytes=8 * 2**20),
        cost_estimate=pl.CostEstimate(flops=0, bytes_accessed=2**20, transcendentals=0),
    )(*args)


def attention_kernel(
    q_ref, g_ref, o_ref, first, second, given, bias,
    bias_grad, dq_ref, dkv_ref,
    stack, wide, raw, low, inner,
):
    ri, rj, core = (lax.axis_index(a) for a in ("ri", "rj", "core"))
    own = pl.ds(pl.multiple_of(core * HEAD, HEAD), HEAD)
    rounds = [2 * core, 2 * core + 1, 2 - 2 * core, 3 - 2 * core]
    blocks = [lax.rem(ri + 2 * N - rj - t, N) for t in rounds]

    def query_side(i, s):
        if s < SEQS // 2:
            return (q_ref, g_ref, o_ref)[i][s, own, :]
        at = (i * (SEQS // 2) + s - SEQS // 2) * HEAD
        return given[at : at + HEAD, :]

    def key_side(part, t, s):
        if t < 2:
            half = pl.ds(pl.multiple_of((2 * part + core) * HEAD, HEAD), HEAD)
            return (first, second)[t][s, half, :]
        there = (s + SEQS // 2) % SEQS
        at = (3 * (SEQS // 2) + ((t - 2) * SEQS + there) * 2 + part) * HEAD
        return given[at : at + HEAD, :]

    channel = lax.broadcasted_iota(jnp.int32, (2 * HEAD, ROWS), 0) // HEAD

    for s in range(SEQS):
        for part in range(2):
            at = slice(part * ROWS, (part + 1) * ROWS)
            one = jnp.where(channel == part, jnp.concatenate([query_side(0, s), query_side(1, s)]), 0)
            wide[s, :, at] = one
            stack[s, at, :] = one.T
        dots = query_side(1, s).astype(F32) * query_side(2, s).astype(F32)
        sums = jnp.sum(dots, axis=0, keepdims=True)
        inner[s] = jnp.broadcast_to(sums, (LANES, ROWS)).T

    for s in range(SEQS):
        for t in range(N):
            at = slice(t * ROWS, (t + 1) * ROWS)
            kv = jnp.concatenate([key_side(0, t, s), key_side(1, t, s)])
            raw[s, :, at] = lax.dot_general(stack[s], kv, NN, preferred_element_type=F32)

    @pl.loop(0, ROWS // CHUNK, unroll=UNROLL)
    def _(i):
        r0 = pl.multiple_of(i * CHUNK, CHUNK)
        at_logits = pl.ds(r0, CHUNK)
        at_grads = pl.ds(pl.multiple_of(ROWS + r0, CHUNK), CHUNK)
        pair = jnp.concatenate([bias[b, at_logits, :] for b in blocks], axis=1).astype(F32)
        total = None
        for s in range(SEQS):
            logits = raw[s, at_logits, :] * SCALE + pair
            top = jnp.max(logits, axis=1, keepdims=True)
            weights = jnp.exp(logits - top)
            weights = weights * (1.0 / jnp.sum(weights, axis=1, keepdims=True))
            dots = jnp.concatenate([inner[s, at_logits, :]] * (KEYS // LANES), axis=1)
            grad = weights * (raw[s, at_grads, :] - dots)
            low[s, at_logits, :] = grad.astype(BF)
            low[s, at_grads, :] = weights.astype(BF)
            total = grad if total is None else total + grad
        total = total.astype(BF)
        quarter = i // (64 // CHUNK)
        within = pl.ds(pl.multiple_of(lax.rem(i, 64 // CHUNK) * CHUNK, CHUNK), CHUNK)
        for t, b in enumerate(blocks):
            bias_grad[quarter * N + b, within, :] = total[:, t * ROWS : (t + 1) * ROWS]

    for s in range(SEQS):
        query_grads = None
        for t, b in enumerate(blocks):
            at = slice(t * ROWS, (t + 1) * ROWS)
            grads = lax.dot_general(wide[s], low[s, :, at], NN, preferred_element_type=F32)
            grads = jnp.where(channel == 0, grads * SCALE, grads)
            dkv_ref[lax.rem(b + N - rj, N), s] = grads.astype(BF)
            key = key_side(0, t, s)
            term = lax.dot_general(low[s, :ROWS, at], key, NT, preferred_element_type=F32)
            query_grads = term if query_grads is None else query_grads + term
        dq_ref[s] = (query_grads.T * SCALE).astype(BF)


def attention(*args):
    vmem = pl.BlockSpec(memory_space=pltpu.VMEM)
    return pl.pallas_call(
        attention_kernel,
        out_shape=(
            jax.ShapeDtypeStruct((N * N, 64, ROWS), BF),
            jax.ShapeDtypeStruct((SEQS, HEAD, ROWS), BF),
            jax.ShapeDtypeStruct((N, SEQS, 2 * HEAD, ROWS), BF),
        ),
        in_specs=[vmem] * 7,
        out_specs=(vmem,) * 3,
        scratch_shapes=[
            pltpu.VMEM((SEQS, 2 * ROWS, 2 * HEAD), BF),
            pltpu.VMEM((SEQS, 2 * HEAD, 2 * ROWS), BF),
            pltpu.VMEM((SEQS, 2 * ROWS, KEYS), F32),
            pltpu.VMEM((SEQS, 2 * ROWS, KEYS), BF),
            pltpu.VMEM((SEQS, ROWS, LANES), F32),
        ],
        compiler_params=pltpu.CompilerParams(vmem_limit_bytes=32 * 2**20),
        cost_estimate=pl.CostEstimate(
            flops=5 * 2 * 2**25, bytes_accessed=6 * 2**20, transcendentals=2**20
        ),
    )(*args)


def split_kernel(after, x_ref, *outs):
    for t, out in enumerate(outs):
        out[...] = x_ref[t]


def choose_kernel(after, *refs):
    ri, rj = lax.axis_index("ri"), lax.axis_index("rj")
    for t, out in enumerate(refs[N:]):
        wanted = lax.rem(rj + 2 * N - ri - t, N)
        for source, x_ref in enumerate(refs[:N]):

            @pl.when(wanted == source)
            def _():
                out[...] = x_ref[...]


def hand_on(kernel, after, *args):
    anywhere, vmem = pl.BlockSpec(memory_space=pl.ANY), pl.BlockSpec(memory_space=pltpu.VMEM)
    return pl.pallas_call(
        kernel,
        out_shape=[jax.ShapeDtypeStruct(args[0].shape[-3:], BF)] * N,
        in_specs=[anywhere] + [vmem] * len(args),
        out_specs=[vmem] * N,
        compiler_params=pltpu.CompilerParams(vmem_limit_bytes=8 * 2**20),
        cost_estimate=pl.CostEstimate(flops=0, bytes_accessed=2**21, transcendentals=0),
    )(after, *args)


def place_heads(x_ref, out_ref, wide, sem, head):
    copies = []
    for j in range(N):
        for x in range(N):
            at = (x * N + j) * 64
            wide[j, x * 64 : (x + 1) * 64, :] = x_ref[at : at + 64, :].astype(F32)
        copies.append(pltpu.make_async_copy(wide.at[j], out_ref.at[2 * j + head], sem.at[j]))
        copies[-1].start()
    return copies


def place_kernel(x_ref, out_ref, wide, sem):
    for c in place_heads(x_ref, out_ref, wide, sem, lax.axis_index("core")):
        c.wait()


def finish_kernel(x_ref, own_ref, before, out_ref, dk_ref, dv_ref, dq_ref, wide, both, sem):
    core = lax.axis_index("core")
    copies = place_heads(x_ref, out_ref, wide, sem, 1 - core)
    mine = pl.ds(pl.multiple_of(core * HEAD, HEAD), HEAD)
    theirs = pl.ds(pl.multiple_of((1 - core) * HEAD, HEAD), HEAD)
    for i, grad_ref in enumerate((dk_ref, dv_ref, dq_ref)):
        for s in range(SEQS // 2):
            at = N * ROWS + (s * 3 + i) * HEAD
            both[i, s, mine, :] = own_ref[s, i * HEAD : (i + 1) * HEAD, :]
            both[i, s, theirs, :] = x_ref[at : at + HEAD, :]
        copies.append(pltpu.make_async_copy(both.at[i], grad_ref, sem.at[N + i]))
        copies[-1].start()
    for c in copies:
        c.wait()


def place(x):
    anywhere, vmem = pl.BlockSpec(memory_space=pl.ANY), pl.BlockSpec(memory_space=pltpu.VMEM)
    return pl.pallas_call(
        place_kernel,
        out_shape=jax.ShapeDtypeStruct((2 * N, ROWS, ROWS), F32),
        in_specs=[vmem],
        out_specs=anywhere,
        scratch_shapes=[pltpu.VMEM((N, ROWS, ROWS), F32), pltpu.SemaphoreType.DMA((N,))],
        compiler_params=pltpu.CompilerParams(vmem_limit_bytes=8 * 2**20),
        cost_estimate=pl.CostEstimate(flops=2**18, bytes_accessed=3 * 2**19, transcendentals=0),
    )(x)


def finish(x, own, before):
    anywhere, vmem = pl.BlockSpec(memory_space=pl.ANY), pl.BlockSpec(memory_space=pltpu.VMEM)
    grad = jax.ShapeDtypeStruct((SEQS // 2, 2 * HEAD, ROWS), BF)
    return pl.pallas_call(
        finish_kernel,
        out_shape=(jax.ShapeDtypeStruct(before.shape, F32), grad, grad, grad),
        in_specs=[vmem, vmem, anywhere],
        out_specs=(anywhere,) * 4,
        scratch_shapes=[
            pltpu.VMEM((N, ROWS, ROWS), F32),
            pltpu.VMEM((3, *grad.shape), BF),
            pltpu.SemaphoreType.DMA((N + 3,)),
        ],
        input_output_aliases={2: 0},
        compiler_params=pltpu.CompilerParams(vmem_limit_bytes=8 * 2**20),
        cost_estimate=pl.CostEstimate(flops=2**18, bytes_accessed=2**21, transcendentals=0),
    )(x, own, before)


def swap(x, axis, pairs):
    return lax.ppermute(x, axis, [(a, b) for a, b in pairs] + [(b, a) for a, b in pairs])


def add(a, b):
    return (a.astype(F32) + b.astype(F32)).astype(BF)


def body(query_proj, key_proj, value_proj, pair_bias, attn_output, output_grad):
    q, k, v, o, g = (
        jnp.swapaxes(x, 1, 2)
        for x in (query_proj, key_proj, value_proj, attn_output, output_grad)
    )
    grid = [(a, b) for a in range(N) for b in range(N)]

    core = lax.axis_index("core")
    held = jnp.concatenate([k, v], axis=1)
    bias = lax.dynamic_index_in_dim(pair_bias.reshape(N, 2, ROWS, ROWS), core, 1, False)
    theirs, bias = lax.optimization_barrier((swap(held, "core", [(0, 1)]), bias))
    kv = jnp.concatenate([held, theirs])
    spread = []
    for i in range(2):
        steps = []
        for c in range(2):
            for a, b in grid:
                target = (a + b + 2 * c + i) % N * N + a
                steps.append((c * N * N + a * N + b, c * N * N + target))
        spread.append(lax.ppermute(kv, ("core", "ri", "rj"), steps))
    bias = lax.all_to_all(bias, "rj", 0, 0, tiled=True)
    given = swap(pick(q, g, o, *spread), "core", [(0, 1)])

    total, dq, dkv = attention(q, g, o, *spread, given, bias)

    def spread_out(parts, axis):
        return [parts[0]] + [
            lax.ppermute(parts[t], axis, [(a, (a + t) % N) for a in range(N)])
            for t in range(1, N)
        ]

    spread = lax.all_to_all(total, ("x", "rj"), 0, 0, tiled=True)
    total = jnp.sum(spread.reshape(N, N, 64, ROWS).astype(F32), axis=0).astype(BF)
    other = swap(total, "zh", [(0, 1), (2, 3)])
    parts = spread_out(hand_on(split_kernel, total, dkv), "rj")
    total = add(total, other)
    other = swap(total, "zh", [(1, 2), (3, 0)])
    parts = spread_out(hand_on(choose_kernel, total, *parts), "ri")
    total = add(total, other)
    mine = lax.all_gather(total, "x", axis=0, tiled=True).reshape(-1, ROWS)

    dkv = sum(x.astype(F32) for x in parts).astype(BF)
    grads = jnp.concatenate([dkv, dq], axis=1)
    own, others = grads[: SEQS // 2], grads[SEQS // 2 :]
    theirs = swap(jnp.concatenate([mine, others.reshape(-1, ROWS)]), "core", [(0, 1)])
    bias_grad, dk, dv, dq = finish(theirs, own, place(mine))
    return *(jnp.swapaxes(x, 1, 2) for x in (dq, dk, dv)), bias_grad


def solution(mesh):
    split = Mesh(mesh.devices.reshape(N, N, 2, N, N), ("zh", "x", "core", "ri", "rj"))
    seq = ("zh", "x", "core")
    rows, keys, tile = P(seq, "ri", "rj"), P(seq, "rj", "ri"), P(None, "ri", "rj")
    return jax.shard_map(
        body,
        mesh=split,
        in_specs=(rows, keys, keys, tile, rows, rows),
        out_specs=(rows, keys, keys, tile),
        check_vma=False,
    )
```

```python
import jax
import jax.numpy as jnp
from jax import lax
from jax.experimental import pallas as pl
from jax.experimental.pallas import tpu as pltpu
from jax.sharding import Mesh
from jax.sharding import PartitionSpec as P

HEAD = 32
SCALE = HEAD**-0.5
N = 4
ROWS = 256
KEYS = N * ROWS
LANES = 128
SEQS = 4
CHUNK = 32
UNROLL = 8
BF = jnp.bfloat16
F32 = jnp.float32
NT = (((1,), (1,)), ((), ()))
NN = (((1,), (0,)), ((), ()))


def pick_kernel(q_ref, g_ref, o_ref, first, second, bias, send):
    other = 1 - lax.axis_index("core")
    at = 0
    half = pl.ds(pl.multiple_of(other * HEAD, HEAD), HEAD)
    for x_ref in (q_ref, g_ref, o_ref):
        for s in range(SEQS // 2):
            send[at : at + HEAD, :] = x_ref[s, half, :]
            at += HEAD
    for x_ref in (first, second):
        for s in range(SEQS):
            for part in range(2):
                half = pl.ds(pl.multiple_of((2 * part + other) * HEAD, HEAD), HEAD)
                send[at : at + HEAD, :] = x_ref[s, half, :]
                at += HEAD
    send[at : at + ROWS, :] = bias[other]


def pick(*args):
    vmem = pl.BlockSpec(memory_space=pltpu.VMEM)
    rows = (3 * (SEQS // 2) + 2 * SEQS * 2) * HEAD + ROWS
    return pl.pallas_call(
        pick_kernel,
        out_shape=jax.ShapeDtypeStruct((rows, ROWS), BF),
        in_specs=[vmem] * 6,
        out_specs=vmem,
        compiler_params=pltpu.CompilerParams(vmem_limit_bytes=8 * 2**20),
        cost_estimate=pl.CostEstimate(flops=0, bytes_accessed=2**20, transcendentals=0),
    )(*args)


def attention_kernel(
    q_ref, g_ref, o_ref, first, second, given, bias_own, bias_near, bias_far,
    bias_grad, dq_ref, dkv_ref,
    stack, wide, raw, low, inner, bias,
):
    ri, rj, core = (lax.axis_index(a) for a in ("ri", "rj", "core"))
    own = pl.ds(pl.multiple_of(core * HEAD, HEAD), HEAD)
    rounds = [2 * core, 2 * core + 1, 2 - 2 * core, 3 - 2 * core]
    blocks = [lax.rem(ri + 2 * N - rj - t, N) for t in rounds]

    def query_side(i, s):
        if s < SEQS // 2:
            return (q_ref, g_ref, o_ref)[i][s, own, :]
        at = (i * (SEQS // 2) + s - SEQS // 2) * HEAD
        return given[at : at + HEAD, :]

    def key_side(part, t, s):
        if t < 2:
            half = pl.ds(pl.multiple_of((2 * part + core) * HEAD, HEAD), HEAD)
            return (first, second)[t][s, half, :]
        there = (s + SEQS // 2) % SEQS
        at = (3 * (SEQS // 2) + ((t - 2) * SEQS + there) * 2 + part) * HEAD
        return given[at : at + HEAD, :]

    channel = lax.broadcasted_iota(jnp.int32, (2 * HEAD, ROWS), 0) // HEAD

    bias[rj] = bias_own[...]
    bias[lax.rem(rj + N - 1 - 2 * core, N)] = bias_near[core]
    bias[lax.rem(rj + 1 + 2 * core, N)] = given[given.shape[0] - ROWS :, :]
    bias[lax.rem(rj + 2, N)] = bias_far[...]

    for s in range(SEQS):
        for part in range(2):
            at = slice(part * ROWS, (part + 1) * ROWS)
            one = jnp.where(channel == part, jnp.concatenate([query_side(0, s), query_side(1, s)]), 0)
            wide[s, :, at] = one
            stack[s, at, :] = one.T
        dots = query_side(1, s).astype(F32) * query_side(2, s).astype(F32)
        sums = jnp.sum(dots, axis=0, keepdims=True)
        inner[s] = jnp.broadcast_to(sums, (LANES, ROWS)).T

    for s in range(SEQS):
        for t in range(N):
            at = slice(t * ROWS, (t + 1) * ROWS)
            kv = jnp.concatenate([key_side(0, t, s), key_side(1, t, s)])
            raw[s, :, at] = lax.dot_general(stack[s], kv, NN, preferred_element_type=F32)

    @pl.loop(0, ROWS // CHUNK, unroll=UNROLL)
    def _(i):
        r0 = pl.multiple_of(i * CHUNK, CHUNK)
        at_logits = pl.ds(r0, CHUNK)
        at_grads = pl.ds(pl.multiple_of(ROWS + r0, CHUNK), CHUNK)
        pair = jnp.concatenate([bias[b, at_logits, :] for b in blocks], axis=1).astype(F32)
        total = None
        for s in range(SEQS):
            logits = raw[s, at_logits, :] * SCALE + pair
            top = jnp.max(logits, axis=1, keepdims=True)
            weights = jnp.exp(logits - top)
            weights = weights * (1.0 / jnp.sum(weights, axis=1, keepdims=True))
            dots = jnp.concatenate([inner[s, at_logits, :]] * (KEYS // LANES), axis=1)
            grad = weights * (raw[s, at_grads, :] - dots)
            low[s, at_logits, :] = grad.astype(BF)
            low[s, at_grads, :] = weights.astype(BF)
            total = grad if total is None else total + grad
        total = total.astype(BF)
        quarter = i // (64 // CHUNK)
        within = pl.ds(pl.multiple_of(lax.rem(i, 64 // CHUNK) * CHUNK, CHUNK), CHUNK)
        for t, b in enumerate(blocks):
            bias_grad[quarter * N + b, within, :] = total[:, t * ROWS : (t + 1) * ROWS]

    for s in range(SEQS):
        query_grads = None
        for t, b in enumerate(blocks):
            at = slice(t * ROWS, (t + 1) * ROWS)
            grads = lax.dot_general(wide[s], low[s, :, at], NN, preferred_element_type=F32)
            grads = jnp.where(channel == 0, grads * SCALE, grads)
            dkv_ref[lax.rem(b + N - rj, N), s] = grads.astype(BF)
            key = key_side(0, t, s)
            term = lax.dot_general(low[s, :ROWS, at], key, NT, preferred_element_type=F32)
            query_grads = term if query_grads is None else query_grads + term
        dq_ref[s] = (query_grads.T * SCALE).astype(BF)


def attention(*args):
    vmem = pl.BlockSpec(memory_space=pltpu.VMEM)
    return pl.pallas_call(
        attention_kernel,
        out_shape=(
            jax.ShapeDtypeStruct((N * N, 64, ROWS), BF),
            jax.ShapeDtypeStruct((SEQS, HEAD, ROWS), BF),
            jax.ShapeDtypeStruct((N, SEQS, 2 * HEAD, ROWS), BF),
        ),
        in_specs=[vmem] * 9,
        out_specs=(vmem,) * 3,
        scratch_shapes=[
            pltpu.VMEM((SEQS, 2 * ROWS, 2 * HEAD), BF),
            pltpu.VMEM((SEQS, 2 * HEAD, 2 * ROWS), BF),
            pltpu.VMEM((SEQS, 2 * ROWS, KEYS), F32),
            pltpu.VMEM((SEQS, 2 * ROWS, KEYS), BF),
            pltpu.VMEM((SEQS, ROWS, LANES), F32),
            pltpu.VMEM((N, ROWS, ROWS), BF),
        ],
        compiler_params=pltpu.CompilerParams(vmem_limit_bytes=32 * 2**20),
        cost_estimate=pl.CostEstimate(
            flops=5 * 2 * 2**25, bytes_accessed=6 * 2**20, transcendentals=2**20
        ),
    )(*args)


def split_kernel(after, x_ref, *outs):
    for t, out in enumerate(outs):
        out[...] = x_ref[t]


def choose_kernel(after, *refs):
    ri, rj = lax.axis_index("ri"), lax.axis_index("rj")
    for t, out in enumerate(refs[N:]):
        wanted = lax.rem(rj + 2 * N - ri - t, N)
        for source, x_ref in enumerate(refs[:N]):

            @pl.when(wanted == source)
            def _():
                out[...] = x_ref[...]


def hand_on(kernel, after, *args):
    anywhere, vmem = pl.BlockSpec(memory_space=pl.ANY), pl.BlockSpec(memory_space=pltpu.VMEM)
    return pl.pallas_call(
        kernel,
        out_shape=[jax.ShapeDtypeStruct(args[0].shape[-3:], BF)] * N,
        in_specs=[anywhere] + [vmem] * len(args),
        out_specs=[vmem] * N,
        compiler_params=pltpu.CompilerParams(vmem_limit_bytes=8 * 2**20),
        cost_estimate=pl.CostEstimate(flops=0, bytes_accessed=2**21, transcendentals=0),
    )(after, *args)


def place_heads(x_ref, out_ref, wide, sem, head):
    copies = []
    for j in range(N):
        for x in range(N):
            at = (x * N + j) * 64
            wide[j, x * 64 : (x + 1) * 64, :] = x_ref[at : at + 64, :].astype(F32)
        copies.append(pltpu.make_async_copy(wide.at[j], out_ref.at[2 * j + head], sem.at[j]))
        copies[-1].start()
    return copies


def place_kernel(x_ref, out_ref, wide, sem):
    for c in place_heads(x_ref, out_ref, wide, sem, lax.axis_index("core")):
        c.wait()


def finish_kernel(x_ref, own_ref, before, out_ref, dk_ref, dv_ref, dq_ref, wide, both, sem):
    core = lax.axis_index("core")
    copies = place_heads(x_ref, out_ref, wide, sem, 1 - core)
    mine = pl.ds(pl.multiple_of(core * HEAD, HEAD), HEAD)
    theirs = pl.ds(pl.multiple_of((1 - core) * HEAD, HEAD), HEAD)
    for i, grad_ref in enumerate((dk_ref, dv_ref, dq_ref)):
        for s in range(SEQS // 2):
            at = N * ROWS + (s * 3 + i) * HEAD
            both[i, s, mine, :] = own_ref[s, i * HEAD : (i + 1) * HEAD, :]
            both[i, s, theirs, :] = x_ref[at : at + HEAD, :]
        copies.append(pltpu.make_async_copy(both.at[i], grad_ref, sem.at[N + i]))
        copies[-1].start()
    for c in copies:
        c.wait()


def place(x):
    anywhere, vmem = pl.BlockSpec(memory_space=pl.ANY), pl.BlockSpec(memory_space=pltpu.VMEM)
    return pl.pallas_call(
        place_kernel,
        out_shape=jax.ShapeDtypeStruct((2 * N, ROWS, ROWS), F32),
        in_specs=[vmem],
        out_specs=anywhere,
        scratch_shapes=[pltpu.VMEM((N, ROWS, ROWS), F32), pltpu.SemaphoreType.DMA((N,))],
        compiler_params=pltpu.CompilerParams(vmem_limit_bytes=8 * 2**20),
        cost_estimate=pl.CostEstimate(flops=2**18, bytes_accessed=3 * 2**19, transcendentals=0),
    )(x)


def finish(x, own, before):
    anywhere, vmem = pl.BlockSpec(memory_space=pl.ANY), pl.BlockSpec(memory_space=pltpu.VMEM)
    grad = jax.ShapeDtypeStruct((SEQS // 2, 2 * HEAD, ROWS), BF)
    return pl.pallas_call(
        finish_kernel,
        out_shape=(jax.ShapeDtypeStruct(before.shape, F32), grad, grad, grad),
        in_specs=[vmem, vmem, anywhere],
        out_specs=(anywhere,) * 4,
        scratch_shapes=[
            pltpu.VMEM((N, ROWS, ROWS), F32),
            pltpu.VMEM((3, *grad.shape), BF),
            pltpu.SemaphoreType.DMA((N + 3,)),
        ],
        input_output_aliases={2: 0},
        compiler_params=pltpu.CompilerParams(vmem_limit_bytes=8 * 2**20),
        cost_estimate=pl.CostEstimate(flops=2**18, bytes_accessed=2**21, transcendentals=0),
    )(x, own, before)


def swap(x, axis, pairs):
    return lax.ppermute(x, axis, [(a, b) for a, b in pairs] + [(b, a) for a, b in pairs])


def add(a, b):
    return (a.astype(F32) + b.astype(F32)).astype(BF)


def body(query_proj, key_proj, value_proj, pair_bias, attn_output, output_grad):
    q, k, v, o, g = (
        jnp.swapaxes(x, 1, 2)
        for x in (query_proj, key_proj, value_proj, attn_output, output_grad)
    )
    grid = [(a, b) for a in range(N) for b in range(N)]

    core = lax.axis_index("core")
    held = jnp.concatenate([k, v], axis=1)
    rj = lax.axis_index("rj")
    heads = pair_bias.reshape(N, 2, ROWS, ROWS)
    near = lax.dynamic_index_in_dim(heads, lax.rem(rj + 1 + 2 * core, N), 0, False)
    far = lax.dynamic_index_in_dim(pair_bias, 2 * lax.rem(rj + 2, N) + core, 0, False)
    bias_own = lax.dynamic_index_in_dim(pair_bias, 2 * rj + core, 0, False)
    theirs, near, far, bias_own = lax.optimization_barrier(
        (swap(held, "core", [(0, 1)]), near, far, bias_own)
    )
    kv = jnp.concatenate([held, theirs])
    spread = []
    for i in range(2):
        steps = []
        for c in range(2):
            for a, b in grid:
                target = (a + b + 2 * c + i) % N * N + a
                steps.append((c * N * N + a * N + b, c * N * N + target))
        spread.append(lax.ppermute(kv, ("core", "ri", "rj"), steps))
    steps = [(c * N + a, c * N + (a + 1 + 2 * c) % N) for c in range(2) for a in range(N)]
    near = lax.ppermute(near, ("core", "rj"), steps)
    far = lax.ppermute(far, "rj", [(a, (a + 2) % N) for a in range(N)])
    near, far, *spread = lax.optimization_barrier((near, far, *spread))
    given = swap(pick(q, g, o, *spread, near), "core", [(0, 1)])

    total, dq, dkv = attention(q, g, o, *spread, given, bias_own, near, far)

    def spread_out(parts, axis):
        return [parts[0]] + [
            lax.ppermute(parts[t], axis, [(a, (a + t) % N) for a in range(N)])
            for t in range(1, N)
        ]

    spread = lax.all_to_all(total, ("x", "rj"), 0, 0, tiled=True)
    total = jnp.sum(spread.reshape(N, N, 64, ROWS).astype(F32), axis=0).astype(BF)
    other = swap(total, "zh", [(0, 1), (2, 3)])
    parts = spread_out(hand_on(split_kernel, total, dkv), "rj")
    total = add(total, other)
    other = swap(total, "zh", [(1, 2), (3, 0)])
    parts = spread_out(hand_on(choose_kernel, total, *parts), "ri")
    total = add(total, other)
    mine = lax.all_gather(total, "x", axis=0, tiled=True).reshape(-1, ROWS)

    dkv = sum(x.astype(F32) for x in parts).astype(BF)
    grads = jnp.concatenate([dkv, dq], axis=1)
    own, others = grads[: SEQS // 2], grads[SEQS // 2 :]
    theirs = swap(jnp.concatenate([mine, others.reshape(-1, ROWS)]), "core", [(0, 1)])
    bias_grad, dk, dv, dq = finish(theirs, own, place(mine))
    return *(jnp.swapaxes(x, 1, 2) for x in (dq, dk, dv)), bias_grad


def solution(mesh):
    split = Mesh(mesh.devices.reshape(N, N, 2, N, N), ("zh", "x", "core", "ri", "rj"))
    seq = ("zh", "x", "core")
    rows, keys, tile = P(seq, "ri", "rj"), P(seq, "rj", "ri"), P(None, "ri", "rj")
    return jax.shard_map(
        body,
        mesh=split,
        in_specs=(rows, keys, keys, tile, rows, rows),
        out_specs=(rows, keys, keys, tile),
        check_vma=False,
    )
```

```python
import jax
import jax.numpy as jnp
from jax import lax
from jax.experimental import pallas as pl
from jax.experimental.pallas import tpu as pltpu
from jax.sharding import Mesh
from jax.sharding import PartitionSpec as P

HEAD = 32
SCALE = HEAD**-0.5
N = 4
ROWS = 256
KEYS = N * ROWS
LANES = 128
SEQS = 4
CHUNK = 32
UNROLL = 8
BF = jnp.bfloat16
F32 = jnp.float32
NT = (((1,), (1,)), ((), ()))
NN = (((1,), (0,)), ((), ()))


def pick_kernel(q_ref, g_ref, o_ref, first, second, send):
    other = 1 - lax.axis_index("core")
    at = 0
    half = pl.ds(pl.multiple_of(other * HEAD, HEAD), HEAD)
    for x_ref in (q_ref, g_ref, o_ref):
        for s in range(SEQS // 2):
            send[at : at + HEAD, :] = x_ref[s, half, :]
            at += HEAD
    for x_ref in (first, second):
        for s in range(SEQS):
            for part in range(2):
                half = pl.ds(pl.multiple_of((2 * part + other) * HEAD, HEAD), HEAD)
                send[at : at + HEAD, :] = x_ref[s, half, :]
                at += HEAD


def pick(*args):
    vmem = pl.BlockSpec(memory_space=pltpu.VMEM)
    rows = (3 * (SEQS // 2) + 2 * SEQS * 2) * HEAD
    return pl.pallas_call(
        pick_kernel,
        out_shape=jax.ShapeDtypeStruct((rows, ROWS), BF),
        in_specs=[vmem] * 5,
        out_specs=vmem,
        compiler_params=pltpu.CompilerParams(vmem_limit_bytes=8 * 2**20),
        cost_estimate=pl.CostEstimate(flops=0, bytes_accessed=2**20, transcendentals=0),
    )(*args)


def attention_kernel(
    q_ref, g_ref, o_ref, first, second, given, bias,
    bias_grad, dq_ref, dkv_ref,
    stack, wide, raw, low, inner,
):
    ri, rj, core = (lax.axis_index(a) for a in ("ri", "rj", "core"))
    own = pl.ds(pl.multiple_of(core * HEAD, HEAD), HEAD)
    rounds = [2 * core, 2 * core + 1, 2 - 2 * core, 3 - 2 * core]
    blocks = [lax.rem(ri + 2 * N - rj - t, N) for t in rounds]

    def query_side(i, s):
        if s < SEQS // 2:
            return (q_ref, g_ref, o_ref)[i][s, own, :]
        at = (i * (SEQS // 2) + s - SEQS // 2) * HEAD
        return given[at : at + HEAD, :]

    def key_side(part, t, s):
        if t < 2:
            half = pl.ds(pl.multiple_of((2 * part + core) * HEAD, HEAD), HEAD)
            return (first, second)[t][s, half, :]
        there = (s + SEQS // 2) % SEQS
        at = (3 * (SEQS // 2) + ((t - 2) * SEQS + there) * 2 + part) * HEAD
        return given[at : at + HEAD, :]

    channel = lax.broadcasted_iota(jnp.int32, (2 * HEAD, ROWS), 0) // HEAD

    for s in range(SEQS):
        for part in range(2):
            at = slice(part * ROWS, (part + 1) * ROWS)
            one = jnp.where(channel == part, jnp.concatenate([query_side(0, s), query_side(1, s)]), 0)
            wide[s, :, at] = one
            stack[s, at, :] = one.T
        dots = query_side(1, s).astype(F32) * query_side(2, s).astype(F32)
        sums = jnp.sum(dots, axis=0, keepdims=True)
        inner[s] = jnp.broadcast_to(sums, (LANES, ROWS)).T

    for s in range(SEQS):
        for t in range(N):
            at = slice(t * ROWS, (t + 1) * ROWS)
            kv = jnp.concatenate([key_side(0, t, s), key_side(1, t, s)])
            raw[s, :, at] = lax.dot_general(stack[s], kv, NN, preferred_element_type=F32)

    @pl.loop(0, ROWS // CHUNK, unroll=UNROLL)
    def _(i):
        r0 = pl.multiple_of(i * CHUNK, CHUNK)
        at_logits = pl.ds(r0, CHUNK)
        at_grads = pl.ds(pl.multiple_of(ROWS + r0, CHUNK), CHUNK)
        pair = jnp.concatenate([bias[b, at_logits, :] for b in blocks], axis=1).astype(F32)
        total = None
        for s in range(SEQS):
            logits = raw[s, at_logits, :] * SCALE + pair
            top = jnp.max(logits, axis=1, keepdims=True)
            weights = jnp.exp(logits - top)
            weights = weights * (1.0 / jnp.sum(weights, axis=1, keepdims=True))
            dots = jnp.concatenate([inner[s, at_logits, :]] * (KEYS // LANES), axis=1)
            grad = weights * (raw[s, at_grads, :] - dots)
            low[s, at_logits, :] = grad.astype(BF)
            low[s, at_grads, :] = weights.astype(BF)
            total = grad if total is None else total + grad
        total = total.astype(BF)
        quarter = i // (64 // CHUNK)
        within = pl.ds(pl.multiple_of(lax.rem(i, 64 // CHUNK) * CHUNK, CHUNK), CHUNK)
        for t, b in enumerate(blocks):
            bias_grad[quarter * N + b, within, :] = total[:, t * ROWS : (t + 1) * ROWS]

    for s in range(SEQS):
        query_grads = None
        for t, b in enumerate(blocks):
            at = slice(t * ROWS, (t + 1) * ROWS)
            grads = lax.dot_general(wide[s], low[s, :, at], NN, preferred_element_type=F32)
            grads = jnp.where(channel == 0, grads * SCALE, grads)
            dkv_ref[lax.rem(b + N - rj, N), s] = grads.astype(BF)
            key = key_side(0, t, s)
            term = lax.dot_general(low[s, :ROWS, at], key, NT, preferred_element_type=F32)
            query_grads = term if query_grads is None else query_grads + term
        dq_ref[s] = (query_grads.T * SCALE).astype(BF)


def attention(*args):
    vmem = pl.BlockSpec(memory_space=pltpu.VMEM)
    return pl.pallas_call(
        attention_kernel,
        out_shape=(
            jax.ShapeDtypeStruct((N * N, 64, ROWS), BF),
            jax.ShapeDtypeStruct((SEQS, HEAD, ROWS), BF),
            jax.ShapeDtypeStruct((N, SEQS, 2 * HEAD, ROWS), BF),
        ),
        in_specs=[vmem] * 7,
        out_specs=(vmem,) * 3,
        scratch_shapes=[
            pltpu.VMEM((SEQS, 2 * ROWS, 2 * HEAD), BF),
            pltpu.VMEM((SEQS, 2 * HEAD, 2 * ROWS), BF),
            pltpu.VMEM((SEQS, 2 * ROWS, KEYS), F32),
            pltpu.VMEM((SEQS, 2 * ROWS, KEYS), BF),
            pltpu.VMEM((SEQS, ROWS, LANES), F32),
        ],
        compiler_params=pltpu.CompilerParams(vmem_limit_bytes=32 * 2**20),
        cost_estimate=pl.CostEstimate(
            flops=5 * 2 * 2**25, bytes_accessed=6 * 2**20, transcendentals=2**20
        ),
    )(*args)


def split_kernel(after, x_ref, *outs):
    for t, out in enumerate(outs):
        out[...] = x_ref[t]


def choose_kernel(after, *refs):
    ri, rj = lax.axis_index("ri"), lax.axis_index("rj")
    for t, out in enumerate(refs[N:]):
        wanted = lax.rem(rj + 2 * N - ri - t, N)
        for source, x_ref in enumerate(refs[:N]):

            @pl.when(wanted == source)
            def _():
                out[...] = x_ref[...]


def hand_on(kernel, after, *args):
    anywhere, vmem = pl.BlockSpec(memory_space=pl.ANY), pl.BlockSpec(memory_space=pltpu.VMEM)
    return pl.pallas_call(
        kernel,
        out_shape=[jax.ShapeDtypeStruct(args[0].shape[-3:], BF)] * N,
        in_specs=[anywhere] + [vmem] * len(args),
        out_specs=[vmem] * N,
        compiler_params=pltpu.CompilerParams(vmem_limit_bytes=8 * 2**20),
        cost_estimate=pl.CostEstimate(flops=0, bytes_accessed=2**21, transcendentals=0),
    )(after, *args)


def place_heads(x_ref, out_ref, wide, sem, head):
    copies = []
    for j in range(N):
        for x in range(N):
            at = (x * N + j) * 64
            wide[j, x * 64 : (x + 1) * 64, :] = x_ref[at : at + 64, :].astype(F32)
        copies.append(pltpu.make_async_copy(wide.at[j], out_ref.at[2 * j + head], sem.at[j]))
        copies[-1].start()
    return copies


def place_kernel(x_ref, out_ref, wide, sem):
    for c in place_heads(x_ref, out_ref, wide, sem, lax.axis_index("core")):
        c.wait()


def finish_kernel(x_ref, own_ref, before, out_ref, dk_ref, dv_ref, dq_ref, wide, both, sem):
    core = lax.axis_index("core")
    copies = place_heads(x_ref, out_ref, wide, sem, 1 - core)
    mine = pl.ds(pl.multiple_of(core * HEAD, HEAD), HEAD)
    theirs = pl.ds(pl.multiple_of((1 - core) * HEAD, HEAD), HEAD)
    for i, grad_ref in enumerate((dk_ref, dv_ref, dq_ref)):
        for s in range(SEQS // 2):
            at = N * ROWS + (s * 3 + i) * HEAD
            both[i, s, mine, :] = own_ref[s, i * HEAD : (i + 1) * HEAD, :]
            both[i, s, theirs, :] = x_ref[at : at + HEAD, :]
        copies.append(pltpu.make_async_copy(both.at[i], grad_ref, sem.at[N + i]))
        copies[-1].start()
    for c in copies:
        c.wait()


def place(x):
    anywhere, vmem = pl.BlockSpec(memory_space=pl.ANY), pl.BlockSpec(memory_space=pltpu.VMEM)
    return pl.pallas_call(
        place_kernel,
        out_shape=jax.ShapeDtypeStruct((2 * N, ROWS, ROWS), F32),
        in_specs=[vmem],
        out_specs=anywhere,
        scratch_shapes=[pltpu.VMEM((N, ROWS, ROWS), F32), pltpu.SemaphoreType.DMA((N,))],
        compiler_params=pltpu.CompilerParams(vmem_limit_bytes=8 * 2**20),
        cost_estimate=pl.CostEstimate(flops=2**18, bytes_accessed=3 * 2**19, transcendentals=0),
    )(x)


def finish(x, own, before):
    anywhere, vmem = pl.BlockSpec(memory_space=pl.ANY), pl.BlockSpec(memory_space=pltpu.VMEM)
    grad = jax.ShapeDtypeStruct((SEQS // 2, 2 * HEAD, ROWS), BF)
    return pl.pallas_call(
        finish_kernel,
        out_shape=(jax.ShapeDtypeStruct(before.shape, F32), grad, grad, grad),
        in_specs=[vmem, vmem, anywhere],
        out_specs=(anywhere,) * 4,
        scratch_shapes=[
            pltpu.VMEM((N, ROWS, ROWS), F32),
            pltpu.VMEM((3, *grad.shape), BF),
            pltpu.SemaphoreType.DMA((N + 3,)),
        ],
        input_output_aliases={2: 0},
        compiler_params=pltpu.CompilerParams(vmem_limit_bytes=8 * 2**20),
        cost_estimate=pl.CostEstimate(flops=2**18, bytes_accessed=2**21, transcendentals=0),
    )(x, own, before)


def swap(x, axis, pairs):
    return lax.ppermute(x, axis, [(a, b) for a, b in pairs] + [(b, a) for a, b in pairs])


def add(a, b):
    return (a.astype(F32) + b.astype(F32)).astype(BF)


def beside_ring(x, step):
    pairs = []
    for core in range(2):
        for zh in range(N):
            up = (zh + step + core) % 2 == 0
            pairs.append((zh * 2 + core, (zh + (1 if up else -1)) % N * 2 + core))
    return lax.ppermute(x, ("zh", "core"), pairs)


def body(query_proj, key_proj, value_proj, pair_bias, attn_output, output_grad):
    q, k, v, o, g = (
        jnp.swapaxes(x, 1, 2)
        for x in (query_proj, key_proj, value_proj, attn_output, output_grad)
    )
    grid = [(a, b) for a in range(N) for b in range(N)]

    core = lax.axis_index("core")
    held = jnp.concatenate([k, v], axis=1)
    bias = lax.dynamic_index_in_dim(pair_bias.reshape(N, 2, ROWS, ROWS), core, 1, False)
    theirs, bias = lax.optimization_barrier((swap(held, "core", [(0, 1)]), bias))
    kv = jnp.concatenate([held, theirs])
    spread = []
    for i in range(2):
        steps = []
        for c in range(2):
            for a, b in grid:
                target = (a + b + 2 * c + i) % N * N + a
                steps.append((c * N * N + a * N + b, c * N * N + target))
        spread.append(lax.ppermute(kv, ("core", "ri", "rj"), steps))
    bias = lax.all_to_all(bias, "rj", 0, 0, tiled=True)
    given = swap(pick(q, g, o, *spread), "core", [(0, 1)])

    total, dq, dkv = attention(q, g, o, *spread, given, bias)

    def spread_out(parts, axis):
        return [parts[0]] + [
            lax.ppermute(parts[t], axis, [(a, (a + t) % N) for a in range(N)])
            for t in range(1, N)
        ]

    spread = lax.all_to_all(total, ("x", "rj"), 0, 0, tiled=True)
    total = jnp.sum(spread.reshape(N, N, 64, ROWS).astype(F32), axis=0).astype(BF)
    other = beside_ring(total, 0)
    parts = spread_out(hand_on(split_kernel, total, dkv), "rj")
    total = add(total, other)
    other = beside_ring(total, 1)
    parts = spread_out(hand_on(choose_kernel, total, *parts), "ri")
    total = add(total, other)
    mine = lax.all_gather(total, "x", axis=0, tiled=True).reshape(-1, ROWS)

    dkv = sum(x.astype(F32) for x in parts).astype(BF)
    grads = jnp.concatenate([dkv, dq], axis=1)
    own, others = grads[: SEQS // 2], grads[SEQS // 2 :]
    theirs = swap(jnp.concatenate([mine, others.reshape(-1, ROWS)]), "core", [(0, 1)])
    bias_grad, dk, dv, dq = finish(theirs, own, place(mine))
    return *(jnp.swapaxes(x, 1, 2) for x in (dq, dk, dv)), bias_grad


def solution(mesh):
    split = Mesh(mesh.devices.reshape(N, N, 2, N, N), ("zh", "x", "core", "ri", "rj"))
    seq = ("zh", "x", "core")
    rows, keys, tile = P(seq, "ri", "rj"), P(seq, "rj", "ri"), P(None, "ri", "rj")
    return jax.shard_map(
        body,
        mesh=split,
        in_specs=(rows, keys, keys, tile, rows, rows),
        out_specs=(rows, keys, keys, tile),
        check_vma=False,
    )
```

```python
import jax
import jax.numpy as jnp
from jax import lax
from jax.experimental import pallas as pl
from jax.experimental.pallas import tpu as pltpu
from jax.sharding import Mesh
from jax.sharding import PartitionSpec as P

HEAD = 32
SCALE = HEAD**-0.5
N = 4
ROWS = 256
KEYS = N * ROWS
LANES = 128
SEQS = 4
CHUNK = 32
UNROLL = 8
BF = jnp.bfloat16
F32 = jnp.float32
NT = (((1,), (1,)), ((), ()))
NN = (((1,), (0,)), ((), ()))


def pick_kernel(q_ref, g_ref, o_ref, first, second, send):
    other = 1 - lax.axis_index("core")
    at = 0
    half = pl.ds(pl.multiple_of(other * HEAD, HEAD), HEAD)
    for x_ref in (q_ref, g_ref, o_ref):
        for s in range(SEQS // 2):
            send[at : at + HEAD, :] = x_ref[s, half, :]
            at += HEAD
    for x_ref in (first, second):
        for s in range(SEQS):
            for part in range(2):
                half = pl.ds(pl.multiple_of((2 * part + other) * HEAD, HEAD), HEAD)
                send[at : at + HEAD, :] = x_ref[s, half, :]
                at += HEAD


def pick(*args):
    vmem = pl.BlockSpec(memory_space=pltpu.VMEM)
    rows = (3 * (SEQS // 2) + 2 * SEQS * 2) * HEAD
    return pl.pallas_call(
        pick_kernel,
        out_shape=jax.ShapeDtypeStruct((rows, ROWS), BF),
        in_specs=[vmem] * 5,
        out_specs=vmem,
        compiler_params=pltpu.CompilerParams(vmem_limit_bytes=8 * 2**20),
        cost_estimate=pl.CostEstimate(flops=0, bytes_accessed=2**20, transcendentals=0),
    )(*args)


def attention_kernel(
    q_ref, g_ref, o_ref, first, second, given, bias,
    bias_grad, dq_ref, dkv_ref,
    stack, wide, raw, low, inner,
):
    ri, rj, core = (lax.axis_index(a) for a in ("ri", "rj", "core"))
    own = pl.ds(pl.multiple_of(core * HEAD, HEAD), HEAD)
    rounds = [2 * core, 2 * core + 1, 2 - 2 * core, 3 - 2 * core]
    blocks = [lax.rem(ri + 2 * N - rj - t, N) for t in rounds]

    def query_side(i, s):
        if s < SEQS // 2:
            return (q_ref, g_ref, o_ref)[i][s, own, :]
        at = (i * (SEQS // 2) + s - SEQS // 2) * HEAD
        return given[at : at + HEAD, :]

    def key_side(part, t, s):
        if t < 2:
            half = pl.ds(pl.multiple_of((2 * part + core) * HEAD, HEAD), HEAD)
            return (first, second)[t][s, half, :]
        there = (s + SEQS // 2) % SEQS
        at = (3 * (SEQS // 2) + ((t - 2) * SEQS + there) * 2 + part) * HEAD
        return given[at : at + HEAD, :]

    channel = lax.broadcasted_iota(jnp.int32, (2 * HEAD, ROWS), 0) // HEAD

    for s in range(SEQS):
        for part in range(2):
            at = slice(part * ROWS, (part + 1) * ROWS)
            one = jnp.where(channel == part, jnp.concatenate([query_side(0, s), query_side(1, s)]), 0)
            wide[s, :, at] = one
            stack[s, at, :] = one.T
        dots = query_side(1, s).astype(F32) * query_side(2, s).astype(F32)
        sums = jnp.sum(dots, axis=0, keepdims=True)
        inner[s] = jnp.broadcast_to(sums, (LANES, ROWS)).T

    for s in range(SEQS):
        for t in range(N):
            at = slice(t * ROWS, (t + 1) * ROWS)
            kv = jnp.concatenate([key_side(0, t, s), key_side(1, t, s)])
            raw[s, :, at] = lax.dot_general(stack[s], kv, NN, preferred_element_type=F32)

    @pl.loop(0, ROWS // CHUNK, unroll=UNROLL)
    def _(i):
        r0 = pl.multiple_of(i * CHUNK, CHUNK)
        at_logits = pl.ds(r0, CHUNK)
        at_grads = pl.ds(pl.multiple_of(ROWS + r0, CHUNK), CHUNK)
        pair = jnp.concatenate([bias[b, at_logits, :] for b in blocks], axis=1).astype(F32)
        total = None
        for s in range(SEQS):
            logits = raw[s, at_logits, :] * SCALE + pair
            top = jnp.max(logits, axis=1, keepdims=True)
            weights = jnp.exp(logits - top)
            weights = weights * (1.0 / jnp.sum(weights, axis=1, keepdims=True))
            dots = jnp.concatenate([inner[s, at_logits, :]] * (KEYS // LANES), axis=1)
            grad = weights * (raw[s, at_grads, :] - dots)
            low[s, at_logits, :] = grad.astype(BF)
            low[s, at_grads, :] = weights.astype(BF)
            total = grad if total is None else total + grad
        total = total.astype(BF)
        quarter = i // (64 // CHUNK)
        within = pl.ds(pl.multiple_of(lax.rem(i, 64 // CHUNK) * CHUNK, CHUNK), CHUNK)
        for t, b in enumerate(blocks):
            bias_grad[quarter * N + b, within, :] = total[:, t * ROWS : (t + 1) * ROWS]

    for s in range(SEQS):
        query_grads = None
        for t, b in enumerate(blocks):
            at = slice(t * ROWS, (t + 1) * ROWS)
            grads = lax.dot_general(wide[s], low[s, :, at], NN, preferred_element_type=F32)
            grads = jnp.where(channel == 0, grads * SCALE, grads)
            dkv_ref[lax.rem(b + N - rj, N), s] = grads.astype(BF)
            key = key_side(0, t, s)
            term = lax.dot_general(low[s, :ROWS, at], key, NT, preferred_element_type=F32)
            query_grads = term if query_grads is None else query_grads + term
        dq_ref[s] = (query_grads.T * SCALE).astype(BF)


def attention(*args):
    vmem = pl.BlockSpec(memory_space=pltpu.VMEM)
    return pl.pallas_call(
        attention_kernel,
        out_shape=(
            jax.ShapeDtypeStruct((N * N, 64, ROWS), BF),
            jax.ShapeDtypeStruct((SEQS, HEAD, ROWS), BF),
            jax.ShapeDtypeStruct((N, SEQS, 2 * HEAD, ROWS), BF),
        ),
        in_specs=[vmem] * 7,
        out_specs=(vmem,) * 3,
        scratch_shapes=[
            pltpu.VMEM((SEQS, 2 * ROWS, 2 * HEAD), BF),
            pltpu.VMEM((SEQS, 2 * HEAD, 2 * ROWS), BF),
            pltpu.VMEM((SEQS, 2 * ROWS, KEYS), F32),
            pltpu.VMEM((SEQS, 2 * ROWS, KEYS), BF),
            pltpu.VMEM((SEQS, ROWS, LANES), F32),
        ],
        compiler_params=pltpu.CompilerParams(vmem_limit_bytes=32 * 2**20),
        cost_estimate=pl.CostEstimate(
            flops=5 * 2 * 2**25, bytes_accessed=6 * 2**20, transcendentals=2**20
        ),
    )(*args)


def split_kernel(after, x_ref, *outs):
    for t, out in enumerate(outs):
        out[...] = x_ref[t]


def choose_kernel(after, *refs):
    ri, rj = lax.axis_index("ri"), lax.axis_index("rj")
    for t, out in enumerate(refs[N:]):
        wanted = lax.rem(rj + 2 * N - ri - t, N)
        for source, x_ref in enumerate(refs[:N]):

            @pl.when(wanted == source)
            def _():
                out[...] = x_ref[...]


def hand_on(kernel, after, *args):
    anywhere, vmem = pl.BlockSpec(memory_space=pl.ANY), pl.BlockSpec(memory_space=pltpu.VMEM)
    return pl.pallas_call(
        kernel,
        out_shape=[jax.ShapeDtypeStruct(args[0].shape[-3:], BF)] * N,
        in_specs=[anywhere] + [vmem] * len(args),
        out_specs=[vmem] * N,
        compiler_params=pltpu.CompilerParams(vmem_limit_bytes=8 * 2**20),
        cost_estimate=pl.CostEstimate(flops=0, bytes_accessed=2**21, transcendentals=0),
    )(after, *args)


def place_heads(x_ref, out_ref, wide, sem, head):
    copies = []
    for j in range(N):
        for x in range(N):
            at = (x * N + j) * 64
            wide[j, x * 64 : (x + 1) * 64, :] = x_ref[at : at + 64, :].astype(F32)
        copies.append(pltpu.make_async_copy(wide.at[j], out_ref.at[2 * j + head], sem.at[j]))
        copies[-1].start()
    return copies


def place_kernel(x_ref, out_ref, wide, sem):
    for c in place_heads(x_ref, out_ref, wide, sem, lax.axis_index("core")):
        c.wait()


def finish_kernel(x_ref, own_ref, before, out_ref, dk_ref, dv_ref, dq_ref, wide, both, sem):
    core = lax.axis_index("core")
    copies = place_heads(x_ref, out_ref, wide, sem, 1 - core)
    mine = pl.ds(pl.multiple_of(core * HEAD, HEAD), HEAD)
    theirs = pl.ds(pl.multiple_of((1 - core) * HEAD, HEAD), HEAD)
    for i, grad_ref in enumerate((dk_ref, dv_ref, dq_ref)):
        for s in range(SEQS // 2):
            at = N * ROWS + (s * 3 + i) * HEAD
            both[i, s, mine, :] = own_ref[s, i * HEAD : (i + 1) * HEAD, :]
            both[i, s, theirs, :] = x_ref[at : at + HEAD, :]
        copies.append(pltpu.make_async_copy(both.at[i], grad_ref, sem.at[N + i]))
        copies[-1].start()
    for c in copies:
        c.wait()


def place(x):
    anywhere, vmem = pl.BlockSpec(memory_space=pl.ANY), pl.BlockSpec(memory_space=pltpu.VMEM)
    return pl.pallas_call(
        place_kernel,
        out_shape=jax.ShapeDtypeStruct((2 * N, ROWS, ROWS), F32),
        in_specs=[vmem],
        out_specs=anywhere,
        scratch_shapes=[pltpu.VMEM((N, ROWS, ROWS), F32), pltpu.SemaphoreType.DMA((N,))],
        compiler_params=pltpu.CompilerParams(vmem_limit_bytes=8 * 2**20),
        cost_estimate=pl.CostEstimate(flops=2**18, bytes_accessed=3 * 2**19, transcendentals=0),
    )(x)


def finish(x, own, before):
    anywhere, vmem = pl.BlockSpec(memory_space=pl.ANY), pl.BlockSpec(memory_space=pltpu.VMEM)
    grad = jax.ShapeDtypeStruct((SEQS // 2, 2 * HEAD, ROWS), BF)
    return pl.pallas_call(
        finish_kernel,
        out_shape=(jax.ShapeDtypeStruct(before.shape, F32), grad, grad, grad),
        in_specs=[vmem, vmem, anywhere],
        out_specs=(anywhere,) * 4,
        scratch_shapes=[
            pltpu.VMEM((N, ROWS, ROWS), F32),
            pltpu.VMEM((3, *grad.shape), BF),
            pltpu.SemaphoreType.DMA((N + 3,)),
        ],
        input_output_aliases={2: 0},
        compiler_params=pltpu.CompilerParams(vmem_limit_bytes=8 * 2**20),
        cost_estimate=pl.CostEstimate(flops=2**18, bytes_accessed=2**21, transcendentals=0),
    )(x, own, before)


def swap(x, axis, pairs):
    return lax.ppermute(x, axis, [(a, b) for a, b in pairs] + [(b, a) for a, b in pairs])


def add(a, b):
    return (a.astype(F32) + b.astype(F32)).astype(BF)


def beside_ring(x, step):
    pairs = []
    for core in range(2):
        for zh in range(N):
            up = (zh + step + core) % 2 == 1
            pairs.append((zh * 2 + core, (zh + (1 if up else -1)) % N * 2 + core))
    return lax.ppermute(x, ("zh", "core"), pairs)


def body(query_proj, key_proj, value_proj, pair_bias, attn_output, output_grad):
    q, k, v, o, g = (
        jnp.swapaxes(x, 1, 2)
        for x in (query_proj, key_proj, value_proj, attn_output, output_grad)
    )
    grid = [(a, b) for a in range(N) for b in range(N)]

    core = lax.axis_index("core")
    held = jnp.concatenate([k, v], axis=1)
    bias = lax.dynamic_index_in_dim(pair_bias.reshape(N, 2, ROWS, ROWS), core, 1, False)
    theirs, bias = lax.optimization_barrier((swap(held, "core", [(0, 1)]), bias))
    kv = jnp.concatenate([held, theirs])
    spread = []
    for i in range(2):
        steps = []
        for c in range(2):
            for a, b in grid:
                target = (a + b + 2 * c + i) % N * N + a
                steps.append((c * N * N + a * N + b, c * N * N + target))
        spread.append(lax.ppermute(kv, ("core", "ri", "rj"), steps))
    bias = lax.all_to_all(bias, "rj", 0, 0, tiled=True)
    given = swap(pick(q, g, o, *spread), "core", [(0, 1)])

    total, dq, dkv = attention(q, g, o, *spread, given, bias)

    def spread_out(parts, axis):
        return [parts[0]] + [
            lax.ppermute(parts[t], axis, [(a, (a + t) % N) for a in range(N)])
            for t in range(1, N)
        ]

    spread = lax.all_to_all(total, ("x", "rj"), 0, 0, tiled=True)
    total = jnp.sum(spread.reshape(N, N, 64, ROWS).astype(F32), axis=0).astype(BF)
    other = beside_ring(total, 0)
    parts = spread_out(hand_on(split_kernel, total, dkv), "rj")
    total = add(total, other)
    other = beside_ring(total, 1)
    parts = spread_out(hand_on(choose_kernel, total, *parts), "ri")
    total = add(total, other)
    mine = lax.all_gather(total, "x", axis=0, tiled=True).reshape(-1, ROWS)

    dkv = sum(x.astype(F32) for x in parts).astype(BF)
    grads = jnp.concatenate([dkv, dq], axis=1)
    own, others = grads[: SEQS // 2], grads[SEQS // 2 :]
    theirs = swap(jnp.concatenate([mine, others.reshape(-1, ROWS)]), "core", [(0, 1)])
    bias_grad, dk, dv, dq = finish(theirs, own, place(mine))
    return *(jnp.swapaxes(x, 1, 2) for x in (dq, dk, dv)), bias_grad


def solution(mesh):
    split = Mesh(mesh.devices.reshape(N, N, 2, N, N), ("zh", "x", "core", "ri", "rj"))
    seq = ("zh", "x", "core")
    rows, keys, tile = P(seq, "ri", "rj"), P(seq, "rj", "ri"), P(None, "ri", "rj")
    return jax.shard_map(
        body,
        mesh=split,
        in_specs=(rows, keys, keys, tile, rows, rows),
        out_specs=(rows, keys, keys, tile),
        check_vma=False,
    )
```

```python
import jax
import jax.numpy as jnp
from jax import lax
from jax.experimental import pallas as pl
from jax.experimental.pallas import tpu as pltpu
from jax.sharding import Mesh
from jax.sharding import PartitionSpec as P

HEAD = 32
SCALE = HEAD**-0.5
N = 4
ROWS = 256
KEYS = N * ROWS
LANES = 128
SEQS = 4
CHUNK = 32
UNROLL = 8
BF = jnp.bfloat16
F32 = jnp.float32
NT = (((1,), (1,)), ((), ()))
NN = (((1,), (0,)), ((), ()))


def pick_kernel(q_ref, g_ref, o_ref, first, second, send):
    other = 1 - lax.axis_index("core")
    at = 0
    half = pl.ds(pl.multiple_of(other * HEAD, HEAD), HEAD)
    for x_ref in (q_ref, g_ref, o_ref):
        for s in range(SEQS // 2):
            send[at : at + HEAD, :] = x_ref[s, half, :]
            at += HEAD
    for x_ref in (first, second):
        for s in range(SEQS):
            for part in range(2):
                half = pl.ds(pl.multiple_of((2 * part + other) * HEAD, HEAD), HEAD)
                send[at : at + HEAD, :] = x_ref[s, half, :]
                at += HEAD


def pick(*args):
    vmem = pl.BlockSpec(memory_space=pltpu.VMEM)
    rows = (3 * (SEQS // 2) + 2 * SEQS * 2) * HEAD
    return pl.pallas_call(
        pick_kernel,
        out_shape=jax.ShapeDtypeStruct((rows, ROWS), BF),
        in_specs=[vmem] * 5,
        out_specs=vmem,
        compiler_params=pltpu.CompilerParams(vmem_limit_bytes=8 * 2**20),
        cost_estimate=pl.CostEstimate(flops=0, bytes_accessed=2**20, transcendentals=0),
    )(*args)


def attention_kernel(
    q_ref, g_ref, o_ref, first, second, given, bias,
    bias_grad, dq_ref, dkv_ref,
    stack, wide, raw, low, inner,
):
    ri, rj, core = (lax.axis_index(a) for a in ("ri", "rj", "core"))
    own = pl.ds(pl.multiple_of(core * HEAD, HEAD), HEAD)
    rounds = [2 * core, 2 * core + 1, 2 - 2 * core, 3 - 2 * core]
    blocks = [lax.rem(ri + 2 * N - rj - t, N) for t in rounds]

    def query_side(i, s):
        if s < SEQS // 2:
            return (q_ref, g_ref, o_ref)[i][s, own, :]
        at = (i * (SEQS // 2) + s - SEQS // 2) * HEAD
        return given[at : at + HEAD, :]

    def key_side(part, t, s):
        if t < 2:
            half = pl.ds(pl.multiple_of((2 * part + core) * HEAD, HEAD), HEAD)
            return (first, second)[t][s, half, :]
        there = (s + SEQS // 2) % SEQS
        at = (3 * (SEQS // 2) + ((t - 2) * SEQS + there) * 2 + part) * HEAD
        return given[at : at + HEAD, :]

    channel = lax.broadcasted_iota(jnp.int32, (2 * HEAD, ROWS), 0) // HEAD

    for s in range(SEQS):
        for part in range(2):
            at = slice(part * ROWS, (part + 1) * ROWS)
            one = jnp.where(channel == part, jnp.concatenate([query_side(0, s), query_side(1, s)]), 0)
            wide[s, :, at] = one
            stack[s, at, :] = one.T
        dots = query_side(1, s).astype(F32) * query_side(2, s).astype(F32)
        sums = jnp.sum(dots, axis=0, keepdims=True)
        inner[s] = jnp.broadcast_to(sums, (LANES, ROWS)).T

    for s in range(SEQS):
        for t in range(N):
            at = slice(t * ROWS, (t + 1) * ROWS)
            kv = jnp.concatenate([key_side(0, t, s), key_side(1, t, s)])
            raw[s, :, at] = lax.dot_general(stack[s], kv, NN, preferred_element_type=F32)

    @pl.loop(0, ROWS // CHUNK, unroll=UNROLL)
    def _(i):
        r0 = pl.multiple_of(i * CHUNK, CHUNK)
        at_logits = pl.ds(r0, CHUNK)
        at_grads = pl.ds(pl.multiple_of(ROWS + r0, CHUNK), CHUNK)
        pair = jnp.concatenate([bias[b, at_logits, :] for b in blocks], axis=1).astype(F32)
        total = None
        for s in range(SEQS):
            logits = raw[s, at_logits, :] * SCALE + pair
            top = jnp.max(logits, axis=1, keepdims=True)
            weights = jnp.exp(logits - top)
            weights = weights * (1.0 / jnp.sum(weights, axis=1, keepdims=True))
            dots = jnp.concatenate([inner[s, at_logits, :]] * (KEYS // LANES), axis=1)
            grad = weights * (raw[s, at_grads, :] - dots)
            low[s, at_logits, :] = grad.astype(BF)
            low[s, at_grads, :] = weights.astype(BF)
            total = grad if total is None else total + grad
        total = total.astype(BF)
        quarter = i // (64 // CHUNK)
        within = pl.ds(pl.multiple_of(lax.rem(i, 64 // CHUNK) * CHUNK, CHUNK), CHUNK)
        for t, b in enumerate(blocks):
            bias_grad[quarter * N + b, within, :] = total[:, t * ROWS : (t + 1) * ROWS]

    for s in range(SEQS):
        query_grads = None
        for t, b in enumerate(blocks):
            at = slice(t * ROWS, (t + 1) * ROWS)
            grads = lax.dot_general(wide[s], low[s, :, at], NN, preferred_element_type=F32)
            grads = jnp.where(channel == 0, grads * SCALE, grads)
            dkv_ref[b, s] = grads.astype(BF)
            key = key_side(0, t, s)
            term = lax.dot_general(low[s, :ROWS, at], key, NT, preferred_element_type=F32)
            query_grads = term if query_grads is None else query_grads + term
        dq_ref[s] = (query_grads.T * SCALE).astype(BF)


def attention(*args):
    vmem = pl.BlockSpec(memory_space=pltpu.VMEM)
    return pl.pallas_call(
        attention_kernel,
        out_shape=(
            jax.ShapeDtypeStruct((N * N, 64, ROWS), BF),
            jax.ShapeDtypeStruct((SEQS, HEAD, ROWS), BF),
            jax.ShapeDtypeStruct((N, SEQS, 2 * HEAD, ROWS), BF),
        ),
        in_specs=[vmem] * 7,
        out_specs=(vmem,) * 3,
        scratch_shapes=[
            pltpu.VMEM((SEQS, 2 * ROWS, 2 * HEAD), BF),
            pltpu.VMEM((SEQS, 2 * HEAD, 2 * ROWS), BF),
            pltpu.VMEM((SEQS, 2 * ROWS, KEYS), F32),
            pltpu.VMEM((SEQS, 2 * ROWS, KEYS), BF),
            pltpu.VMEM((SEQS, ROWS, LANES), F32),
        ],
        compiler_params=pltpu.CompilerParams(vmem_limit_bytes=32 * 2**20),
        cost_estimate=pl.CostEstimate(
            flops=5 * 2 * 2**25, bytes_accessed=6 * 2**20, transcendentals=2**20
        ),
    )(*args)


def place_heads(x_ref, out_ref, wide, sem, head):
    copies = []
    for j in range(N):
        for x in range(N):
            at = (x * N + j) * 64
            wide[j, x * 64 : (x + 1) * 64, :] = x_ref[at : at + 64, :].astype(F32)
        copies.append(pltpu.make_async_copy(wide.at[j], out_ref.at[2 * j + head], sem.at[j]))
        copies[-1].start()
    return copies


def place_kernel(x_ref, out_ref, wide, sem):
    for c in place_heads(x_ref, out_ref, wide, sem, lax.axis_index("core")):
        c.wait()


def finish_kernel(x_ref, own_ref, before, out_ref, dk_ref, dv_ref, dq_ref, wide, both, sem):
    core = lax.axis_index("core")
    copies = place_heads(x_ref, out_ref, wide, sem, 1 - core)
    mine = pl.ds(pl.multiple_of(core * HEAD, HEAD), HEAD)
    theirs = pl.ds(pl.multiple_of((1 - core) * HEAD, HEAD), HEAD)
    for i, grad_ref in enumerate((dk_ref, dv_ref, dq_ref)):
        for s in range(SEQS // 2):
            at = N * ROWS + (s * 3 + i) * HEAD
            both[i, s, mine, :] = own_ref[s, i * HEAD : (i + 1) * HEAD, :]
            both[i, s, theirs, :] = x_ref[at : at + HEAD, :]
        copies.append(pltpu.make_async_copy(both.at[i], grad_ref, sem.at[N + i]))
        copies[-1].start()
    for c in copies:
        c.wait()


def place(x):
    anywhere, vmem = pl.BlockSpec(memory_space=pl.ANY), pl.BlockSpec(memory_space=pltpu.VMEM)
    return pl.pallas_call(
        place_kernel,
        out_shape=jax.ShapeDtypeStruct((2 * N, ROWS, ROWS), F32),
        in_specs=[vmem],
        out_specs=anywhere,
        scratch_shapes=[pltpu.VMEM((N, ROWS, ROWS), F32), pltpu.SemaphoreType.DMA((N,))],
        compiler_params=pltpu.CompilerParams(vmem_limit_bytes=8 * 2**20),
        cost_estimate=pl.CostEstimate(flops=2**18, bytes_accessed=3 * 2**19, transcendentals=0),
    )(x)


def finish(x, own, before):
    anywhere, vmem = pl.BlockSpec(memory_space=pl.ANY), pl.BlockSpec(memory_space=pltpu.VMEM)
    grad = jax.ShapeDtypeStruct((SEQS // 2, 2 * HEAD, ROWS), BF)
    return pl.pallas_call(
        finish_kernel,
        out_shape=(jax.ShapeDtypeStruct(before.shape, F32), grad, grad, grad),
        in_specs=[vmem, vmem, anywhere],
        out_specs=(anywhere,) * 4,
        scratch_shapes=[
            pltpu.VMEM((N, ROWS, ROWS), F32),
            pltpu.VMEM((3, *grad.shape), BF),
            pltpu.SemaphoreType.DMA((N + 3,)),
        ],
        input_output_aliases={2: 0},
        compiler_params=pltpu.CompilerParams(vmem_limit_bytes=8 * 2**20),
        cost_estimate=pl.CostEstimate(flops=2**18, bytes_accessed=2**21, transcendentals=0),
    )(x, own, before)


def swap(x, axis, pairs):
    return lax.ppermute(x, axis, [(a, b) for a, b in pairs] + [(b, a) for a, b in pairs])


def add(a, b):
    return (a.astype(F32) + b.astype(F32)).astype(BF)


def beside_ring(x, step):
    pairs = []
    for core in range(2):
        for zh in range(N):
            up = (zh + step + core) % 2 == 0
            pairs.append((zh * 2 + core, (zh + (1 if up else -1)) % N * 2 + core))
    return lax.ppermute(x, ("zh", "core"), pairs)


def body(query_proj, key_proj, value_proj, pair_bias, attn_output, output_grad):
    q, k, v, o, g = (
        jnp.swapaxes(x, 1, 2)
        for x in (query_proj, key_proj, value_proj, attn_output, output_grad)
    )
    grid = [(a, b) for a in range(N) for b in range(N)]

    core = lax.axis_index("core")
    held = jnp.concatenate([k, v], axis=1)
    bias = lax.dynamic_index_in_dim(pair_bias.reshape(N, 2, ROWS, ROWS), core, 1, False)
    theirs, bias = lax.optimization_barrier((swap(held, "core", [(0, 1)]), bias))
    kv = jnp.concatenate([held, theirs])
    spread = []
    for i in range(2):
        steps = []
        for c in range(2):
            for a, b in grid:
                target = (a + b + 2 * c + i) % N * N + a
                steps.append((c * N * N + a * N + b, c * N * N + target))
        spread.append(lax.ppermute(kv, ("core", "ri", "rj"), steps))
    bias = lax.all_to_all(bias, "rj", 0, 0, tiled=True)
    given = swap(pick(q, g, o, *spread), "core", [(0, 1)])

    total, dq, dkv = attention(q, g, o, *spread, given, bias)

    spread = lax.all_to_all(total, ("x", "rj"), 0, 0, tiled=True)
    back = lax.psum_scatter(dkv.reshape(-1, ROWS), "ri", scatter_dimension=0, tiled=True)
    total = jnp.sum(spread.reshape(N, N, 64, ROWS).astype(F32), axis=0).astype(BF)
    total = add(total, beside_ring(total, 0))
    total = add(total, beside_ring(total, 1))
    total, back = lax.optimization_barrier((total, back))
    back = lax.ppermute(back, ("ri", "rj"), [(a * N + b, b * N + a) for a, b in grid])
    mine, back = lax.optimization_barrier((lax.all_gather(total, "x", axis=0, tiled=True), back))
    mine = mine.reshape(-1, ROWS)

    grads = jnp.concatenate([back.reshape(dkv.shape[1:]), dq], axis=1)
    own, others = grads[: SEQS // 2], grads[SEQS // 2 :]
    theirs = swap(jnp.concatenate([mine, others.reshape(-1, ROWS)]), "core", [(0, 1)])
    bias_grad, dk, dv, dq = finish(theirs, own, place(mine))
    return *(jnp.swapaxes(x, 1, 2) for x in (dq, dk, dv)), bias_grad


def solution(mesh):
    split = Mesh(mesh.devices.reshape(N, N, 2, N, N), ("zh", "x", "core", "ri", "rj"))
    seq = ("zh", "x", "core")
    rows, keys, tile = P(seq, "ri", "rj"), P(seq, "rj", "ri"), P(None, "ri", "rj")
    return jax.shard_map(
        body,
        mesh=split,
        in_specs=(rows, keys, keys, tile, rows, rows),
        out_specs=(rows, keys, keys, tile),
        check_vma=False,
    )
```

```python
import jax
import jax.numpy as jnp
from jax import lax
from jax.experimental import pallas as pl
from jax.experimental.pallas import tpu as pltpu
from jax.sharding import Mesh
from jax.sharding import PartitionSpec as P

HEAD = 32
SCALE = HEAD**-0.5
N = 4
ROWS = 256
KEYS = N * ROWS
LANES = 128
SEQS = 4
CHUNK = 32
UNROLL = 8
BF = jnp.bfloat16
F32 = jnp.float32
NT = (((1,), (1,)), ((), ()))
NN = (((1,), (0,)), ((), ()))


def pick_kernel(q_ref, g_ref, o_ref, first, second, send):
    other = 1 - lax.axis_index("core")
    at = 0
    half = pl.ds(pl.multiple_of(other * HEAD, HEAD), HEAD)
    for x_ref in (q_ref, g_ref, o_ref):
        for s in range(SEQS // 2):
            send[at : at + HEAD, :] = x_ref[s, half, :]
            at += HEAD
    for x_ref in (first, second):
        for s in range(SEQS):
            for part in range(2):
                half = pl.ds(pl.multiple_of((2 * part + other) * HEAD, HEAD), HEAD)
                send[at : at + HEAD, :] = x_ref[s, half, :]
                at += HEAD


def pick(*args):
    vmem = pl.BlockSpec(memory_space=pltpu.VMEM)
    rows = (3 * (SEQS // 2) + 2 * SEQS * 2) * HEAD
    return pl.pallas_call(
        pick_kernel,
        out_shape=jax.ShapeDtypeStruct((rows, ROWS), BF),
        in_specs=[vmem] * 5,
        out_specs=vmem,
        compiler_params=pltpu.CompilerParams(vmem_limit_bytes=8 * 2**20),
        cost_estimate=pl.CostEstimate(flops=0, bytes_accessed=2**20, transcendentals=0),
    )(*args)


def attention_kernel(
    q_ref, g_ref, o_ref, first, second, given, bias,
    bias_grad, dq_ref, dkv_ref,
    stack, wide, raw, low, inner,
):
    ri, rj, core = (lax.axis_index(a) for a in ("ri", "rj", "core"))
    own = pl.ds(pl.multiple_of(core * HEAD, HEAD), HEAD)
    rounds = [core, core + 2, 1 - core, 3 - core]
    blocks = [lax.rem(ri + 2 * N - rj - t, N) for t in rounds]

    def query_side(i, s):
        if s < SEQS // 2:
            return (q_ref, g_ref, o_ref)[i][s, own, :]
        at = (i * (SEQS // 2) + s - SEQS // 2) * HEAD
        return given[at : at + HEAD, :]

    def key_side(part, t, s):
        if t < 2:
            half = pl.ds(pl.multiple_of((2 * part + core) * HEAD, HEAD), HEAD)
            return (first, second)[t][s, half, :]
        there = (s + SEQS // 2) % SEQS
        at = (3 * (SEQS // 2) + ((t - 2) * SEQS + there) * 2 + part) * HEAD
        return given[at : at + HEAD, :]

    channel = lax.broadcasted_iota(jnp.int32, (2 * HEAD, ROWS), 0) // HEAD

    for s in range(SEQS):
        for part in range(2):
            at = slice(part * ROWS, (part + 1) * ROWS)
            one = jnp.where(channel == part, jnp.concatenate([query_side(0, s), query_side(1, s)]), 0)
            wide[s, :, at] = one
            stack[s, at, :] = one.T
        dots = query_side(1, s).astype(F32) * query_side(2, s).astype(F32)
        sums = jnp.sum(dots, axis=0, keepdims=True)
        inner[s] = jnp.broadcast_to(sums, (LANES, ROWS)).T

    for s in range(SEQS):
        for t in range(N):
            at = slice(t * ROWS, (t + 1) * ROWS)
            kv = jnp.concatenate([key_side(0, t, s), key_side(1, t, s)])
            raw[s, :, at] = lax.dot_general(stack[s], kv, NN, preferred_element_type=F32)

    @pl.loop(0, ROWS // CHUNK, unroll=UNROLL)
    def _(i):
        r0 = pl.multiple_of(i * CHUNK, CHUNK)
        at_logits = pl.ds(r0, CHUNK)
        at_grads = pl.ds(pl.multiple_of(ROWS + r0, CHUNK), CHUNK)
        pair = jnp.concatenate([bias[b, at_logits, :] for b in blocks], axis=1).astype(F32)
        total = None
        for s in range(SEQS):
            logits = raw[s, at_logits, :] * SCALE + pair
            top = jnp.max(logits, axis=1, keepdims=True)
            weights = jnp.exp(logits - top)
            weights = weights * (1.0 / jnp.sum(weights, axis=1, keepdims=True))
            dots = jnp.concatenate([inner[s, at_logits, :]] * (KEYS // LANES), axis=1)
            grad = weights * (raw[s, at_grads, :] - dots)
            low[s, at_logits, :] = grad.astype(BF)
            low[s, at_grads, :] = weights.astype(BF)
            total = grad if total is None else total + grad
        total = total.astype(BF)
        quarter = i // (64 // CHUNK)
        within = pl.ds(pl.multiple_of(lax.rem(i, 64 // CHUNK) * CHUNK, CHUNK), CHUNK)
        for t, b in enumerate(blocks):
            bias_grad[quarter * N + b, within, :] = total[:, t * ROWS : (t + 1) * ROWS]

    for s in range(SEQS):
        query_grads = None
        for t, b in enumerate(blocks):
            at = slice(t * ROWS, (t + 1) * ROWS)
            grads = lax.dot_general(wide[s], low[s, :, at], NN, preferred_element_type=F32)
            grads = jnp.where(channel == 0, grads * SCALE, grads)
            dkv_ref[lax.rem(b + N - rj, N), s] = grads.astype(BF)
            key = key_side(0, t, s)
            term = lax.dot_general(low[s, :ROWS, at], key, NT, preferred_element_type=F32)
            query_grads = term if query_grads is None else query_grads + term
        dq_ref[s] = (query_grads.T * SCALE).astype(BF)


def attention(*args):
    vmem = pl.BlockSpec(memory_space=pltpu.VMEM)
    return pl.pallas_call(
        attention_kernel,
        out_shape=(
            jax.ShapeDtypeStruct((N * N, 64, ROWS), BF),
            jax.ShapeDtypeStruct((SEQS, HEAD, ROWS), BF),
            jax.ShapeDtypeStruct((N, SEQS, 2 * HEAD, ROWS), BF),
        ),
        in_specs=[vmem] * 7,
        out_specs=(vmem,) * 3,
        scratch_shapes=[
            pltpu.VMEM((SEQS, 2 * ROWS, 2 * HEAD), BF),
            pltpu.VMEM((SEQS, 2 * HEAD, 2 * ROWS), BF),
            pltpu.VMEM((SEQS, 2 * ROWS, KEYS), F32),
            pltpu.VMEM((SEQS, 2 * ROWS, KEYS), BF),
            pltpu.VMEM((SEQS, ROWS, LANES), F32),
        ],
        compiler_params=pltpu.CompilerParams(vmem_limit_bytes=32 * 2**20),
        cost_estimate=pl.CostEstimate(
            flops=5 * 2 * 2**25, bytes_accessed=6 * 2**20, transcendentals=2**20
        ),
    )(*args)


def split_kernel(after, x_ref, *outs):
    for t, out in enumerate(outs):
        out[...] = x_ref[t]


def choose_kernel(after, *refs):
    ri, rj = lax.axis_index("ri"), lax.axis_index("rj")
    for t, out in enumerate(refs[N:]):
        wanted = lax.rem(rj + 2 * N - ri - t, N)
        for source, x_ref in enumerate(refs[:N]):

            @pl.when(wanted == source)
            def _():
                out[...] = x_ref[...]


def hand_on(kernel, after, *args):
    anywhere, vmem = pl.BlockSpec(memory_space=pl.ANY), pl.BlockSpec(memory_space=pltpu.VMEM)
    return pl.pallas_call(
        kernel,
        out_shape=[jax.ShapeDtypeStruct(args[0].shape[-3:], BF)] * N,
        in_specs=[anywhere] + [vmem] * len(args),
        out_specs=[vmem] * N,
        compiler_params=pltpu.CompilerParams(vmem_limit_bytes=8 * 2**20),
        cost_estimate=pl.CostEstimate(flops=0, bytes_accessed=2**21, transcendentals=0),
    )(after, *args)


def place_heads(x_ref, out_ref, wide, sem, head):
    copies = []
    for j in range(N):
        for x in range(N):
            at = (x * N + j) * 64
            wide[j, x * 64 : (x + 1) * 64, :] = x_ref[at : at + 64, :].astype(F32)
        copies.append(pltpu.make_async_copy(wide.at[j], out_ref.at[2 * j + head], sem.at[j]))
        copies[-1].start()
    return copies


def place_kernel(x_ref, out_ref, wide, sem):
    for c in place_heads(x_ref, out_ref, wide, sem, lax.axis_index("core")):
        c.wait()


def finish_kernel(x_ref, own_ref, before, out_ref, dk_ref, dv_ref, dq_ref, wide, both, sem):
    core = lax.axis_index("core")
    copies = place_heads(x_ref, out_ref, wide, sem, 1 - core)
    mine = pl.ds(pl.multiple_of(core * HEAD, HEAD), HEAD)
    theirs = pl.ds(pl.multiple_of((1 - core) * HEAD, HEAD), HEAD)
    for i, grad_ref in enumerate((dk_ref, dv_ref, dq_ref)):
        for s in range(SEQS // 2):
            at = N * ROWS + (s * 3 + i) * HEAD
            both[i, s, mine, :] = own_ref[s, i * HEAD : (i + 1) * HEAD, :]
            both[i, s, theirs, :] = x_ref[at : at + HEAD, :]
        copies.append(pltpu.make_async_copy(both.at[i], grad_ref, sem.at[N + i]))
        copies[-1].start()
    for c in copies:
        c.wait()


def place(x):
    anywhere, vmem = pl.BlockSpec(memory_space=pl.ANY), pl.BlockSpec(memory_space=pltpu.VMEM)
    return pl.pallas_call(
        place_kernel,
        out_shape=jax.ShapeDtypeStruct((2 * N, ROWS, ROWS), F32),
        in_specs=[vmem],
        out_specs=anywhere,
        scratch_shapes=[pltpu.VMEM((N, ROWS, ROWS), F32), pltpu.SemaphoreType.DMA((N,))],
        compiler_params=pltpu.CompilerParams(vmem_limit_bytes=8 * 2**20),
        cost_estimate=pl.CostEstimate(flops=2**18, bytes_accessed=3 * 2**19, transcendentals=0),
    )(x)


def finish(x, own, before):
    anywhere, vmem = pl.BlockSpec(memory_space=pl.ANY), pl.BlockSpec(memory_space=pltpu.VMEM)
    grad = jax.ShapeDtypeStruct((SEQS // 2, 2 * HEAD, ROWS), BF)
    return pl.pallas_call(
        finish_kernel,
        out_shape=(jax.ShapeDtypeStruct(before.shape, F32), grad, grad, grad),
        in_specs=[vmem, vmem, anywhere],
        out_specs=(anywhere,) * 4,
        scratch_shapes=[
            pltpu.VMEM((N, ROWS, ROWS), F32),
            pltpu.VMEM((3, *grad.shape), BF),
            pltpu.SemaphoreType.DMA((N + 3,)),
        ],
        input_output_aliases={2: 0},
        compiler_params=pltpu.CompilerParams(vmem_limit_bytes=8 * 2**20),
        cost_estimate=pl.CostEstimate(flops=2**18, bytes_accessed=2**21, transcendentals=0),
    )(x, own, before)


def swap(x, axis, pairs):
    return lax.ppermute(x, axis, [(a, b) for a, b in pairs] + [(b, a) for a, b in pairs])


def add(a, b):
    return (a.astype(F32) + b.astype(F32)).astype(BF)


def beside_ring(x, step):
    pairs = []
    for core in range(2):
        for zh in range(N):
            up = (zh + step + core) % 2 == 0
            pairs.append((zh * 2 + core, (zh + (1 if up else -1)) % N * 2 + core))
    return lax.ppermute(x, ("zh", "core"), pairs)


def body(query_proj, key_proj, value_proj, pair_bias, attn_output, output_grad):
    q, k, v, o, g = (
        jnp.swapaxes(x, 1, 2)
        for x in (query_proj, key_proj, value_proj, attn_output, output_grad)
    )
    grid = [(a, b) for a in range(N) for b in range(N)]

    core = lax.axis_index("core")
    held = jnp.concatenate([k, v], axis=1)
    bias = lax.dynamic_index_in_dim(pair_bias.reshape(N, 2, ROWS, ROWS), core, 1, False)
    theirs, bias = lax.optimization_barrier((swap(held, "core", [(0, 1)]), bias))
    kv = jnp.concatenate([held, theirs])
    spread = []
    for i in range(2):
        steps = []
        for c in range(2):
            for a, b in grid:
                target = (a + b + c + 2 * i) % N * N + a
                steps.append((c * N * N + a * N + b, c * N * N + target))
        spread.append(lax.ppermute(kv, ("core", "ri", "rj"), steps))
    bias = lax.all_to_all(bias, "rj", 0, 0, tiled=True)
    given = swap(pick(q, g, o, *spread), "core", [(0, 1)])

    total, dq, dkv = attention(q, g, o, *spread, given, bias)

    def spread_out(parts, axis):
        return [parts[0]] + [
            lax.ppermute(parts[t], axis, [(a, (a + t) % N) for a in range(N)])
            for t in range(1, N)
        ]

    spread = lax.all_to_all(total, ("x", "rj"), 0, 0, tiled=True)
    total = jnp.sum(spread.reshape(N, N, 64, ROWS).astype(F32), axis=0).astype(BF)
    other = beside_ring(total, 0)
    parts = spread_out(hand_on(split_kernel, total, dkv), "rj")
    total = add(total, other)
    other = beside_ring(total, 1)
    parts = spread_out(hand_on(choose_kernel, total, *parts), "ri")
    total = add(total, other)
    mine = lax.all_gather(total, "x", axis=0, tiled=True).reshape(-1, ROWS)

    dkv = sum(x.astype(F32) for x in parts).astype(BF)
    grads = jnp.concatenate([dkv, dq], axis=1)
    own, others = grads[: SEQS // 2], grads[SEQS // 2 :]
    theirs = swap(jnp.concatenate([mine, others.reshape(-1, ROWS)]), "core", [(0, 1)])
    bias_grad, dk, dv, dq = finish(theirs, own, place(mine))
    return *(jnp.swapaxes(x, 1, 2) for x in (dq, dk, dv)), bias_grad


def solution(mesh):
    split = Mesh(mesh.devices.reshape(N, N, 2, N, N), ("zh", "x", "core", "ri", "rj"))
    seq = ("zh", "x", "core")
    rows, keys, tile = P(seq, "ri", "rj"), P(seq, "rj", "ri"), P(None, "ri", "rj")
    return jax.shard_map(
        body,
        mesh=split,
        in_specs=(rows, keys, keys, tile, rows, rows),
        out_specs=(rows, keys, keys, tile),
        check_vma=False,
    )
```

```python
import jax
import jax.numpy as jnp
from jax import lax
from jax.experimental import pallas as pl
from jax.experimental.pallas import tpu as pltpu
from jax.sharding import Mesh
from jax.sharding import PartitionSpec as P

HEAD = 32
SCALE = HEAD**-0.5
N = 4
ROWS = 256
KEYS = N * ROWS
LANES = 128
SEQS = 4
CHUNK = 32
UNROLL = 8
BF = jnp.bfloat16
F32 = jnp.float32
NT = (((1,), (1,)), ((), ()))
NN = (((1,), (0,)), ((), ()))


def pick_kernel(q_ref, g_ref, o_ref, first, second, send):
    other = 1 - lax.axis_index("core")
    at = 0
    half = pl.ds(pl.multiple_of(other * HEAD, HEAD), HEAD)
    for x_ref in (q_ref, g_ref, o_ref):
        for s in range(SEQS // 2):
            send[at : at + HEAD, :] = x_ref[s, half, :]
            at += HEAD
    for x_ref in (first, second):
        for s in range(SEQS):
            for part in range(2):
                half = pl.ds(pl.multiple_of((2 * part + other) * HEAD, HEAD), HEAD)
                send[at : at + HEAD, :] = x_ref[s, half, :]
                at += HEAD


def pick(*args):
    vmem = pl.BlockSpec(memory_space=pltpu.VMEM)
    rows = (3 * (SEQS // 2) + 2 * SEQS * 2) * HEAD
    return pl.pallas_call(
        pick_kernel,
        out_shape=jax.ShapeDtypeStruct((rows, ROWS), BF),
        in_specs=[vmem] * 5,
        out_specs=vmem,
        compiler_params=pltpu.CompilerParams(vmem_limit_bytes=8 * 2**20),
        cost_estimate=pl.CostEstimate(flops=0, bytes_accessed=2**20, transcendentals=0),
    )(*args)


def attention_kernel(
    q_ref, g_ref, o_ref, first, second, given, bias,
    bias_grad, dq_ref, dkv_ref,
    stack, wide, raw, low, inner,
):
    ri, rj, core = (lax.axis_index(a) for a in ("ri", "rj", "core"))
    own = pl.ds(pl.multiple_of(core * HEAD, HEAD), HEAD)
    rounds = [2 * core, 2 * core + 1, 2 - 2 * core, 3 - 2 * core]
    blocks = [lax.rem(ri + 2 * N - rj - t, N) for t in rounds]

    def query_side(i, s):
        if s < SEQS // 2:
            return (q_ref, g_ref, o_ref)[i][s, own, :]
        at = (i * (SEQS // 2) + s - SEQS // 2) * HEAD
        return given[at : at + HEAD, :]

    def key_side(part, t, s):
        if t < 2:
            half = pl.ds(pl.multiple_of((2 * part + core) * HEAD, HEAD), HEAD)
            return (first, second)[t][s, half, :]
        there = (s + SEQS // 2) % SEQS
        at = (3 * (SEQS // 2) + ((t - 2) * SEQS + there) * 2 + part) * HEAD
        return given[at : at + HEAD, :]

    channel = lax.broadcasted_iota(jnp.int32, (2 * HEAD, ROWS), 0) // HEAD

    for s in range(SEQS):
        for part in range(2):
            at = slice(part * ROWS, (part + 1) * ROWS)
            one = jnp.where(channel == part, jnp.concatenate([query_side(0, s), query_side(1, s)]), 0)
            wide[s, :, at] = one
            stack[s, at, :] = one.T
        dots = query_side(1, s).astype(F32) * query_side(2, s).astype(F32)
        sums = jnp.sum(dots, axis=0, keepdims=True)
        inner[s] = jnp.broadcast_to(sums, (LANES, ROWS)).T

    for s in range(SEQS):
        for t in range(N):
            at = slice(t * ROWS, (t + 1) * ROWS)
            kv = jnp.concatenate([key_side(0, t, s), key_side(1, t, s)])
            raw[s, :, at] = lax.dot_general(stack[s], kv, NN, preferred_element_type=F32)

    @pl.loop(0, ROWS // CHUNK, unroll=UNROLL)
    def _(i):
        r0 = pl.multiple_of(i * CHUNK, CHUNK)
        at_logits = pl.ds(r0, CHUNK)
        at_grads = pl.ds(pl.multiple_of(ROWS + r0, CHUNK), CHUNK)
        pair = jnp.concatenate([bias[b, at_logits, :] for b in blocks], axis=1).astype(F32)
        total = None
        for s in range(SEQS):
            logits = raw[s, at_logits, :] * SCALE + pair
            top = jnp.max(logits, axis=1, keepdims=True)
            weights = jnp.exp(logits - top)
            weights = weights * (1.0 / jnp.sum(weights, axis=1, keepdims=True))
            dots = jnp.concatenate([inner[s, at_logits, :]] * (KEYS // LANES), axis=1)
            grad = weights * (raw[s, at_grads, :] - dots)
            low[s, at_logits, :] = grad.astype(BF)
            low[s, at_grads, :] = weights.astype(BF)
            total = grad if total is None else total + grad
        total = total.astype(BF)
        quarter = i // (64 // CHUNK)
        within = pl.ds(pl.multiple_of(lax.rem(i, 64 // CHUNK) * CHUNK, CHUNK), CHUNK)
        for t, b in enumerate(blocks):
            bias_grad[quarter * N + b, within, :] = total[:, t * ROWS : (t + 1) * ROWS]

    for s in range(SEQS):
        query_grads = None
        for t, b in enumerate(blocks):
            at = slice(t * ROWS, (t + 1) * ROWS)
            grads = lax.dot_general(wide[s], low[s, :, at], NN, preferred_element_type=F32)
            grads = jnp.where(channel == 0, grads * SCALE, grads)
            dkv_ref[lax.rem(b + N - rj, N), s] = grads.astype(BF)
            key = key_side(0, t, s)
            term = lax.dot_general(low[s, :ROWS, at], key, NT, preferred_element_type=F32)
            query_grads = term if query_grads is None else query_grads + term
        dq_ref[s] = (query_grads.T * SCALE).astype(BF)


def attention(*args):
    vmem = pl.BlockSpec(memory_space=pltpu.VMEM)
    return pl.pallas_call(
        attention_kernel,
        out_shape=(
            jax.ShapeDtypeStruct((N * N, 64, ROWS), BF),
            jax.ShapeDtypeStruct((SEQS, HEAD, ROWS), BF),
            jax.ShapeDtypeStruct((N, SEQS, 2 * HEAD, ROWS), BF),
        ),
        in_specs=[vmem] * 7,
        out_specs=(vmem,) * 3,
        scratch_shapes=[
            pltpu.VMEM((SEQS, 2 * ROWS, 2 * HEAD), BF),
            pltpu.VMEM((SEQS, 2 * HEAD, 2 * ROWS), BF),
            pltpu.VMEM((SEQS, 2 * ROWS, KEYS), F32),
            pltpu.VMEM((SEQS, 2 * ROWS, KEYS), BF),
            pltpu.VMEM((SEQS, ROWS, LANES), F32),
        ],
        compiler_params=pltpu.CompilerParams(vmem_limit_bytes=32 * 2**20),
        cost_estimate=pl.CostEstimate(
            flops=5 * 2 * 2**25, bytes_accessed=6 * 2**20, transcendentals=2**20
        ),
    )(*args)


def split_kernel(after, x_ref, *outs):
    for t, out in enumerate(outs):
        out[...] = x_ref[t]


def choose_kernel(after, *refs):
    ri, rj = lax.axis_index("ri"), lax.axis_index("rj")
    for t, out in enumerate(refs[N:]):
        wanted = lax.rem(rj + 2 * N - ri - t, N)
        for source, x_ref in enumerate(refs[:N]):

            @pl.when(wanted == source)
            def _():
                out[...] = x_ref[...]


def hand_on(kernel, after, *args):
    anywhere, vmem = pl.BlockSpec(memory_space=pl.ANY), pl.BlockSpec(memory_space=pltpu.VMEM)
    return pl.pallas_call(
        kernel,
        out_shape=[jax.ShapeDtypeStruct(args[0].shape[-3:], BF)] * N,
        in_specs=[anywhere] + [vmem] * len(args),
        out_specs=[vmem] * N,
        compiler_params=pltpu.CompilerParams(vmem_limit_bytes=8 * 2**20),
        cost_estimate=pl.CostEstimate(flops=0, bytes_accessed=2**21, transcendentals=0),
    )(after, *args)


def place_heads(x_ref, out_ref, wide, sem, head):
    copies = []
    for j in range(N):
        for x in range(N):
            at = (x * N + j) * 64
            wide[j, x * 64 : (x + 1) * 64, :] = x_ref[at : at + 64, :].astype(F32)
        copies.append(pltpu.make_async_copy(wide.at[j], out_ref.at[2 * j + head], sem.at[j]))
        copies[-1].start()
    return copies


def place_kernel(x_ref, out_ref, wide, sem):
    for c in place_heads(x_ref, out_ref, wide, sem, lax.axis_index("core")):
        c.wait()


def finish_kernel(x_ref, own_ref, before, out_ref, dk_ref, dv_ref, dq_ref, wide, both, sem):
    core = lax.axis_index("core")
    copies = place_heads(x_ref, out_ref, wide, sem, 1 - core)
    mine = pl.ds(pl.multiple_of(core * HEAD, HEAD), HEAD)
    theirs = pl.ds(pl.multiple_of((1 - core) * HEAD, HEAD), HEAD)
    for i, grad_ref in enumerate((dk_ref, dv_ref, dq_ref)):
        for s in range(SEQS // 2):
            at = N * ROWS + (s * 3 + i) * HEAD
            both[i, s, mine, :] = own_ref[s, i * HEAD : (i + 1) * HEAD, :]
            both[i, s, theirs, :] = x_ref[at : at + HEAD, :]
        copies.append(pltpu.make_async_copy(both.at[i], grad_ref, sem.at[N + i]))
        copies[-1].start()
    for c in copies:
        c.wait()


def place(x):
    anywhere, vmem = pl.BlockSpec(memory_space=pl.ANY), pl.BlockSpec(memory_space=pltpu.VMEM)
    return pl.pallas_call(
        place_kernel,
        out_shape=jax.ShapeDtypeStruct((2 * N, ROWS, ROWS), F32),
        in_specs=[vmem],
        out_specs=anywhere,
        scratch_shapes=[pltpu.VMEM((N, ROWS, ROWS), F32), pltpu.SemaphoreType.DMA((N,))],
        compiler_params=pltpu.CompilerParams(vmem_limit_bytes=8 * 2**20),
        cost_estimate=pl.CostEstimate(flops=2**18, bytes_accessed=3 * 2**19, transcendentals=0),
    )(x)


def finish(x, own, before):
    anywhere, vmem = pl.BlockSpec(memory_space=pl.ANY), pl.BlockSpec(memory_space=pltpu.VMEM)
    grad = jax.ShapeDtypeStruct((SEQS // 2, 2 * HEAD, ROWS), BF)
    return pl.pallas_call(
        finish_kernel,
        out_shape=(jax.ShapeDtypeStruct(before.shape, F32), grad, grad, grad),
        in_specs=[vmem, vmem, anywhere],
        out_specs=(anywhere,) * 4,
        scratch_shapes=[
            pltpu.VMEM((N, ROWS, ROWS), F32),
            pltpu.VMEM((3, *grad.shape), BF),
            pltpu.SemaphoreType.DMA((N + 3,)),
        ],
        input_output_aliases={2: 0},
        compiler_params=pltpu.CompilerParams(vmem_limit_bytes=8 * 2**20),
        cost_estimate=pl.CostEstimate(flops=2**18, bytes_accessed=2**21, transcendentals=0),
    )(x, own, before)


def swap(x, axis, pairs):
    return lax.ppermute(x, axis, [(a, b) for a, b in pairs] + [(b, a) for a, b in pairs])


def add(a, b):
    return (a.astype(F32) + b.astype(F32)).astype(BF)


def beside_ring(x, step):
    pairs = []
    for core in range(2):
        for zh in range(N):
            up = (zh + step + core) % 2 == 0
            pairs.append((zh * 2 + core, (zh + (1 if up else -1)) % N * 2 + core))
    return lax.ppermute(x, ("zh", "core"), pairs)


def body(query_proj, key_proj, value_proj, pair_bias, attn_output, output_grad):
    q, k, v, o, g = (
        jnp.swapaxes(x, 1, 2)
        for x in (query_proj, key_proj, value_proj, attn_output, output_grad)
    )
    grid = [(a, b) for a in range(N) for b in range(N)]

    core = lax.axis_index("core")
    held = jnp.concatenate([k, v], axis=1)
    bias = lax.dynamic_index_in_dim(pair_bias.reshape(N, 2, ROWS, ROWS), core, 1, False)
    theirs, bias = lax.optimization_barrier((swap(held, "core", [(0, 1)]), bias))
    kv = jnp.concatenate([held, theirs])
    spread = []
    for i in range(2):
        steps = []
        for c in range(2):
            for a, b in grid:
                target = (a + b + 2 * c + i) % N * N + a
                steps.append((c * N * N + a * N + b, c * N * N + target))
        spread.append(lax.ppermute(kv, ("core", "ri", "rj"), steps))
    bias = lax.all_to_all(bias, "rj", 0, 0, tiled=True)
    given = swap(pick(q, g, o, *spread), "core", [(0, 1)])

    total, dq, dkv = attention(q, g, o, *spread, given, bias)

    def spread_out(parts, axis):
        return [parts[0]] + [
            lax.ppermute(parts[t], axis, [(a, (a + t) % N) for a in range(N)])
            for t in range(1, N)
        ]

    spread = lax.all_to_all(total, ("x", "rj"), 0, 0, tiled=True)
    total = jnp.sum(spread.reshape(N, N, 64, ROWS).astype(F32), axis=0).astype(BF)
    other = beside_ring(total, 0)
    parts = spread_out(hand_on(split_kernel, total, dkv), "rj")
    total = add(total, other)
    other = beside_ring(total, 1)
    parts = spread_out(hand_on(choose_kernel, total, *parts), "ri")
    total = add(total, other)
    copies = jnp.broadcast_to(total, (N, *total.shape))
    mine = lax.all_to_all(copies, "x", 0, 0, tiled=True).reshape(-1, ROWS)

    dkv = sum(x.astype(F32) for x in parts).astype(BF)
    grads = jnp.concatenate([dkv, dq], axis=1)
    own, others = grads[: SEQS // 2], grads[SEQS // 2 :]
    theirs = swap(jnp.concatenate([mine, others.reshape(-1, ROWS)]), "core", [(0, 1)])
    bias_grad, dk, dv, dq = finish(theirs, own, place(mine))
    return *(jnp.swapaxes(x, 1, 2) for x in (dq, dk, dv)), bias_grad


def solution(mesh):
    split = Mesh(mesh.devices.reshape(N, N, 2, N, N), ("zh", "x", "core", "ri", "rj"))
    seq = ("zh", "x", "core")
    rows, keys, tile = P(seq, "ri", "rj"), P(seq, "rj", "ri"), P(None, "ri", "rj")
    return jax.shard_map(
        body,
        mesh=split,
        in_specs=(rows, keys, keys, tile, rows, rows),
        out_specs=(rows, keys, keys, tile),
        check_vma=False,
    )
```

```python
import jax
import jax.numpy as jnp
from jax import lax
from jax.experimental import pallas as pl
from jax.experimental.pallas import tpu as pltpu
from jax.sharding import Mesh
from jax.sharding import PartitionSpec as P

HEAD = 32
SCALE = HEAD**-0.5
N = 4
ROWS = 256
KEYS = N * ROWS
LANES = 128
SEQS = 4
CHUNK = 32
UNROLL = 8
BF = jnp.bfloat16
F32 = jnp.float32
NT = (((1,), (1,)), ((), ()))
NN = (((1,), (0,)), ((), ()))


def pick_kernel(q_ref, g_ref, o_ref, first, second, send):
    other = 1 - lax.axis_index("core")
    at = 0
    half = pl.ds(pl.multiple_of(other * HEAD, HEAD), HEAD)
    for x_ref in (q_ref, g_ref, o_ref):
        for s in range(SEQS // 2):
            send[at : at + HEAD, :] = x_ref[s, half, :]
            at += HEAD
    for x_ref in (first, second):
        for s in range(SEQS):
            for part in range(2):
                half = pl.ds(pl.multiple_of((2 * part + other) * HEAD, HEAD), HEAD)
                send[at : at + HEAD, :] = x_ref[s, half, :]
                at += HEAD


def pick(*args):
    vmem = pl.BlockSpec(memory_space=pltpu.VMEM)
    rows = (3 * (SEQS // 2) + 2 * SEQS * 2) * HEAD
    return pl.pallas_call(
        pick_kernel,
        out_shape=jax.ShapeDtypeStruct((rows, ROWS), BF),
        in_specs=[vmem] * 5,
        out_specs=vmem,
        compiler_params=pltpu.CompilerParams(vmem_limit_bytes=8 * 2**20),
        cost_estimate=pl.CostEstimate(flops=0, bytes_accessed=2**20, transcendentals=0),
    )(*args)


def attention_kernel(
    q_ref, g_ref, o_ref, first, second, given, bias,
    bias_grad, dq_ref, dkv_ref,
    stack, wide, raw, low, inner,
):
    ri, rj, core = (lax.axis_index(a) for a in ("ri", "rj", "core"))
    own = pl.ds(pl.multiple_of(core * HEAD, HEAD), HEAD)
    rounds = [2 * core, 2 * core + 1, 2 - 2 * core, 3 - 2 * core]
    blocks = [lax.rem(ri + 2 * N - rj - t, N) for t in rounds]

    def query_side(i, s):
        if s < SEQS // 2:
            return (q_ref, g_ref, o_ref)[i][s, own, :]
        at = (i * (SEQS // 2) + s - SEQS // 2) * HEAD
        return given[at : at + HEAD, :]

    def key_side(part, t, s):
        if t < 2:
            half = pl.ds(pl.multiple_of((2 * part + core) * HEAD, HEAD), HEAD)
            return (first, second)[t][s, half, :]
        there = (s + SEQS // 2) % SEQS
        at = (3 * (SEQS // 2) + ((t - 2) * SEQS + there) * 2 + part) * HEAD
        return given[at : at + HEAD, :]

    channel = lax.broadcasted_iota(jnp.int32, (2 * HEAD, ROWS), 0) // HEAD

    for s in range(SEQS):
        for part in range(2):
            at = slice(part * ROWS, (part + 1) * ROWS)
            one = jnp.where(channel == part, jnp.concatenate([query_side(0, s), query_side(1, s)]), 0)
            wide[s, :, at] = one
            stack[s, at, :] = one.T
        dots = query_side(1, s).astype(F32) * query_side(2, s).astype(F32)
        sums = jnp.sum(dots, axis=0, keepdims=True)
        inner[s] = jnp.broadcast_to(sums, (LANES, ROWS)).T

    for s in range(SEQS):
        for t in range(N):
            at = slice(t * ROWS, (t + 1) * ROWS)
            kv = jnp.concatenate([key_side(0, t, s), key_side(1, t, s)])
            raw[s, :, at] = lax.dot_general(stack[s], kv, NN, preferred_element_type=F32)

    @pl.loop(0, ROWS // CHUNK, unroll=UNROLL)
    def _(i):
        r0 = pl.multiple_of(i * CHUNK, CHUNK)
        at_logits = pl.ds(r0, CHUNK)
        at_grads = pl.ds(pl.multiple_of(ROWS + r0, CHUNK), CHUNK)
        pair = jnp.concatenate([bias[b, at_logits, :] for b in blocks], axis=1).astype(F32)
        total = None
        for s in range(SEQS):
            logits = raw[s, at_logits, :] * SCALE + pair
            top = jnp.max(logits, axis=1, keepdims=True)
            weights = jnp.exp(logits - top)
            weights = weights * (1.0 / jnp.sum(weights, axis=1, keepdims=True))
            dots = jnp.concatenate([inner[s, at_logits, :]] * (KEYS // LANES), axis=1)
            grad = weights * (raw[s, at_grads, :] - dots)
            low[s, at_logits, :] = grad.astype(BF)
            low[s, at_grads, :] = weights.astype(BF)
            total = grad if total is None else total + grad
        total = total.astype(BF)
        quarter = i // (64 // CHUNK)
        within = pl.ds(pl.multiple_of(lax.rem(i, 64 // CHUNK) * CHUNK, CHUNK), CHUNK)
        for t, b in enumerate(blocks):
            bias_grad[quarter * N + b, within, :] = total[:, t * ROWS : (t + 1) * ROWS]

    for s in range(SEQS):
        query_grads = None
        for t, b in enumerate(blocks):
            at = slice(t * ROWS, (t + 1) * ROWS)
            grads = lax.dot_general(wide[s], low[s, :, at], NN, preferred_element_type=F32)
            grads = jnp.where(channel == 0, grads * SCALE, grads)
            dkv_ref[lax.rem(b + N - rj, N), s] = grads.astype(BF)
            key = key_side(0, t, s)
            term = lax.dot_general(low[s, :ROWS, at], key, NT, preferred_element_type=F32)
            query_grads = term if query_grads is None else query_grads + term
        dq_ref[s] = (query_grads.T * SCALE).astype(BF)


def attention(*args):
    vmem = pl.BlockSpec(memory_space=pltpu.VMEM)
    return pl.pallas_call(
        attention_kernel,
        out_shape=(
            jax.ShapeDtypeStruct((N * N, 64, ROWS), BF),
            jax.ShapeDtypeStruct((SEQS, HEAD, ROWS), BF),
            jax.ShapeDtypeStruct((N, SEQS, 2 * HEAD, ROWS), BF),
        ),
        in_specs=[vmem] * 7,
        out_specs=(vmem,) * 3,
        scratch_shapes=[
            pltpu.VMEM((SEQS, 2 * ROWS, 2 * HEAD), BF),
            pltpu.VMEM((SEQS, 2 * HEAD, 2 * ROWS), BF),
            pltpu.VMEM((SEQS, 2 * ROWS, KEYS), F32),
            pltpu.VMEM((SEQS, 2 * ROWS, KEYS), BF),
            pltpu.VMEM((SEQS, ROWS, LANES), F32),
        ],
        compiler_params=pltpu.CompilerParams(vmem_limit_bytes=32 * 2**20),
        cost_estimate=pl.CostEstimate(
            flops=5 * 2 * 2**25, bytes_accessed=6 * 2**20, transcendentals=2**20
        ),
    )(*args)


def split_kernel(after, x_ref, *outs):
    for t, out in enumerate(outs):
        out[...] = x_ref[t]


def choose_kernel(after, *refs):
    ri, rj = lax.axis_index("ri"), lax.axis_index("rj")
    for t, out in enumerate(refs[N:]):
        wanted = lax.rem(rj + 2 * N - ri - t, N)
        for source, x_ref in enumerate(refs[:N]):

            @pl.when(wanted == source)
            def _():
                out[...] = x_ref[...]


def hand_on(kernel, after, *args):
    anywhere, vmem = pl.BlockSpec(memory_space=pl.ANY), pl.BlockSpec(memory_space=pltpu.VMEM)
    return pl.pallas_call(
        kernel,
        out_shape=[jax.ShapeDtypeStruct(args[0].shape[-3:], BF)] * N,
        in_specs=[anywhere] + [vmem] * len(args),
        out_specs=[vmem] * N,
        compiler_params=pltpu.CompilerParams(vmem_limit_bytes=8 * 2**20),
        cost_estimate=pl.CostEstimate(flops=0, bytes_accessed=2**21, transcendentals=0),
    )(after, *args)


def place_heads(x_ref, out_ref, wide, sem, head):
    copies = []
    for j in range(N):
        for x in range(N):
            at = (x * N + j) * 64
            wide[j, x * 64 : (x + 1) * 64, :] = x_ref[at : at + 64, :].astype(F32)
        copies.append(pltpu.make_async_copy(wide.at[j], out_ref.at[2 * j + head], sem.at[j]))
        copies[-1].start()
    return copies


def place_kernel(x_ref, out_ref, wide, sem):
    for c in place_heads(x_ref, out_ref, wide, sem, lax.axis_index("core")):
        c.wait()


def finish_kernel(x_ref, own_ref, before, out_ref, dk_ref, dv_ref, dq_ref, wide, both, sem):
    core = lax.axis_index("core")
    copies = place_heads(x_ref, out_ref, wide, sem, 1 - core)
    mine = pl.ds(pl.multiple_of(core * HEAD, HEAD), HEAD)
    theirs = pl.ds(pl.multiple_of((1 - core) * HEAD, HEAD), HEAD)
    for i, grad_ref in enumerate((dk_ref, dv_ref, dq_ref)):
        for s in range(SEQS // 2):
            at = N * ROWS + (s * 3 + i) * HEAD
            both[i, s, mine, :] = own_ref[s, i * HEAD : (i + 1) * HEAD, :]
            both[i, s, theirs, :] = x_ref[at : at + HEAD, :]
        copies.append(pltpu.make_async_copy(both.at[i], grad_ref, sem.at[N + i]))
        copies[-1].start()
    for c in copies:
        c.wait()


def place(x):
    anywhere, vmem = pl.BlockSpec(memory_space=pl.ANY), pl.BlockSpec(memory_space=pltpu.VMEM)
    return pl.pallas_call(
        place_kernel,
        out_shape=jax.ShapeDtypeStruct((2 * N, ROWS, ROWS), F32),
        in_specs=[vmem],
        out_specs=anywhere,
        scratch_shapes=[pltpu.VMEM((N, ROWS, ROWS), F32), pltpu.SemaphoreType.DMA((N,))],
        compiler_params=pltpu.CompilerParams(vmem_limit_bytes=8 * 2**20),
        cost_estimate=pl.CostEstimate(flops=2**18, bytes_accessed=3 * 2**19, transcendentals=0),
    )(x)


def finish(x, own, before):
    anywhere, vmem = pl.BlockSpec(memory_space=pl.ANY), pl.BlockSpec(memory_space=pltpu.VMEM)
    grad = jax.ShapeDtypeStruct((SEQS // 2, 2 * HEAD, ROWS), BF)
    return pl.pallas_call(
        finish_kernel,
        out_shape=(jax.ShapeDtypeStruct(before.shape, F32), grad, grad, grad),
        in_specs=[vmem, vmem, anywhere],
        out_specs=(anywhere,) * 4,
        scratch_shapes=[
            pltpu.VMEM((N, ROWS, ROWS), F32),
            pltpu.VMEM((3, *grad.shape), BF),
            pltpu.SemaphoreType.DMA((N + 3,)),
        ],
        input_output_aliases={2: 0},
        compiler_params=pltpu.CompilerParams(vmem_limit_bytes=8 * 2**20),
        cost_estimate=pl.CostEstimate(flops=2**18, bytes_accessed=2**21, transcendentals=0),
    )(x, own, before)


def swap(x, axis, pairs):
    return lax.ppermute(x, axis, [(a, b) for a, b in pairs] + [(b, a) for a, b in pairs])


def add(a, b):
    return (a.astype(F32) + b.astype(F32)).astype(BF)


def repeat_kernel(a_ref, b_ref, out):
    total = (a_ref[...].astype(F32) + b_ref[...].astype(F32)).astype(BF)
    for t in range(N):
        out[t] = total


def repeat(a, b):
    vmem = pl.BlockSpec(memory_space=pltpu.VMEM)
    return pl.pallas_call(
        repeat_kernel,
        out_shape=jax.ShapeDtypeStruct((N, *a.shape), BF),
        in_specs=[vmem] * 2,
        out_specs=vmem,
        compiler_params=pltpu.CompilerParams(vmem_limit_bytes=8 * 2**20),
        cost_estimate=pl.CostEstimate(flops=2**16, bytes_accessed=2**20, transcendentals=0),
    )(a, b)


def beside_ring(x, step):
    pairs = []
    for core in range(2):
        for zh in range(N):
            up = (zh + step + core) % 2 == 0
            pairs.append((zh * 2 + core, (zh + (1 if up else -1)) % N * 2 + core))
    return lax.ppermute(x, ("zh", "core"), pairs)


def body(query_proj, key_proj, value_proj, pair_bias, attn_output, output_grad):
    q, k, v, o, g = (
        jnp.swapaxes(x, 1, 2)
        for x in (query_proj, key_proj, value_proj, attn_output, output_grad)
    )
    grid = [(a, b) for a in range(N) for b in range(N)]

    core = lax.axis_index("core")
    held = jnp.concatenate([k, v], axis=1)
    bias = lax.dynamic_index_in_dim(pair_bias.reshape(N, 2, ROWS, ROWS), core, 1, False)
    theirs, bias = lax.optimization_barrier((swap(held, "core", [(0, 1)]), bias))
    kv = jnp.concatenate([held, theirs])
    spread = []
    for i in range(2):
        steps = []
        for c in range(2):
            for a, b in grid:
                target = (a + b + 2 * c + i) % N * N + a
                steps.append((c * N * N + a * N + b, c * N * N + target))
        spread.append(lax.ppermute(kv, ("core", "ri", "rj"), steps))
    bias = lax.all_to_all(bias, "rj", 0, 0, tiled=True)
    given = swap(pick(q, g, o, *spread), "core", [(0, 1)])

    total, dq, dkv = attention(q, g, o, *spread, given, bias)

    def spread_out(parts, axis):
        return [parts[0]] + [
            lax.ppermute(parts[t], axis, [(a, (a + t) % N) for a in range(N)])
            for t in range(1, N)
        ]

    spread = lax.all_to_all(total, ("x", "rj"), 0, 0, tiled=True)
    total = jnp.sum(spread.reshape(N, N, 64, ROWS).astype(F32), axis=0).astype(BF)
    other = beside_ring(total, 0)
    parts = spread_out(hand_on(split_kernel, total, dkv), "rj")
    total = add(total, other)
    other = beside_ring(total, 1)
    parts = spread_out(hand_on(choose_kernel, total, *parts), "ri")
    copies = repeat(total, other)
    mine = lax.all_to_all(copies, "x", 0, 0, tiled=True).reshape(-1, ROWS)

    dkv = sum(x.astype(F32) for x in parts).astype(BF)
    grads = jnp.concatenate([dkv, dq], axis=1)
    own, others = grads[: SEQS // 2], grads[SEQS // 2 :]
    theirs = swap(jnp.concatenate([mine, others.reshape(-1, ROWS)]), "core", [(0, 1)])
    bias_grad, dk, dv, dq = finish(theirs, own, place(mine))
    return *(jnp.swapaxes(x, 1, 2) for x in (dq, dk, dv)), bias_grad


def solution(mesh):
    split = Mesh(mesh.devices.reshape(N, N, 2, N, N), ("zh", "x", "core", "ri", "rj"))
    seq = ("zh", "x", "core")
    rows, keys, tile = P(seq, "ri", "rj"), P(seq, "rj", "ri"), P(None, "ri", "rj")
    return jax.shard_map(
        body,
        mesh=split,
        in_specs=(rows, keys, keys, tile, rows, rows),
        out_specs=(rows, keys, keys, tile),
        check_vma=False,
    )
```
